32 devices in a mesh: seq: 2 (over x), dp: 4 (over y, core), rep: 4 (over z).
Axes of the slice: x: 2, y: 2, z: 4, core: 2. Of those that a mesh axis runs over, the one named last changes fastest.
Arguments:
- inputs: bfloat16 [2, 16, 2048, 1024], P(None, ('dp', 'rep'), 'seq'), may hold values from -6 to 6
- segments: int32 [2, 16, 2048], P(None, ('dp', 'rep')), may hold values from 0 to 6, as said below
- cotangent: bfloat16 [2, 16, 2048, 1024], P(None, ('dp', 'rep'), 'seq'), may hold values from -6 to 6
- attn_gain: bfloat16 [1024], P(('seq', 'dp')), may hold values from 0.25 to 1.75
- mlp_gain: bfloat16 [1024], P(('seq', 'dp')), may hold values from 0.25 to 1.75
- w_qkv: bfloat16 [1024, 3072], P(('seq', 'dp')), may hold values from -0.1875 to 0.1875
- w_out: bfloat16 [1024, 1024], P(('seq', 'dp')), may hold values from -3 to 3
- w_in: bfloat16 [1024, 5248], P(('seq', 'dp')), may hold values from -0.1875 to 0.1875
- w_down: bfloat16 [2624, 1024], P(('seq', 'dp')), may hold values from -0.125 to 0.125
Outputs:
- outputs: bfloat16 [2, 16, 2048, 1024], P(None, ('dp', 'rep'), 'seq')
- grad_inputs: float32 [2, 16, 2048, 1024], P(None, ('dp', 'rep'), 'seq')
- grad_attn_gain: float32 [1024], P(('seq', 'dp'))
- grad_mlp_gain: float32 [1024], P(('seq', 'dp'))
- grad_qkv: float32 [1024, 3072], P(('seq', 'dp'))
- grad_out: float32 [1024, 1024], P(('seq', 'dp'))
- grad_in: float32 [1024, 5248], P(('seq', 'dp'))
- grad_down: float32 [2624, 1024], P(('seq', 'dp'))
The draws below stay inside these ranges and needn't reach their ends.
Inputs may be any that keep to these rules, and one draw needn't show every extreme that they name: `segments`: along each packed sequence the document number never falls; it is 0 at the first token and 6 at the last.
All inputs are finite; a program needn't handle non-finite values.
Results may differ from the reference program's by a relative error of at most 0.02.
Values may be sent and summed in bfloat16 or wider, within the bound.
A program may use at most 576 MiB of HBM per device.

```python
import jax
import jax.numpy as jnp
from jax import lax

D = 1024
HEADS = 16
HEAD_DIM = 64
FF = 2624
HALF = 512
MB = 2
CUTS = 6
LENGTH = 2048
STRETCH = 1024
SEQS = 16


def draw_segments(key, part):
    key = jax.random.fold_in(key, 7)
    key_cuts, key_pick = jax.random.split(key)
    boundaries = jax.random.randint(key_cuts, (MB, SEQS, CUTS), 1, LENGTH)
    chosen = jax.random.randint(key_pick, (1, SEQS, 1), 0, MB)
    batches = lax.broadcasted_iota(jnp.int32, (MB, SEQS, CUTS), 0)
    modulus = STRETCH - 1
    edges = jnp.where(boundaries < LENGTH // 2, 1 + boundaries % modulus, LENGTH - 1 - boundaries % modulus)
    boundaries = jnp.where(batches == chosen, edges, boundaries)
    places = lax.broadcasted_iota(jnp.int32, (MB, SEQS, LENGTH), 2)
    return jnp.sum((boundaries[:, :, None, :] <= places[..., None]).astype(jnp.int32), axis=-1)


def steps_of(stream_key, dims, shards, least, largest):
    loudness = 1.0
    for dim, blocks in shards:
        draws = jax.random.uniform(jax.random.fold_in(jax.random.fold_in(stream_key, 6), dim), (blocks,), jnp.float32, least / len(shards), largest / len(shards))
        loudness = loudness * jnp.repeat(jnp.exp(draws), dims[dim] // blocks).reshape((-1,) + (1,) * (len(dims) - 1 - dim))
    return loudness


def bell_draw(key, extent, scale, most, cuts=(), held_as=jnp.bfloat16):
    values = jax.random.normal(key, extent, jnp.float32) * scale
    if len(cuts) > 0:
        values = steps_of(key, extent, cuts, -0.22, 0.18) * values
    return jnp.clip(values, min=-most, max=most).astype(held_as)


def setup_inputs(seed: int = 0) -> dict:
    arg_keys = jax.random.split(jax.random.key(seed), 10)
    inputs = bell_draw(arg_keys[0], (MB, SEQS, LENGTH, D), 1.0, 6.0, ((1, 16), (2, 2)))
    segments = draw_segments(jax.random.fold_in(arg_keys[9], 71), 0)
    cotangent = bell_draw(arg_keys[2], (MB, SEQS, LENGTH, D), 1.0, 6.0, ((1, 16), (2, 2)))
    attn_gain = jnp.clip(1.0 + 0.15 * jax.random.normal(arg_keys[3], (D,), jnp.float32), 0.25, 1.75).astype(jnp.bfloat16)
    mlp_gain = jnp.clip(1.0 + 0.15 * jax.random.normal(arg_keys[4], (D,), jnp.float32), 0.25, 1.75).astype(jnp.bfloat16)
    w_qkv = bell_draw(arg_keys[5], (D, 3 * D), D ** -0.5, 0.1875, ((0, 8),))
    w_out = bell_draw(arg_keys[6], (D, D), 4 ** -0.5, 3.0, ((0, 8),))
    w_in = bell_draw(arg_keys[7], (D, 2 * FF), D ** -0.5, 0.1875, ((0, 8),))
    w_down = bell_draw(arg_keys[8], (FF, D), FF ** -0.5, 0.125, ((0, 8),))
    return dict(inputs=inputs, segments=segments, cotangent=cotangent, attn_gain=attn_gain, mlp_gain=mlp_gain, w_qkv=w_qkv, w_out=w_out, w_in=w_in, w_down=w_down)


EPS = 1e-05
THETA = 10000.0
MASKED = -1e+30
HIGH = lax.Precision.HIGHEST

@jax.custom_vjp
def low(v):
    return lax.optimization_barrier(v.astype(jnp.bfloat16)).astype(jnp.float32)

@jax.custom_vjp
def low_back(v):
    return v

def low_keep(v):
    return (low(v), None)

def low_pass(kept, grad):
    return (grad,)

def back_keep(v):
    return (v, None)

def back_low(kept, grad):
    return (low(grad),)
low.defvjp(low_keep, low_pass)
low_back.defvjp(back_keep, back_low)

def layer_norm(values, scaling):
    centre = values - lax.optimization_barrier(jnp.mean(values, axis=-1, keepdims=True))
    spread = lax.optimization_barrier(jnp.mean(centre * centre, axis=-1, keepdims=True))
    return centre * lax.rsqrt(spread + EPS) * scaling

def positions_of(labels):
    places = jnp.arange(labels.shape[0], dtype=jnp.int32)
    changes = jnp.concatenate([jnp.ones((1,), dtype=bool), labels[1:] != labels[:-1]])
    starts = lax.cummax(jnp.where(changes, places, 0), axis=0)
    return places - starts

def rope_tables(positions, head_size):
    half_dim = head_size // 2
    frequency = THETA ** (-(jnp.arange(half_dim, dtype=jnp.float32) * 2.0 / head_size))
    angles = positions.astype(jnp.float32)[:, None] * frequency[None, :]
    return (jnp.cos(angles)[:, None, :], jnp.sin(angles)[:, None, :])

def rotate(values, cosines, sines):
    half_dim = values.shape[-1] // 2
    leading = values[..., :half_dim]
    trailing = values[..., half_dim:]
    return jnp.concatenate([leading * cosines - trailing * sines, trailing * cosines + leading * sines], axis=-1)

def window_mask(query_labels, key_labels, half_window):
    gaps = jnp.arange(key_labels.shape[0], dtype=jnp.int32)[None, :] - jnp.arange(query_labels.shape[0], dtype=jnp.int32)[:, None]
    return (gaps >= 0) & (gaps <= 2 * half_window) & (query_labels[:, None] == key_labels[None, :])

def attend(queries, keys, values, labels):
    length_rows = queries.shape[0]
    block_rows = min(512, length_rows)
    key_span = block_rows + 2 * HALF
    padding = ((HALF, HALF), (0, 0), (0, 0))
    key_pad = jnp.pad(keys, padding)
    value_pad = jnp.pad(values, padding)
    label_pad = jnp.pad(labels, (HALF, HALF), constant_values=-1)
    score_scale = HEAD_DIM ** (-0.5)

    def one_block(number):
        first_row = number * block_rows
        query_rows = lax.dynamic_slice_in_dim(queries, first_row, block_rows, 0)
        key_rows = lax.dynamic_slice_in_dim(key_pad, first_row, key_span, 0)
        value_rows = lax.dynamic_slice_in_dim(value_pad, first_row, key_span, 0)
        allowed = window_mask(lax.dynamic_slice_in_dim(labels, first_row, block_rows, 0), lax.dynamic_slice_in_dim(label_pad, first_row, key_span, 0), HALF)
        scores = low_back(jnp.einsum('qhd,khd->hqk', query_rows, key_rows, precision=HIGH) * score_scale)
        scores = jnp.where(allowed[None], scores, MASKED)
        highest = lax.optimization_barrier(jnp.max(scores, axis=-1, keepdims=True))
        powers = jnp.exp(scores - highest)
        probs = powers / lax.optimization_barrier(jnp.sum(powers, axis=-1, keepdims=True))
        return jnp.einsum('hqk,khd->qhd', low(probs), value_rows, precision=HIGH)
    mixed = lax.map(jax.checkpoint(one_block), jnp.arange(length_rows // block_rows, dtype=jnp.int32))
    return mixed.reshape(length_rows, HEADS * HEAD_DIM)

def layer(stream, labels, gain_one, gain_two, qkv_weight, out_weight, in_weight, down_weight):
    length_rows = stream.shape[0]
    cosines, sines = rope_tables(positions_of(labels), HEAD_DIM)
    normed_one = low(layer_norm(stream, gain_one))
    projected = low_back(jnp.dot(normed_one, qkv_weight, precision=HIGH))
    query_raw = projected[:, :D].reshape(length_rows, HEADS, HEAD_DIM)
    key_raw = projected[:, D:2 * D].reshape(length_rows, HEADS, HEAD_DIM)
    value_raw = projected[:, 2 * D:].reshape(length_rows, HEADS, HEAD_DIM)
    queries = low(rotate(query_raw, cosines, sines))
    keys = low(rotate(key_raw, cosines, sines))
    values = low(value_raw)
    mixed = low_back(low(attend(queries, keys, values, labels)))
    branch_one = low_back(jnp.dot(mixed, out_weight, precision=HIGH))
    after_attn = stream + branch_one
    normed_two = low(layer_norm(after_attn, gain_two))
    gate_up = low_back(jnp.dot(normed_two, in_weight, precision=HIGH))
    hidden_units = low(jax.nn.gelu(gate_up[:, :FF], approximate=False) * gate_up[:, FF:])
    branch_two = low_back(jnp.dot(hidden_units, down_weight, precision=HIGH))
    return after_attn + branch_two

def reference(inputs, segments, cotangent, attn_gain, mlp_gain, w_qkv, w_out, w_in, w_down):
    params = tuple((array.astype(jnp.float32) for array in (attn_gain, mlp_gain, w_qkv, w_out, w_in, w_down)))
    count = inputs.shape[0] * inputs.shape[1]
    rows = inputs.reshape(count, LENGTH, D).astype(jnp.float32)
    labels = segments.reshape(count, LENGTH)
    seeds = cotangent.reshape(count, LENGTH, D).astype(jnp.float32)

    def step(totals, item):
        row_stream, row_labels, row_seed = item

        def forward(stream, *weights):
            return layer(stream, row_labels, *weights)
        result, back = jax.vjp(forward, row_stream, *params)
        gradients = back(row_seed)
        totals = tuple((total + grad for total, grad in zip(totals, gradients[1:])))
        return (totals, (result.astype(jnp.bfloat16), gradients[0]))
    starting = tuple((jnp.zeros_like(array) for array in params))
    totals, (results, input_grads) = lax.scan(step, starting, (rows, labels, seeds))
    return (results.reshape(inputs.shape), input_grads.reshape(inputs.shape), totals[0], totals[1], totals[2], totals[3], totals[4], totals[5])
```

```python
import functools

import jax
import jax.numpy as jnp
from jax import lax
from jax.experimental import pallas as pl
from jax.experimental.pallas import tpu as pltpu
from jax.sharding import PartitionSpec as P

HEADS = 16
HEAD_DIM = 64
FF = 2624
HALF = 512
DOCS = 7

EPS = 1e-05
THETA = 10000.0
MASKED = -1e30

TILE = 256
REACH = HALF // TILE
LANES = 128
FF_PAD = -(-FF // LANES) * LANES
PAIRS = HEADS // 2
WIDE = 4
WIDE_BACK = 2
VMEM = 60 * 1024 * 1024

F32 = jnp.float32
BF16 = jnp.bfloat16

NN = (((1,), (0,)), ((), ()))
NT = (((1,), (1,)), ((), ()))


def dot(left, right, dims=NN):
    return lax.dot_general(left, right, dims, preferred_element_type=F32)


def params(**more):
    return pltpu.CompilerParams(vmem_limit_bytes=VMEM, **more)


def normed(values):
    centre = values - jnp.mean(values, axis=-1, keepdims=True)
    spread = jnp.mean(centre * centre, axis=-1, keepdims=True)
    inverse = lax.rsqrt(spread + EPS)
    return centre * inverse, inverse


def norm_back(grads, unit, inverse):
    first = jnp.mean(grads, axis=-1, keepdims=True)
    second = jnp.mean(grads * unit, axis=-1, keepdims=True)
    return (grads - first - unit * second) * inverse


def swapped(values):
    lane = lax.broadcasted_iota(jnp.int32, values.shape, 1)
    ahead = pltpu.roll(values, LANES - HEAD_DIM // 2, 1)
    behind = pltpu.roll(values, HEAD_DIM // 2, 1)
    return jnp.where(lane % HEAD_DIM < HEAD_DIM // 2, ahead, behind)


def project_kernel(keep, shards, x_ref, w_ref, cos_ref, sin_ref, *outs):
    qkv_ref = outs[-1]
    width = x_ref.shape[2]
    share = width // shards
    gain = jnp.concatenate(
        [w_ref[share * i : share * i + 1, 3 * width : 3 * width + share] for i in range(shards)], axis=1
    ).astype(F32)
    unit, _ = normed(x_ref[0].astype(F32))
    h1 = (unit * gain).astype(BF16)
    if keep:
        outs[0][...] = h1.T
    cosines, sines = cos_ref[0], sin_ref[0]
    for start in range(0, 3 * width, 512):
        part = dot(h1, w_ref[:, start : start + 512])
        for column in range(0, 512, LANES):
            piece = part[:, column : column + LANES]
            if start < 2 * width:
                piece = piece * cosines + swapped(piece) * sines
            if start < width:
                piece = piece * HEAD_DIM**-0.5
            qkv_ref[0, :, start + column : start + column + LANES] = piece.astype(BF16)


def project(x, weight, cosines, sines, first_tile, held, extent, shards):
    batch, rows, width = x.shape
    steps = rows // TILE
    grid = (batch, steps)
    keep = held is None
    block = lambda b, i: (b, i, 0)
    shifted = lambda b, i: (b, i + first_tile, 0)
    qkv_spec = pl.BlockSpec((1, TILE, 3 * width), shifted)
    qkv_shape = jax.ShapeDtypeStruct((batch, extent, 3 * width), BF16)
    in_specs = [
        pl.BlockSpec((1, TILE, width), block),
        pl.BlockSpec(weight.shape, lambda b, i: (0, 0), pipeline_mode=pl.Buffered(1)),
        pl.BlockSpec((1, TILE, LANES), shifted),
        pl.BlockSpec((1, TILE, LANES), shifted),
    ]
    cost = pl.CostEstimate(
        flops=2 * batch * rows * width * 3 * width,
        bytes_accessed=8 * batch * rows * width + 6 * width * width,
        transcendentals=0,
    )
    if keep:
        return pl.pallas_call(
            functools.partial(project_kernel, True, shards),
            grid=grid,
            in_specs=in_specs,
            out_specs=[pl.BlockSpec((width, TILE), lambda b, i: (0, b * steps + i)), qkv_spec],
            out_shape=[jax.ShapeDtypeStruct((width, batch * rows), BF16), qkv_shape],
            compiler_params=params(),
            cost_estimate=cost,
            name="project_own",
        )(x, weight, cosines, sines)

    def halo_kernel(x_ref, w_ref, cos_ref, sin_ref, held_ref, qkv_ref):
        project_kernel(False, shards, x_ref, w_ref, cos_ref, sin_ref, qkv_ref)

    return pl.pallas_call(
        halo_kernel,
        grid=grid,
        in_specs=in_specs + [pl.BlockSpec(memory_space=pl.ANY)],
        out_specs=qkv_spec,
        out_shape=qkv_shape,
        input_output_aliases={4: 0},
        compiler_params=params(),
        cost_estimate=cost,
        name="project_halo",
    )(x, weight, cosines, sines, held)


def edge_masks():
    key = lax.broadcasted_iota(jnp.int32, (TILE, TILE), 0)
    query = lax.broadcasted_iota(jnp.int32, (TILE, TILE), 1)
    return (
        jnp.where(key >= query, 0.0, MASKED).astype(F32),
        jnp.where(key <= query, 0.0, MASKED).astype(F32),
    )


def edge_of(key_tile, query_tile):
    gap = key_tile - query_tile
    return jnp.where(gap == -REACH, 0, jnp.where(gap == REACH, 2, 1))


def low_half(rows):
    return lax.broadcasted_iota(jnp.int32, (rows, LANES), 1) < HEAD_DIM


def split3(values):
    high = values.astype(BF16).astype(F32)
    rest = values - high
    middle = rest.astype(BF16).astype(F32)
    return high, middle, rest - middle


def attend_kernel(tiles, wide, own_ref, lo_ref, hi_ref, q_ref, k_ref, v_ref, ek_ref, eq_ref, o_ref, ot_ref, lse_ref,
                  kx, qx, vx, edges):
    batch = pl.program_id(0)
    stretch, extent = q_ref.shape[1], k_ref.shape[1]

    @pl.when((batch == 0) & (pl.program_id(1) == 0))
    def _():
        before, after = edge_masks()
        edges[0] = before
        edges[1] = jnp.zeros((TILE, TILE), F32)
        edges[2] = after

    low = low_half(extent)
    marks = ek_ref[0]
    ones = jnp.ones((16, extent), BF16)
    for pair in range(wide):
        span = slice(pair * LANES, (pair + 1) * LANES)
        keys = k_ref[0, :, span]
        kx[2 * pair] = jnp.where(low, keys, marks)
        kx[2 * pair + 1] = jnp.where(low, marks, keys)
        turned = q_ref[0, :, span].T
        qx[2 * pair] = jnp.concatenate([turned[:HEAD_DIM], eq_ref[0]], axis=0)
        qx[2 * pair + 1] = jnp.concatenate([eq_ref[0], turned[HEAD_DIM:]], axis=0)
        flipped = v_ref[0, :, span].T
        vx[2 * pair] = jnp.concatenate([flipped[:HEAD_DIM], ones], axis=0)
        vx[2 * pair + 1] = jnp.concatenate([flipped[HEAD_DIM:], ones], axis=0)
    own = own_ref[0]

    def one_tile(index, carry):
        query_tile = own + index
        first, last = lo_ref[batch, query_tile], hi_ref[batch, query_tile]
        columns = pl.ds(pl.multiple_of(index * TILE, TILE), TILE)

        def some(count):
            places, masks = [], []
            for step in range(count):
                key_tile = first + step
                places.append(pl.multiple_of(lax.rem(key_tile - own + tiles, tiles) * TILE, TILE))
                masks.append(edge_of(key_tile, query_tile))

            def score(head):
                return [
                    dot(kx[head, pl.ds(place, TILE), :], qx[head, :, columns]) + edges[mask]
                    for place, mask in zip(places, masks)
                ]

            heads = 2 * wide
            scores = {head: score(head) for head in range(min(1, heads))}
            mixed, waiting = [], []

            def close_head(head, top, powers):
                sums = dot(
                    jnp.concatenate([vx[head, :, pl.ds(place, TILE)] for place in places], axis=1),
                    jnp.concatenate(powers, axis=0),
                )
                total = sums[HEAD_DIM : HEAD_DIM + 1]
                mixed.append(sums[:HEAD_DIM] * (1.0 / total))
                lse_ref[0, head // 2, head % 2 : head % 2 + 1, columns] = top + jnp.log(total)
                if head % 2 == 1:
                    both = jnp.concatenate(mixed[-2:], axis=0)
                    span = slice(head // 2 * LANES, (head // 2 + 1) * LANES)
                    ot_ref[span, columns] = both.astype(BF16)
                    o_ref[0, columns, span] = both.T.astype(BF16)

            for head in range(heads):
                if head + 1 < heads:
                    scores[head + 1] = score(head + 1)
                parts = scores.pop(head)
                top = parts[0]
                for part in parts[1:]:
                    top = jnp.maximum(top, part)
                top = jnp.max(top, axis=0, keepdims=True)
                powers = [jnp.exp(part - top).astype(BF16) for part in parts]
                waiting.append((head, top, powers))
                if len(waiting) > 1:
                    close_head(*waiting.pop(0))
            for item in waiting:
                close_head(*item)

        for count in range(1, 2 * REACH + 2):
            pl.when(last - first == count)(functools.partial(some, count))
        return carry

    lax.fori_loop(0, stretch // TILE, one_tile, 0)


def attend(own, lows, highs, qkv, marks_k, marks_q, stretch):
    batch, extent, _ = qkv.shape
    tiles = extent // TILE
    width = PAIRS * LANES
    wide = WIDE
    groups = PAIRS // wide
    spec = lambda rows, offset: pl.BlockSpec((1, rows, wide * LANES), lambda b, p, *_: (b, 0, p + offset))
    per = pl.BlockSpec((1, extent, LANES), lambda b, p, *_: (b, 0, 0))
    return pl.pallas_call(
        functools.partial(attend_kernel, tiles, wide),
        grid_spec=pltpu.PrefetchScalarGridSpec(
            num_scalar_prefetch=3,
            grid=(batch, groups),
            in_specs=[
                spec(stretch, 0),
                spec(extent, groups),
                spec(extent, 2 * groups),
                per,
                pl.BlockSpec((1, HEAD_DIM, stretch), lambda b, p, *_: (b, 0, 0)),
            ],
            out_specs=[
                spec(stretch, 0),
                pl.BlockSpec((wide * LANES, stretch), lambda b, p, *_: (p, b)),
                pl.BlockSpec((1, wide, 2, stretch), lambda b, p, *_: (b, p, 0, 0)),
            ],
            scratch_shapes=[
                pltpu.VMEM((2 * wide, extent, LANES), BF16),
                pltpu.VMEM((2 * wide, LANES, stretch), BF16),
                pltpu.VMEM((2 * wide, HEAD_DIM + 16, extent), BF16),
                pltpu.VMEM((3, TILE, TILE), F32),
            ],
        ),
        out_shape=[
            jax.ShapeDtypeStruct((batch, stretch, width), BF16),
            jax.ShapeDtypeStruct((width, batch * stretch), BF16),
            jax.ShapeDtypeStruct((batch, PAIRS, 2, stretch), F32),
        ],
        compiler_params=params(),
        cost_estimate=pl.CostEstimate(
            flops=2 * 2 * HEADS * batch * stretch * extent * 128, bytes_accessed=32 * 1024 * 1024, transcendentals=0
        ),
        name="attend",
    )(own, lows, highs, qkv, qkv, qkv, marks_k, marks_q)


def attend_back_kernel(tiles, wide, own_ref, lo_ref, hi_ref, q_ref, k_ref, v_ref, do_ref, doh_ref, st_ref, sth_ref,
                       ek_ref, eq_ref, cos_ref, sin_ref, out_ref,
                       kx, vx, qx, dx, dn, kt, dqt, edges):
    batch = pl.program_id(0)
    extent = k_ref.shape[1]
    stretch = do_ref.shape[1]
    mine = stretch // TILE
    heads = 2 * wide

    @pl.when((batch == 0) & (pl.program_id(1) == 0))
    def _():
        before, after = edge_masks()
        edges[0] = before
        edges[1] = jnp.zeros((TILE, TILE), F32)
        edges[2] = after

    low = low_half(extent)
    marks = ek_ref[0]
    lane = lax.broadcasted_iota(jnp.int32, (extent, LANES), 1) % HEAD_DIM
    units = jnp.where((lane >= 8) & (lane < 11), 1.0, 0.0).astype(BF16)
    row = lax.broadcasted_iota(jnp.int32, (HEAD_DIM, extent), 0)
    label_rows = eq_ref[0].astype(F32)
    dn[:stretch] = do_ref[0]
    dn[stretch:] = doh_ref[0]
    for pair in range(wide):
        span = slice(pair * LANES, (pair + 1) * LANES)
        keys, values = k_ref[0, :, span], v_ref[0, :, span]
        kx[2 * pair] = jnp.where(low, keys, marks)
        kx[2 * pair + 1] = jnp.where(low, marks, keys)
        kt[span] = keys.T
        vx[2 * pair] = jnp.where(low, values, units)
        vx[2 * pair + 1] = jnp.where(low, units, values)
        turned, flipped = q_ref[0, :, span].T, dn[:, span].T
        stats = jnp.concatenate([st_ref[0, pair], sth_ref[0, pair]], axis=1)
        for half in range(2):
            lse = split3(stats[half : half + 1])
            delta = split3(stats[half + 2 : half + 3])
            mark, shift = label_rows, jnp.zeros((HEAD_DIM, extent), F32)
            for place in range(3):
                mark = jnp.where(row == 8 + place, -lse[place], mark)
                shift = jnp.where(row == 8 + place, -delta[place], shift)
            mark, shift = mark.astype(BF16), shift.astype(BF16)
            rows = slice(half * HEAD_DIM, (half + 1) * HEAD_DIM)
            order = (lambda a, b: [a, b]) if half == 0 else (lambda a, b: [b, a])
            qx[2 * pair + half] = jnp.concatenate(order(turned[rows], mark), axis=0)
            dx[2 * pair + half] = jnp.concatenate(order(flipped[rows], shift), axis=0)

    own = own_ref[0]
    dqt[...] = jnp.zeros_like(dqt)
    low_tile = low_half(TILE)

    def place(tile):
        return pl.ds(pl.multiple_of(lax.rem(tile - own + tiles, tiles) * TILE, TILE), TILE)

    def some(key_tile, begin, count, key_grad, out_rows):
        rows = place(key_tile)
        columns = [place(begin + step) for step in range(count)]
        masks = [edge_of(key_tile, begin + step) for step in range(count)]
        items = [(head, step) for head in range(heads) for step in range(count)]
        powers, slopes, sums = {}, {}, {}

        def first_products(head, step):
            score = dot(kx[head, rows, :], qx[head, :, columns[step]]) + edges[masks[step]]
            return score, dot(vx[head, rows, :], dx[head, :, columns[step]])

        def last_products(head, step):
            span = slice(head * HEAD_DIM, (head + 1) * HEAD_DIM)
            dqt[span, columns[step]] += dot(kt[span, rows], slopes[head][step])
            if not key_grad or step + 1 < count:
                return
            pair = slice(head // 2 * LANES, (head // 2 + 1) * LANES)
            grads = jnp.concatenate([dn[column, pair] for column in columns], axis=0)
            queries = jnp.concatenate([q_ref[0, column, pair] for column in columns], axis=0)
            sums[head] = (
                dot(jnp.concatenate(slopes.pop(head), axis=1), queries),
                dot(jnp.concatenate(powers.pop(head), axis=1), grads),
            )
            if head % 2 == 1:
                key_sum, value_sum = (jnp.where(low_tile, a, b) for a, b in zip(sums[head - 1], sums[head]))
                cosines, sines = cos_ref[0, out_rows, :], sin_ref[0, out_rows, :]
                out_ref[1, 0, out_rows, pair] = (key_sum * cosines - swapped(key_sum) * sines).astype(BF16)
                out_ref[2, 0, out_rows, pair] = value_sum.astype(BF16)

        ahead = [first_products(*items[0])]
        for index, (head, step) in enumerate(items):
            if index + 1 < len(items):
                ahead.append(first_products(*items[index + 1]))
            score, slope = ahead.pop(0)
            power = jnp.exp(score)
            powers.setdefault(head, []).append(power.astype(BF16))
            slopes.setdefault(head, []).append((power * slope).astype(BF16))
            if index >= 1:
                last_products(*items[index - 1])
        last_products(*items[-1])

    def own_keys(index, carry):
        key_tile = own + index
        first, last = lo_ref[batch, key_tile], hi_ref[batch, key_tile]
        out_rows = pl.ds(pl.multiple_of(index * TILE, TILE), TILE)
        for count in range(1, 2 * REACH + 2):
            pl.when(last - first == count)(functools.partial(some, key_tile, first, count, True, out_rows))
        return carry

    lax.fori_loop(0, mine, own_keys, 0)

    def other_keys(mem, carry):
        ahead = own + mem
        key_tile = jnp.where(ahead < own + mine + REACH, ahead, ahead - tiles)
        if tiles == mine + REACH:
            key_tile = jnp.where(own == 0, ahead, ahead - tiles)
        valid = (key_tile >= 0) & (key_tile < lo_ref.shape[1])
        safe = jnp.where(valid, key_tile, 0)
        begin = jnp.maximum(lo_ref[batch, safe], own)
        end = jnp.where(valid, jnp.minimum(hi_ref[batch, safe], own + mine), begin)
        for count in range(1, min(REACH, mine) + 1):
            pl.when(end - begin == count)(functools.partial(some, safe, begin, count, False, None))
        return carry

    lax.fori_loop(mine, tiles, other_keys, 0)
    for pair in range(wide):
        span = slice(pair * LANES, (pair + 1) * LANES)
        raw = dqt[span, :stretch].T * HEAD_DIM**-0.5
        out_ref[0, 0, :, span] = (raw * cos_ref[0] - swapped(raw) * sin_ref[0]).astype(BF16)


def attend_back(own, lows, highs, qkv, grads, grads_halo, stats, stats_halo, marks_k, marks_q, cosines, sines):
    batch, extent, _ = qkv.shape
    stretch, width = grads.shape[1:]
    halo = extent - stretch
    tiles = extent // TILE
    wide = WIDE_BACK
    groups = PAIRS // wide
    spec = lambda rows, offset: pl.BlockSpec((1, rows, wide * LANES), lambda b, p, *_: (b, 0, p + offset))
    per = lambda rows: pl.BlockSpec((1, rows, LANES), lambda b, p, *_: (b, 0, 0))
    numbers = lambda rows: pl.BlockSpec((1, wide, 4, rows), lambda b, p, *_: (b, p, 0, 0))
    return pl.pallas_call(
        functools.partial(attend_back_kernel, tiles, wide),
        grid_spec=pltpu.PrefetchScalarGridSpec(
            num_scalar_prefetch=3,
            grid=(batch, groups),
            in_specs=[
                spec(extent, 0),
                spec(extent, groups),
                spec(extent, 2 * groups),
                spec(stretch, 0),
                spec(halo, 0),
                numbers(stretch),
                numbers(halo),
                per(extent),
                pl.BlockSpec((1, HEAD_DIM, extent), lambda b, p, *_: (b, 0, 0)),
                per(stretch),
                per(stretch),
            ],
            out_specs=pl.BlockSpec((3, 1, stretch, wide * LANES), lambda b, p, *_: (0, b, 0, p)),
            scratch_shapes=[
                pltpu.VMEM((2 * wide, extent, LANES), BF16),
                pltpu.VMEM((2 * wide, extent, LANES), BF16),
                pltpu.VMEM((2 * wide, LANES, extent), BF16),
                pltpu.VMEM((2 * wide, LANES, extent), BF16),
                pltpu.VMEM((extent, wide * LANES), BF16),
                pltpu.VMEM((wide * LANES, extent), BF16),
                pltpu.VMEM((wide * LANES, extent), F32),
                pltpu.VMEM((3, TILE, TILE), F32),
            ],
        ),
        out_shape=jax.ShapeDtypeStruct((3, batch, stretch, width), BF16),
        compiler_params=params(),
        cost_estimate=pl.CostEstimate(
            flops=5 * 2 * HEADS * batch * stretch * extent * 128, bytes_accessed=64 * 1024 * 1024, transcendentals=0
        ),
        name="attend_back",
    )(own, lows, highs, qkv, qkv, qkv, grads, grads_halo, stats, stats_halo, marks_k, marks_q, cosines, sines)


def feed_kernel(x_ref, o_ref, g_ref, gain_ref, w_ref, wd_ref,
                out_ref, h2t_ref, hidt_ref, slopes_ref, dr_ref, do_ref, delta_ref):
    mixed = o_ref[0]
    seeds = g_ref[0]
    gain = gain_ref[...]
    width = mixed.shape[1]
    w_out = slice(2 * FF_PAD, 2 * FF_PAD + width)
    r1 = x_ref[0].astype(F32) + dot(mixed, w_ref[:, w_out])
    unit, inverse = normed(r1)
    h2 = (unit * gain).astype(BF16)
    h2t_ref[...] = h2.T
    total = r1
    back = jnp.zeros_like(r1)
    edges = list(range(0, FF - 511, 512))
    for start, stop in zip(edges, edges[1:] + [FF]):
        gates, ups = slice(start, stop), slice(FF_PAD + start, FF_PAD + stop)
        gate = dot(h2, w_ref[:, gates])
        up = dot(h2, w_ref[:, ups])
        grad = dot(seeds, wd_ref[start:stop, :], NT)
        phi = 0.5 + 0.5 * lax.erf(gate * (0.5**0.5))
        bell = jnp.exp(gate * gate * -0.5) * 0.3989422804014327
        act = gate * phi
        hid = (act * up).astype(BF16)
        grad_gate = (grad * up * (phi + gate * bell)).astype(BF16)
        grad_up = (grad * act).astype(BF16)
        hidt_ref[start:stop, :] = hid.T
        slopes_ref[0, :, gates] = grad_gate
        slopes_ref[0, :, ups] = grad_up
        total = total + dot(hid, wd_ref[start:stop, :])
        back = back + dot(grad_gate, w_ref[:, gates], NT) + dot(grad_up, w_ref[:, ups], NT)
    blank = jnp.zeros((TILE, FF_PAD - FF), BF16)
    slopes_ref[0, :, FF:FF_PAD] = blank
    slopes_ref[0, :, FF_PAD + FF : 2 * FF_PAD] = blank
    out_ref[0] = total.astype(BF16)
    dr = seeds.astype(F32) + norm_back(back * gain, unit, inverse)
    dr_ref[0] = dr
    da = dr.astype(BF16)
    slopes_ref[0, :, w_out] = da
    do = dot(da, w_ref[:, w_out], NT).astype(BF16)
    do_ref[0] = do
    product = do.astype(F32) * mixed.astype(F32)
    high = product.astype(BF16)
    rest = (product - high.astype(F32)).astype(BF16)
    head = lax.broadcasted_iota(jnp.int32, (HEADS, width), 0)
    column = lax.broadcasted_iota(jnp.int32, (HEADS, width), 1)
    pick = jnp.where(column // HEAD_DIM == head, 1.0, 0.0).astype(BF16)
    delta = dot(pick, high, NT) + dot(pick, rest, NT)
    for pair in range(PAIRS):
        delta_ref[0, pair] = delta[2 * pair : 2 * pair + 2]


def feed(x, mixed, seeds, gain, w_rest, w_down):
    batch, rows, width = x.shape
    steps = rows // TILE
    block = lambda n: pl.BlockSpec((1, TILE, n), lambda b, i: (b, i, 0))
    turned = lambda n: pl.BlockSpec((n, TILE), lambda b, i: (0, b * steps + i))
    fixed = lambda m, n: pl.BlockSpec((m, n), lambda b, i: (0, 0), pipeline_mode=pl.Buffered(1))
    shape = lambda n, t: jax.ShapeDtypeStruct((batch, rows, n), t)
    columns = w_rest.shape[1]
    return pl.pallas_call(
        feed_kernel,
        grid=(batch, steps),
        in_specs=[
            block(width), block(width), block(width), fixed(1, width), fixed(width, columns), fixed(FF, width),
        ],
        out_specs=[
            block(width), turned(width), turned(FF), block(columns), block(width), block(width),
            pl.BlockSpec((1, PAIRS, 2, TILE), lambda b, i: (b, 0, 0, i)),
        ],
        out_shape=[
            shape(width, BF16),
            jax.ShapeDtypeStruct((width, batch * rows), BF16),
            jax.ShapeDtypeStruct((FF, batch * rows), BF16),
            shape(columns, BF16),
            shape(width, F32),
            shape(width, BF16),
            jax.ShapeDtypeStruct((batch, PAIRS, 2, rows), F32),
        ],
        compiler_params=params(),
        cost_estimate=pl.CostEstimate(
            flops=2 * batch * rows * width * (6 * FF + 2 * width), bytes_accessed=64 * 1024 * 1024, transcendentals=0
        ),
        name="feed",
    )(x, mixed, seeds, gain, w_rest, w_down)


def weigh_kernel(left_ref, right_ref, *outs):
    outs[-1][...] = dot(left_ref[...], right_ref[...].reshape(right_ref.shape[-2:])).astype(BF16)


def weigh(left, right, name, left_block, right_block, out_block, left_map, right_map, out_map, steps, shape, held=None):
    specs = [pl.BlockSpec(left_block, left_map), pl.BlockSpec(right_block, right_map)]
    arrays = [left, right]
    if held is not None:
        specs.append(pl.BlockSpec(memory_space=pl.ANY))
        arrays.append(held)
    rows, columns = out_block
    return pl.pallas_call(
        weigh_kernel,
        grid=(steps,),
        in_specs=specs,
        out_specs=pl.BlockSpec(out_block, out_map),
        out_shape=jax.ShapeDtypeStruct(shape, BF16),
        input_output_aliases={} if held is None else {2: 0},
        compiler_params=params(),
        cost_estimate=pl.CostEstimate(
            flops=2 * steps * rows * columns * left.shape[1], bytes_accessed=16 * 1024 * 1024, transcendentals=0
        ),
        name=name,
    )(*arrays)


MESH = pl.DeviceIdType.MESH
CUT = 512
LAGS = (1, 3, 5, 6, 7, 8)


def close_kernel(blocks, seqs, reps, h1t_ref, right_ref, three_ref, w_ref, x_ref, dr_ref, gain_ref, gi_ref, sum_ref,
                 prod, kept0, kept1x, kept1y, kept2, s0, r0, s1x, r1x, s1y, r1y, s2x, r2x, s2y, r2y,
                 mine, ends, half, others, whole, send_sem, recv_sem):
    step = pl.program_id(0)
    width = h1t_ref.shape[0]
    share = mine.shape[1]
    seq, dp, rep = lax.axis_index("seq"), lax.axis_index("dp"), lax.axis_index("rep")
    core, side = lax.rem(dp, 2), dp // 2
    mate, across = dp + 1 - 2 * core, lax.rem(dp + 2, 4)
    seq_peers = [lax.rem(seq + hop, seqs) for hop in range(1, seqs)]
    inner = (rep == 1) | (rep == 2)
    beside = rep + 1 - 2 * lax.rem(rep, 2)
    slot_seq, slot_side, slot_in = 1, seqs, seqs + 1

    def copy(source, target, n, slot, device):
        return pltpu.make_async_remote_copy(
            src_ref=source, dst_ref=target, send_sem=send_sem.at[n, slot], recv_sem=recv_sem.at[n, slot],
            device_id=device, device_id_type=MESH,
        )

    def rows(first, count):
        return pl.ds(pl.multiple_of(first * share, share), count * share)

    def to_mate(n):
        return [copy(s0.at[n], r0.at[n], n, 0, {"dp": mate})]

    def to_seq(n, source, target):
        return [
            copy(source.at[n // 2, hop], target.at[n // 2, hop], n, slot_seq + hop, {"seq": peer})
            for hop, peer in enumerate(seq_peers)
        ]

    def to_side(n, source, target):
        return [copy(source.at[n // 2], target.at[n // 2], n, slot_side, {"dp": across})]

    def inwards(n):
        return copy(mine.at[n], ends.at[n], n, slot_in, {"rep": beside})

    def between(n):
        return copy(half.at[n], others.at[n], n, slot_in + 1, {"rep": reps - 1 - rep})

    def outwards(n):
        return copy(whole.at[n], whole.at[n], n, slot_in + 2, {"rep": beside})

    def start(copies):
        for each in copies:
            each.start()

    def wait(copies):
        for each in copies:
            each.wait()

    @pl.when(step == 0)
    def _():
        barrier = pltpu.get_barrier_semaphore()
        partners = [{"dp": mate}, {"dp": across}]
        partners += [{"seq": peer} for peer in seq_peers] + [{"rep": beside}]
        for partner in partners:
            pl.semaphore_signal(barrier, inc=1, device_id=partner, device_id_type=MESH)

        @pl.when(inner)
        def _():
            pl.semaphore_signal(barrier, inc=1, device_id={"rep": reps - 1 - rep}, device_id_type=MESH)
            pl.semaphore_wait(barrier, len(partners) + 1)

        @pl.when(jnp.logical_not(inner))
        def _():
            pl.semaphore_wait(barrier, len(partners))

    @pl.when(step < blocks)
    def _():
        prod[...] = dot(h1t_ref[...], right_ref[0])
        for place in range(2 * seqs):
            span = slice(place * share, (place + 1) * share)
            s0[step, span, :] = prod[rows(2 * place + 1 - core, 1), :].astype(BF16)
        start(to_mate(step))
        for place in range(2 * seqs):
            span = slice(place * share, (place + 1) * share)
            kept0[step % 2, span, :] = prod[rows(2 * place + core, 1), :]

    @pl.when((step >= blocks) & (step < blocks + gi_steps(three_ref, right_ref)))
    def _():
        back = None
        for part in range(3):
            term = dot(three_ref[part], w_ref[:, part * width : (part + 1) * width], NT)
            back = term if back is None else back + term
        unit, inverse = normed(x_ref[...].astype(F32))
        gi_ref[...] = dr_ref[...] + norm_back(back * gain_ref[...], unit, inverse)

    n6 = step - LAGS[5]

    @pl.when((n6 >= 0) & (n6 < blocks))
    def _():
        @pl.when(inner)
        def _():
            outwards(n6).wait_send()

        @pl.when(jnp.logical_not(inner))
        def _():
            outwards(n6).wait_recv()

        sum_ref[:, pl.ds(pl.multiple_of(n6 * CUT, CUT), CUT)] = whole[n6].astype(F32)

    n5 = step - LAGS[4]

    @pl.when((n5 >= 0) & (n5 < blocks) & inner)
    def _():
        between(n5).wait()
        whole[n5] = (half[n5].astype(F32) + others[n5].astype(F32)).astype(BF16)
        outwards(n5).start()

    n4 = step - LAGS[3]

    @pl.when((n4 >= 0) & (n4 < blocks) & inner)
    def _():
        inwards(n4).wait_recv()
        half[n4] = (mine[n4].astype(F32) + ends[n4].astype(F32)).astype(BF16)
        between(n4).start()

    @pl.when((n4 >= 0) & (n4 < blocks) & jnp.logical_not(inner))
    def _():
        inwards(n4).wait_send()

    n3 = step - LAGS[2]

    @pl.when((n3 >= 0) & (n3 < blocks))
    def _():
        total = kept2[n3 % 2]

        @pl.when(n3 % 2 == 0)
        def _():
            wait(to_side(n3, s2y, r2y))
            mine[n3] = (total + r2y[n3 // 2].astype(F32)).astype(BF16)

        @pl.when(n3 % 2 == 1)
        def _():
            wait(to_seq(n3, s2x, r2x))
            added = total
            for hop in range(seqs - 1):
                added = added + r2x[n3 // 2, hop].astype(F32)
            mine[n3] = added.astype(BF16)

        @pl.when(jnp.logical_not(inner))
        def _():
            inwards(n3).start()

    n2 = step - LAGS[1]

    @pl.when((n2 >= 0) & (n2 < blocks) & (n2 % 2 == 0))
    def _():
        wait(to_seq(n2, s1x, r1x))
        total = kept1x[...]
        for hop in range(seqs - 1):
            total = total + r1x[n2 // 2, hop].astype(F32)
        kept1x[...] = total
        s2y[n2 // 2] = kept1x[rows(1 - side, 1), :].astype(BF16)
        start(to_side(n2, s2y, r2y))
        kept2[0] = kept1x[rows(side, 1), :]

    @pl.when((n2 >= 0) & (n2 < blocks) & (n2 % 2 == 1))
    def _():
        wait(to_side(n2, s1y, r1y))
        kept1y[...] = kept1y[...] + r1y[n2 // 2].astype(F32)
        for hop, peer in enumerate(seq_peers):
            s2x[n2 // 2, hop] = kept1y[rows(peer, 1), :].astype(BF16)
        start(to_seq(n2, s2x, r2x))
        kept2[1] = kept1y[rows(seq, 1), :]

    n1 = step - LAGS[0]

    @pl.when((n1 >= 0) & (n1 < blocks))
    def _():
        wait(to_mate(n1))
        held = n1 % 2
        kept0[held] = kept0[held] + r0[n1].astype(F32)

        @pl.when(n1 % 2 == 0)
        def _():
            for hop, peer in enumerate(seq_peers):
                s1x[n1 // 2, hop] = kept0[held, rows(2 * peer, 2), :].astype(BF16)
            start(to_seq(n1, s1x, r1x))
            kept1x[...] = kept0[held, rows(2 * seq, 2), :]

        @pl.when(n1 % 2 == 1)
        def _():
            for place in range(seqs):
                s1y[n1 // 2, place * share : (place + 1) * share, :] = kept0[held, rows(2 * place + 1 - side, 1), :].astype(BF16)
            start(to_side(n1, s1y, r1y))
            for place in range(seqs):
                kept1y[place * share : (place + 1) * share, :] = kept0[held, rows(2 * place + side, 1), :]


def gi_steps(three_ref, right_ref):
    return right_ref.shape[1] // three_ref.shape[1]


def close(h1t, slopes, weight, x, dr, gain, seqs, dps, reps):
    assert (dps, reps) == (4, 4)
    width, tokens = h1t.shape
    share = width // (seqs * dps)
    blocks = 3 * width // CUT
    halves = width // CUT
    token_blocks = tokens // TILE
    steps = max(blocks + token_blocks, blocks + LAGS[5])
    late = lambda s: jnp.clip(s - blocks, 0, token_blocks - 1)
    early = lambda s: jnp.minimum(s, blocks - 1)
    fixed = lambda m, n: pl.BlockSpec((m, n), lambda s: (0, 0), pipeline_mode=pl.Buffered(1))
    row = pl.BlockSpec((TILE, width), lambda s: (late(s), 0))
    pairs = (blocks + 1) // 2
    half_rows = 2 * seqs * share
    buffers = lambda *shape: [pltpu.VMEM(shape + (CUT,), BF16)] * 2
    slots = seqs + 4
    return pl.pallas_call(
        functools.partial(close_kernel, blocks, seqs, reps),
        grid=(steps,),
        in_specs=[
            fixed(width, tokens),
            pl.BlockSpec((1, tokens, CUT), lambda s: (early(s) // halves, 0, early(s) % halves)),
            pl.BlockSpec((3, TILE, width), lambda s: (0, late(s), 0)),
            fixed(*weight.shape),
            row,
            row,
            fixed(1, width),
        ],
        out_specs=[row, fixed(share, 3 * width)],
        out_shape=[
            jax.ShapeDtypeStruct((tokens, width), F32),
            jax.ShapeDtypeStruct((share, 3 * width), F32),
        ],
        scratch_shapes=[
            pltpu.VMEM((width, CUT), F32),
            pltpu.VMEM((2, half_rows, CUT), F32),
            pltpu.VMEM((2 * share, CUT), F32),
            pltpu.VMEM((seqs * share, CUT), F32),
            pltpu.VMEM((2, share, CUT), F32),
            *buffers(blocks, half_rows),
            *buffers(pairs, seqs - 1, 2 * share),
            *buffers(pairs, seqs * share),
            *buffers(pairs, seqs - 1, share),
            *buffers(pairs, share),
            *[pltpu.VMEM((blocks, share, CUT), BF16)] * 5,
            pltpu.SemaphoreType.DMA((blocks, slots)),
            pltpu.SemaphoreType.DMA((blocks, slots)),
        ],
        compiler_params=params(collective_id=1, has_side_effects=True),
        cost_estimate=pl.CostEstimate(
            flops=4 * tokens * width * 3 * width, bytes_accessed=48 * 1024 * 1024, transcendentals=0
        ),
        name="close",
    )(h1t, slopes, slopes, weight, x, dr, gain)


def neighbours(block, axis, along):
    count = lax.axis_size(axis)
    rows = block.shape[along]
    if count == 2:
        start = (1 - lax.axis_index(axis)) * (rows - HALF)
        facing = lax.dynamic_slice_in_dim(block, start, HALF, along)
        return lax.ppermute(facing, axis, [(0, 1), (1, 0)])
    step = min(rows, HALF)
    head = lax.slice_in_dim(block, 0, step, axis=along)
    tail = lax.slice_in_dim(block, rows - step, rows, axis=along)
    hops = range(1, HALF // step + 1)
    after = [lax.ppermute(head, axis, [(i + hop, i) for i in range(count - hop)]) for hop in hops]
    before = [lax.ppermute(tail, axis, [(i, i + hop) for i in range(count - hop)]) for hop in reversed(hops)]
    return jnp.concatenate(after + before, axis=along)


def survey(labels, stretch, extent, seq_index, seq_count):
    length = labels.shape[1]
    mem = jnp.arange(extent, dtype=jnp.int32)
    own_start = seq_index * stretch
    wraps = stretch + HALF if seq_count > 2 else jnp.where(seq_index == 0, extent, stretch)
    places = own_start + mem - jnp.where(mem >= wraps, extent, 0)
    padded = jnp.pad(labels, ((0, 0), (HALF, HALF)))
    cut = lambda first, size: lax.dynamic_slice_in_dim(padded, first + HALF, size, 1)
    parts = [cut(own_start, stretch)]
    if seq_count == 2:
        parts.append(cut(jnp.where(seq_index == 0, own_start + stretch, own_start - HALF), HALF))
    else:
        parts += [cut(own_start + stretch, HALF), cut(own_start - HALF, HALF)]
    near = jnp.concatenate(parts, axis=1)
    docs = jnp.arange(DOCS, dtype=jnp.int32)
    starts = jnp.sum(labels[:, :, None] < docs, axis=1, dtype=jnp.int32)
    stops = jnp.sum(labels[:, :, None] <= docs, axis=1, dtype=jnp.int32) - 1
    same = near[:, :, None] == docs
    positions = places - jnp.sum(jnp.where(same, starts[:, None, :], 0), axis=-1)
    lane = jnp.arange(LANES, dtype=jnp.int32)
    half_dim = HEAD_DIM // 2
    frequency = THETA ** (-((lane % half_dim).astype(F32) * 2.0 / HEAD_DIM))
    angles = positions.astype(F32)[:, :, None] * frequency
    cosines = jnp.cos(angles)
    sines = jnp.sin(angles) * jnp.where(lane % HEAD_DIM < half_dim, -1.0, 1.0)
    slot = lane % HEAD_DIM
    marks_k = jnp.where(
        slot < DOCS,
        jnp.where(near[:, :, None] == slot, 0.0, MASKED),
        jnp.where((slot >= 8) & (slot < 11), 1.0, 0.0),
    ).astype(BF16)
    kind = jnp.arange(HEAD_DIM, dtype=jnp.int32)[None, :, None]
    marks_q = jnp.where((kind < DOCS) & (near[:, None, :] == kind), 1.0, 0.0).astype(BF16)
    at = jnp.arange(length // TILE, dtype=jnp.int32) * TILE
    first_label, last_label = labels[:, ::TILE], labels[:, TILE - 1 :: TILE]
    pick = lambda table, which: jnp.sum(
        jnp.where(which[:, :, None] == docs, table[:, None, :], 0), axis=-1
    )
    lows = jnp.maximum(pick(starts, first_label), at - HALF) // TILE
    highs = jnp.minimum(pick(stops, last_label), at + TILE - 1 + HALF) // TILE + 1
    own = (own_start // TILE).astype(jnp.int32).reshape(1)
    return own, lows, highs, cosines, sines, marks_k, marks_q


def body(inputs, segments, cotangent, attn_gain, mlp_gain, w_qkv, w_out, w_in, w_down):
    stretch, width = inputs.shape[2:]
    length = segments.shape[2]
    x = inputs.reshape(-1, stretch, width)
    seeds = cotangent.reshape(-1, stretch, width)
    labels = segments.reshape(-1, length)
    batch = x.shape[0]
    group = ("seq", "dp")
    seq_index = lax.axis_index("seq")
    seq_count = lax.axis_size("seq")

    share = attn_gain.shape[0]
    shards = width // share
    x_halo = neighbours(x, "seq", 1)
    gather = lambda shard: lax.all_gather(shard, group, axis=0, tiled=True)
    gain_rows = jnp.pad(jnp.stack([attn_gain, mlp_gain]), ((0, share - 2), (0, LANES - share)))
    qkv_full = gather(jnp.concatenate([w_qkv, gain_rows], axis=1))
    blank = jnp.zeros((share, FF_PAD - FF), BF16)
    rest_full = gather(jnp.concatenate([w_in[:, :FF], blank, w_in[:, FF:], blank, w_out], axis=1))
    down_full = gather(w_down)
    gains = qkv_full[:, 3 * width : 3 * width + share].reshape(shards, share, share).astype(F32)
    gain_one, gain_two = gains[:, 0].reshape(1, width), gains[:, 1].reshape(1, width)

    halo = x_halo.shape[1]
    extent = stretch + halo
    own, lows, highs, cosines, sines, marks_k, marks_q = survey(labels, stretch, extent, seq_index, seq_count)

    h1t, qkv = project(x, qkv_full, cosines, sines, 0, None, extent, shards)
    qkv = project(x_halo, qkv_full, cosines, sines, stretch // TILE, qkv, extent, shards)
    mixed, mixed_t, lse = attend(own, lows, highs, qkv, marks_k, marks_q, stretch)
    result, h2t, hidt, slopes, dr, do, delta = feed(x, mixed, seeds, gain_two, rest_full, down_full)
    stats = jnp.concatenate([lse, delta], axis=2)
    do_halo = neighbours(do, "seq", 1)
    stats_halo = neighbours(stats, "seq", 3)

    scatter = lambda part: lax.psum_scatter(part, group, scatter_dimension=0, tiled=True)
    tokens = batch * stretch
    columns = rest_full.shape[1]
    flat = slopes.reshape(tokens, columns)
    step = FF_PAD * 2 // 7
    part_rest = weigh(
        h2t, flat, "weigh_in", (width, tokens), (tokens, step), (width, step),
        lambda n: (0, 0), lambda n: (0, n), lambda n: (0, n), 7, (width, columns),
    )
    first = FF_PAD * 2 // TILE
    part_rest = weigh(
        mixed_t, flat, "weigh_out", (width, tokens), (tokens, TILE), (width, TILE),
        lambda n: (0, 0), lambda n: (0, n + first), lambda n: (0, n + first), width // TILE, (width, columns), part_rest,
    )
    shard_rest = scatter(part_rest)
    do_halo, stats_halo, hidt = lax.optimization_barrier((do_halo, stats_halo, hidt))
    step = FF // 4
    part_down = weigh(
        hidt, seeds.reshape(tokens, width), "weigh_down", (step, tokens), (tokens, width), (step, width),
        lambda n: (n, 0), lambda n: (0, 0), lambda n: (n, 0), 4, (FF, width),
    )
    shard_down = scatter(part_down)
    do_halo, stats_halo, part_down, part_rest = lax.optimization_barrier((do_halo, stats_halo, part_down, part_rest))
    rest_sum, down_sum = lax.psum((shard_rest, shard_down), "rep")
    slopes_qkv = attend_back(
        own, lows, highs, qkv, do, do_halo, stats, stats_halo, marks_k, marks_q, cosines, sines
    )
    grad_x, grad_qkv = close(
        h1t, slopes_qkv.reshape(3, tokens, width), qkv_full, x.reshape(tokens, width), dr.reshape(tokens, width),
        gain_one, seq_count, lax.axis_size("dp"), lax.axis_size("rep"),
    )
    rest_sum = rest_sum.astype(F32)
    grad_in = jnp.concatenate([rest_sum[:, :FF], rest_sum[:, FF_PAD : FF_PAD + FF]], axis=1)
    grad_attn_gain = jnp.sum(grad_qkv * w_qkv.astype(F32), axis=1) / attn_gain.astype(F32)
    grad_mlp_gain = jnp.sum(grad_in * w_in.astype(F32), axis=1) / mlp_gain.astype(F32)
    return (
        result.reshape(cotangent.shape),
        grad_x.reshape(inputs.shape),
        grad_attn_gain,
        grad_mlp_gain,
        grad_qkv,
        rest_sum[:, 2 * FF_PAD :],
        grad_in,
        down_sum.astype(F32),
    )


def solution(mesh):
    return jax.shard_map(
        body,
        mesh=mesh,
        in_specs=(
            P(None, ("dp", "rep"), "seq", None),
            P(None, ("dp", "rep"), None),
            P(None, ("dp", "rep"), "seq", None),
            P(("seq", "dp")),
            P(("seq", "dp")),
            P(("seq", "dp"), None),
            P(("seq", "dp"), None),
            P(("seq", "dp"), None),
            P(("seq", "dp"), None),
        ),
        out_specs=(
            P(None, ("dp", "rep"), "seq", None),
            P(None, ("dp", "rep"), "seq", None),
            P(("seq", "dp")),
            P(("seq", "dp")),
            P(("seq", "dp"), None),
            P(("seq", "dp"), None),
            P(("seq", "dp"), None),
            P(("seq", "dp"), None),
        ),
        check_vma=False,
    )
```

```python
import functools

import jax
import jax.numpy as jnp
from jax import lax
from jax.experimental import pallas as pl
from jax.experimental.pallas import tpu as pltpu
from jax.sharding import PartitionSpec as P

HEADS = 16
HEAD_DIM = 64
FF = 2624
HALF = 512
DOCS = 7

EPS = 1e-05
THETA = 10000.0
MASKED = -1e30

TILE = 256
CUT = 512
REACH = HALF // TILE
LANES = 128
FF_PAD = -(-FF // LANES) * LANES
PAIRS = HEADS // 2
WIDE = 4
WIDE_BACK = 2
VMEM = 60 * 1024 * 1024

F32 = jnp.float32
BF16 = jnp.bfloat16

MESH = pl.DeviceIdType.MESH

NN = (((1,), (0,)), ((), ()))
NT = (((1,), (1,)), ((), ()))


def dot(left, right, dims=NN):
    return lax.dot_general(left, right, dims, preferred_element_type=F32)


def params(**more):
    return pltpu.CompilerParams(vmem_limit_bytes=VMEM, **more)


def normed(values):
    centre = values - jnp.mean(values, axis=-1, keepdims=True)
    spread = jnp.mean(centre * centre, axis=-1, keepdims=True)
    inverse = lax.rsqrt(spread + EPS)
    return centre * inverse, inverse


def norm_back(grads, unit, inverse):
    first = jnp.mean(grads, axis=-1, keepdims=True)
    second = jnp.mean(grads * unit, axis=-1, keepdims=True)
    return (grads - first - unit * second) * inverse


def swapped(values):
    lane = lax.broadcasted_iota(jnp.int32, values.shape, 1)
    ahead = pltpu.roll(values, LANES - HEAD_DIM // 2, 1)
    behind = pltpu.roll(values, HEAD_DIM // 2, 1)
    return jnp.where(lane % HEAD_DIM < HEAD_DIM // 2, ahead, behind)


def project_kernel(keep, shards, x_ref, w_ref, cos_ref, sin_ref, *outs):
    qkv_ref = outs[-1]
    width = x_ref.shape[2]
    share = width // shards
    gain = jnp.concatenate(
        [w_ref[share * i : share * i + 1, 3 * width : 3 * width + share] for i in range(shards)], axis=1
    ).astype(F32)
    unit, _ = normed(x_ref[0].astype(F32))
    h1 = (unit * gain).astype(BF16)
    if keep:
        outs[0][...] = h1.T
    cosines, sines = cos_ref[0], sin_ref[0]
    for start in range(0, 3 * width, 512):
        part = dot(h1, w_ref[:, start : start + 512])
        for column in range(0, 512, LANES):
            piece = part[:, column : column + LANES]
            if start < 2 * width:
                piece = piece * cosines + swapped(piece) * sines
            if start < width:
                piece = piece * HEAD_DIM**-0.5
            qkv_ref[0, :, start + column : start + column + LANES] = piece.astype(BF16)


def project(x, weight, cosines, sines, first_tile, held, extent, shards):
    batch, rows, width = x.shape
    steps = rows // TILE
    grid = (batch, steps)
    keep = held is None
    block = lambda b, i: (b, i, 0)
    shifted = lambda b, i: (b, i + first_tile, 0)
    qkv_spec = pl.BlockSpec((1, TILE, 3 * width), shifted)
    qkv_shape = jax.ShapeDtypeStruct((batch, extent, 3 * width), BF16)
    in_specs = [
        pl.BlockSpec((1, TILE, width), block),
        pl.BlockSpec(weight.shape, lambda b, i: (0, 0), pipeline_mode=pl.Buffered(1)),
        pl.BlockSpec((1, TILE, LANES), shifted),
        pl.BlockSpec((1, TILE, LANES), shifted),
    ]
    cost = pl.CostEstimate(
        flops=2 * batch * rows * width * 3 * width,
        bytes_accessed=8 * batch * rows * width + 6 * width * width,
        transcendentals=0,
    )
    if keep:
        return pl.pallas_call(
            functools.partial(project_kernel, True, shards),
            grid=grid,
            in_specs=in_specs,
            out_specs=[pl.BlockSpec((width, TILE), lambda b, i: (0, b * steps + i)), qkv_spec],
            out_shape=[jax.ShapeDtypeStruct((width, batch * rows), BF16), qkv_shape],
            compiler_params=params(),
            cost_estimate=cost,
            name="project_own",
        )(x, weight, cosines, sines)

    def halo_kernel(x_ref, w_ref, cos_ref, sin_ref, held_ref, qkv_ref):
        project_kernel(False, shards, x_ref, w_ref, cos_ref, sin_ref, qkv_ref)

    return pl.pallas_call(
        halo_kernel,
        grid=grid,
        in_specs=in_specs + [pl.BlockSpec(memory_space=pl.ANY)],
        out_specs=qkv_spec,
        out_shape=qkv_shape,
        input_output_aliases={4: 0},
        compiler_params=params(),
        cost_estimate=cost,
        name="project_halo",
    )(x, weight, cosines, sines, held)


def edge_masks():
    key = lax.broadcasted_iota(jnp.int32, (TILE, TILE), 0)
    query = lax.broadcasted_iota(jnp.int32, (TILE, TILE), 1)
    return (
        jnp.where(key >= query, 0.0, MASKED).astype(F32),
        jnp.where(key <= query, 0.0, MASKED).astype(F32),
    )


def edge_of(key_tile, query_tile):
    gap = key_tile - query_tile
    return jnp.where(gap == -REACH, 0, jnp.where(gap == REACH, 2, 1))


def low_half(rows):
    return lax.broadcasted_iota(jnp.int32, (rows, LANES), 1) < HEAD_DIM


def split3(values):
    high = values.astype(BF16).astype(F32)
    rest = values - high
    middle = rest.astype(BF16).astype(F32)
    return high, middle, rest - middle


def attend_kernel(tiles, wide, own_ref, lo_ref, hi_ref, q_ref, k_ref, v_ref, ek_ref, eq_ref, o_ref, ot_ref, lse_ref,
                  kx, qx, vx, edges):
    batch = pl.program_id(0)
    stretch, extent = q_ref.shape[1], k_ref.shape[1]

    @pl.when((batch == 0) & (pl.program_id(1) == 0))
    def _():
        before, after = edge_masks()
        edges[0] = before
        edges[1] = jnp.zeros((TILE, TILE), F32)
        edges[2] = after

    low = low_half(extent)
    marks = ek_ref[0]
    ones = jnp.ones((16, extent), BF16)
    for pair in range(wide):
        span = slice(pair * LANES, (pair + 1) * LANES)
        keys = k_ref[0, :, span]
        kx[2 * pair] = jnp.where(low, keys, marks)
        kx[2 * pair + 1] = jnp.where(low, marks, keys)
        turned = q_ref[0, :, span].T
        qx[2 * pair] = jnp.concatenate([turned[:HEAD_DIM], eq_ref[0]], axis=0)
        qx[2 * pair + 1] = jnp.concatenate([eq_ref[0], turned[HEAD_DIM:]], axis=0)
        flipped = v_ref[0, :, span].T
        vx[2 * pair] = jnp.concatenate([flipped[:HEAD_DIM], ones], axis=0)
        vx[2 * pair + 1] = jnp.concatenate([flipped[HEAD_DIM:], ones], axis=0)
    own = own_ref[0]

    def one_tile(index, carry):
        query_tile = own + index
        first, last = lo_ref[batch, query_tile], hi_ref[batch, query_tile]
        columns = pl.ds(pl.multiple_of(index * TILE, TILE), TILE)

        def some(count):
            places, masks = [], []
            for step in range(count):
                key_tile = first + step
                places.append(pl.multiple_of(lax.rem(key_tile - own + tiles, tiles) * TILE, TILE))
                masks.append(edge_of(key_tile, query_tile))

            def score(head):
                return [
                    dot(kx[head, pl.ds(place, TILE), :], qx[head, :, columns]) + edges[mask]
                    for place, mask in zip(places, masks)
                ]

            heads = 2 * wide
            scores = {head: score(head) for head in range(min(1, heads))}
            mixed, waiting = [], []

            def close_head(head, top, powers):
                sums = dot(
                    jnp.concatenate([vx[head, :, pl.ds(place, TILE)] for place in places], axis=1),
                    jnp.concatenate(powers, axis=0),
                )
                total = sums[HEAD_DIM : HEAD_DIM + 1]
                mixed.append(sums[:HEAD_DIM] * (1.0 / total))
                lse_ref[0, head // 2, head % 2 : head % 2 + 1, columns] = top + jnp.log(total)
                if head % 2 == 1:
                    both = jnp.concatenate(mixed[-2:], axis=0)
                    span = slice(head // 2 * LANES, (head // 2 + 1) * LANES)
                    ot_ref[span, columns] = both.astype(BF16)
                    o_ref[0, columns, span] = both.T.astype(BF16)

            for head in range(heads):
                if head + 1 < heads:
                    scores[head + 1] = score(head + 1)
                parts = scores.pop(head)
                top = parts[0]
                for part in parts[1:]:
                    top = jnp.maximum(top, part)
                top = jnp.max(top, axis=0, keepdims=True)
                powers = [jnp.exp(part - top).astype(BF16) for part in parts]
                waiting.append((head, top, powers))
                if len(waiting) > 1:
                    close_head(*waiting.pop(0))
            for item in waiting:
                close_head(*item)

        for count in range(1, 2 * REACH + 2):
            pl.when(last - first == count)(functools.partial(some, count))
        return carry

    lax.fori_loop(0, stretch // TILE, one_tile, 0)


def attend(own, lows, highs, qkv, marks_k, marks_q, stretch):
    batch, extent, _ = qkv.shape
    tiles = extent // TILE
    width = PAIRS * LANES
    wide = WIDE
    groups = PAIRS // wide
    spec = lambda rows, offset: pl.BlockSpec((1, rows, wide * LANES), lambda b, p, *_: (b, 0, p + offset))
    per = pl.BlockSpec((1, extent, LANES), lambda b, p, *_: (b, 0, 0))
    return pl.pallas_call(
        functools.partial(attend_kernel, tiles, wide),
        grid_spec=pltpu.PrefetchScalarGridSpec(
            num_scalar_prefetch=3,
            grid=(batch, groups),
            in_specs=[
                spec(stretch, 0),
                spec(extent, groups),
                spec(extent, 2 * groups),
                per,
                pl.BlockSpec((1, HEAD_DIM, stretch), lambda b, p, *_: (b, 0, 0)),
            ],
            out_specs=[
                spec(stretch, 0),
                pl.BlockSpec((wide * LANES, stretch), lambda b, p, *_: (p, b)),
                pl.BlockSpec((1, wide, 2, stretch), lambda b, p, *_: (b, p, 0, 0)),
            ],
            scratch_shapes=[
                pltpu.VMEM((2 * wide, extent, LANES), BF16),
                pltpu.VMEM((2 * wide, LANES, stretch), BF16),
                pltpu.VMEM((2 * wide, HEAD_DIM + 16, extent), BF16),
                pltpu.VMEM((3, TILE, TILE), F32),
            ],
        ),
        out_shape=[
            jax.ShapeDtypeStruct((batch, stretch, width), BF16),
            jax.ShapeDtypeStruct((width, batch * stretch), BF16),
            jax.ShapeDtypeStruct((batch, PAIRS, 2, stretch), F32),
        ],
        compiler_params=params(),
        cost_estimate=pl.CostEstimate(
            flops=2 * 2 * HEADS * batch * stretch * extent * 128, bytes_accessed=32 * 1024 * 1024, transcendentals=0
        ),
        name="attend",
    )(own, lows, highs, qkv, qkv, qkv, marks_k, marks_q)


def attend_back_kernel(tiles, wide, own_ref, lo_ref, hi_ref, q_ref, k_ref, v_ref, do_ref, doh_ref, lse_ref, lseh_ref,
                       delta_ref, deltah_ref, ek_ref, eq_ref, cos_ref, sin_ref, out_ref,
                       kx, vx, qx, dx, dn, kt, dqt, edges):
    batch = pl.program_id(0)
    extent = k_ref.shape[1]
    stretch = do_ref.shape[1]
    mine = stretch // TILE
    heads = 2 * wide

    @pl.when((batch == 0) & (pl.program_id(1) == 0))
    def _():
        before, after = edge_masks()
        edges[0] = before
        edges[1] = jnp.zeros((TILE, TILE), F32)
        edges[2] = after

    low = low_half(extent)
    marks = ek_ref[0]
    lane = lax.broadcasted_iota(jnp.int32, (extent, LANES), 1) % HEAD_DIM
    units = jnp.where((lane >= 8) & (lane < 11), 1.0, 0.0).astype(BF16)
    row = lax.broadcasted_iota(jnp.int32, (HEAD_DIM, extent), 0)
    label_rows = eq_ref[0].astype(F32)
    dn[:stretch] = do_ref[0]
    dn[stretch:] = doh_ref[0]
    for pair in range(wide):
        span = slice(pair * LANES, (pair + 1) * LANES)
        keys, values = k_ref[0, :, span], v_ref[0, :, span]
        kx[2 * pair] = jnp.where(low, keys, marks)
        kx[2 * pair + 1] = jnp.where(low, marks, keys)
        kt[span] = keys.T
        vx[2 * pair] = jnp.where(low, values, units)
        vx[2 * pair + 1] = jnp.where(low, units, values)
        turned, flipped = q_ref[0, :, span].T, dn[:, span].T
        lses = jnp.concatenate([lse_ref[0, pair], lseh_ref[0, pair]], axis=1)
        deltas = jnp.concatenate([delta_ref[0, pair], deltah_ref[0, pair]], axis=1)
        for half in range(2):
            lse = split3(lses[half : half + 1])
            delta = split3(deltas[half : half + 1])
            mark, shift = label_rows, jnp.zeros((HEAD_DIM, extent), F32)
            for place in range(3):
                mark = jnp.where(row == 8 + place, -lse[place], mark)
                shift = jnp.where(row == 8 + place, -delta[place], shift)
            mark, shift = mark.astype(BF16), shift.astype(BF16)
            rows = slice(half * HEAD_DIM, (half + 1) * HEAD_DIM)
            order = (lambda a, b: [a, b]) if half == 0 else (lambda a, b: [b, a])
            qx[2 * pair + half] = jnp.concatenate(order(turned[rows], mark), axis=0)
            dx[2 * pair + half] = jnp.concatenate(order(flipped[rows], shift), axis=0)

    own = own_ref[0]
    dqt[...] = jnp.zeros_like(dqt)
    low_tile = low_half(TILE)

    def place(tile):
        return pl.ds(pl.multiple_of(lax.rem(tile - own + tiles, tiles) * TILE, TILE), TILE)

    def some(key_tile, begin, count, key_grad, out_rows):
        rows = place(key_tile)
        columns = [place(begin + step) for step in range(count)]
        masks = [edge_of(key_tile, begin + step) for step in range(count)]
        items = [(head, step) for head in range(heads) for step in range(count)]
        powers, slopes, sums = {}, {}, {}

        def first_products(head, step):
            score = dot(kx[head, rows, :], qx[head, :, columns[step]]) + edges[masks[step]]
            return score, dot(vx[head, rows, :], dx[head, :, columns[step]])

        def last_products(head, step):
            span = slice(head * HEAD_DIM, (head + 1) * HEAD_DIM)
            dqt[span, columns[step]] += dot(kt[span, rows], slopes[head][step])
            if not key_grad or step + 1 < count:
                return
            pair = slice(head // 2 * LANES, (head // 2 + 1) * LANES)
            grads = jnp.concatenate([dn[column, pair] for column in columns], axis=0)
            queries = jnp.concatenate([q_ref[0, column, pair] for column in columns], axis=0)
            sums[head] = (
                dot(jnp.concatenate(slopes.pop(head), axis=1), queries),
                dot(jnp.concatenate(powers.pop(head), axis=1), grads),
            )
            if head % 2 == 1:
                key_sum, value_sum = (jnp.where(low_tile, a, b) for a, b in zip(sums[head - 1], sums[head]))
                cosines, sines = cos_ref[0, out_rows, :], sin_ref[0, out_rows, :]
                out_ref[1, 0, out_rows, pair] = (key_sum * cosines - swapped(key_sum) * sines).astype(BF16)
                out_ref[2, 0, out_rows, pair] = value_sum.astype(BF16)

        ahead = [first_products(*items[0])]
        for index, (head, step) in enumerate(items):
            if index + 1 < len(items):
                ahead.append(first_products(*items[index + 1]))
            score, slope = ahead.pop(0)
            power = jnp.exp(score)
            powers.setdefault(head, []).append(power.astype(BF16))
            slopes.setdefault(head, []).append((power * slope).astype(BF16))
            if index >= 1:
                last_products(*items[index - 1])
        last_products(*items[-1])

    def own_keys(index, carry):
        key_tile = own + index
        first, last = lo_ref[batch, key_tile], hi_ref[batch, key_tile]
        out_rows = pl.ds(pl.multiple_of(index * TILE, TILE), TILE)
        for count in range(1, 2 * REACH + 2):
            pl.when(last - first == count)(functools.partial(some, key_tile, first, count, True, out_rows))
        return carry

    lax.fori_loop(0, mine, own_keys, 0)

    def other_keys(mem, carry):
        ahead = own + mem
        key_tile = jnp.where(ahead < own + mine + REACH, ahead, ahead - tiles)
        if tiles == mine + REACH:
            key_tile = jnp.where(own == 0, ahead, ahead - tiles)
        valid = (key_tile >= 0) & (key_tile < lo_ref.shape[1])
        safe = jnp.where(valid, key_tile, 0)
        begin = jnp.maximum(lo_ref[batch, safe], own)
        end = jnp.where(valid, jnp.minimum(hi_ref[batch, safe], own + mine), begin)
        for count in range(1, min(REACH, mine) + 1):
            pl.when(end - begin == count)(functools.partial(some, safe, begin, count, False, None))
        return carry

    lax.fori_loop(mine, tiles, other_keys, 0)
    for pair in range(wide):
        span = slice(pair * LANES, (pair + 1) * LANES)
        raw = dqt[span, :stretch].T * HEAD_DIM**-0.5
        out_ref[0, 0, :, span] = (raw * cos_ref[0] - swapped(raw) * sin_ref[0]).astype(BF16)


def attend_back(own, lows, highs, qkv, grads, grads_halo, lse, lse_halo, delta, delta_halo, marks_k, marks_q,
                cosines, sines):
    batch, extent, _ = qkv.shape
    stretch, width = grads.shape[1:]
    halo = extent - stretch
    tiles = extent // TILE
    wide = WIDE_BACK
    groups = PAIRS // wide
    spec = lambda rows, offset: pl.BlockSpec((1, rows, wide * LANES), lambda b, p, *_: (b, 0, p + offset))
    per = lambda rows: pl.BlockSpec((1, rows, LANES), lambda b, p, *_: (b, 0, 0))
    numbers = lambda rows: pl.BlockSpec((1, wide, 2, rows), lambda b, p, *_: (b, p, 0, 0))
    return pl.pallas_call(
        functools.partial(attend_back_kernel, tiles, wide),
        grid_spec=pltpu.PrefetchScalarGridSpec(
            num_scalar_prefetch=3,
            grid=(batch, groups),
            in_specs=[
                spec(extent, 0),
                spec(extent, groups),
                spec(extent, 2 * groups),
                spec(stretch, 0),
                spec(halo, 0),
                numbers(stretch),
                numbers(halo),
                numbers(stretch),
                numbers(halo),
                per(extent),
                pl.BlockSpec((1, HEAD_DIM, extent), lambda b, p, *_: (b, 0, 0)),
                per(stretch),
                per(stretch),
            ],
            out_specs=pl.BlockSpec((3, 1, stretch, wide * LANES), lambda b, p, *_: (0, b, 0, p)),
            scratch_shapes=[
                pltpu.VMEM((2 * wide, extent, LANES), BF16),
                pltpu.VMEM((2 * wide, extent, LANES), BF16),
                pltpu.VMEM((2 * wide, LANES, extent), BF16),
                pltpu.VMEM((2 * wide, LANES, extent), BF16),
                pltpu.VMEM((extent, wide * LANES), BF16),
                pltpu.VMEM((wide * LANES, extent), BF16),
                pltpu.VMEM((wide * LANES, extent), F32),
                pltpu.VMEM((3, TILE, TILE), F32),
            ],
        ),
        out_shape=jax.ShapeDtypeStruct((3, batch, stretch, width), BF16),
        compiler_params=params(),
        cost_estimate=pl.CostEstimate(
            flops=5 * 2 * HEADS * batch * stretch * extent * 128, bytes_accessed=64 * 1024 * 1024, transcendentals=0
        ),
        name="attend_back",
    )(own, lows, highs, qkv, qkv, qkv, grads, grads_halo, lse, lse_halo, delta, delta_halo, marks_k, marks_q,
      cosines, sines)


def feed_kernel(seqs, halo_tiles, x_ref, o_ref, g_ref, gain_ref, w_ref, wd_ref,
                out_ref, h2t_ref, hidt_ref, slopes_ref, dr_ref, do_ref, delta_ref, do_halo, delta_halo,
                do_sent, delta_sent, send_sem, recv_sem):
    batch, steps = pl.num_programs(1), pl.num_programs(0)
    step, sequence = pl.program_id(0), pl.program_id(1)
    seq = lax.axis_index("seq")
    mine, tiles = steps, steps + halo_tiles
    reach = -(-REACH // mine)
    hops = [hop for hop in range(-reach, reach + 1) if hop != 0]

    def exists(hop):
        return (seq + hop >= 0) & (seq + hop < seqs)

    def sent(which, tile, hop):
        peer = seq + hop
        place = seq * mine + tile
        wanted = exists(hop) & (place >= peer * mine - REACH) & (place < (peer + 1) * mine + REACH)
        slot = lax.rem(place - peer * mine + tiles, tiles) - mine
        slot = jnp.where(wanted, slot, 0)
        return wanted, halo_copies(which, tile, slot, hops.index(hop), peer)

    def halo_copies(which, tile, slot, hop, peer):
        span = pl.ds(pl.multiple_of(slot * TILE, TILE), TILE)
        pieces = [
            (do_sent.at[which, tile], do_halo.at[which, span]),
            (delta_sent.at[which, tile], delta_halo.at[which, :, :, span]),
        ]
        return [
            pltpu.make_async_remote_copy(
                src_ref=source, dst_ref=target, send_sem=send_sem.at[kind, which, tile, hop],
                recv_sem=recv_sem.at[kind, which, slot], device_id={"seq": peer}, device_id_type=MESH,
            )
            for kind, (source, target) in enumerate(pieces)
        ]

    @pl.when((step == 0) & (sequence == 0))
    def _():
        barrier = pltpu.get_barrier_semaphore()
        for hop in hops:
            @pl.when(exists(hop))
            def _():
                pl.semaphore_signal(barrier, inc=1, device_id={"seq": seq + hop}, device_id_type=MESH)

        for hop in hops:
            @pl.when(exists(hop))
            def _():
                pl.semaphore_wait(barrier, 1)

    mixed = o_ref[0]
    seeds = g_ref[0]
    gain = gain_ref[...]
    width = mixed.shape[1]
    w_out = slice(2 * FF_PAD, 2 * FF_PAD + width)
    r1 = x_ref[0].astype(F32) + dot(mixed, w_ref[:, w_out])
    unit, inverse = normed(r1)
    h2 = (unit * gain).astype(BF16)
    h2t_ref[...] = h2.T
    total = r1
    back = jnp.zeros_like(r1)
    edges = list(range(0, FF - 511, 512))
    for start, stop in zip(edges, edges[1:] + [FF]):
        gates, ups = slice(start, stop), slice(FF_PAD + start, FF_PAD + stop)
        gate = dot(h2, w_ref[:, gates])
        up = dot(h2, w_ref[:, ups])
        grad = dot(seeds, wd_ref[start:stop, :], NT)
        phi = 0.5 + 0.5 * lax.erf(gate * (0.5**0.5))
        bell = jnp.exp(gate * gate * -0.5) * 0.3989422804014327
        act = gate * phi
        hid = (act * up).astype(BF16)
        grad_gate = (grad * up * (phi + gate * bell)).astype(BF16)
        grad_up = (grad * act).astype(BF16)
        hidt_ref[start:stop, :] = hid.T
        slopes_ref[0, :, gates] = grad_gate
        slopes_ref[0, :, ups] = grad_up
        total = total + dot(hid, wd_ref[start:stop, :])
        back = back + dot(grad_gate, w_ref[:, gates], NT) + dot(grad_up, w_ref[:, ups], NT)
    blank = jnp.zeros((TILE, FF_PAD - FF), BF16)
    slopes_ref[0, :, 2 * FF_PAD + width :] = jnp.zeros((TILE, slopes_ref.shape[2] - 2 * FF_PAD - width), BF16)
    slopes_ref[0, :, FF:FF_PAD] = blank
    slopes_ref[0, :, FF_PAD + FF : 2 * FF_PAD] = blank
    out_ref[0] = total.astype(BF16)
    dr = seeds.astype(F32) + norm_back(back * gain, unit, inverse)
    dr_ref[0] = dr
    da = dr.astype(BF16)
    slopes_ref[0, :, w_out] = da
    do = dot(da, w_ref[:, w_out], NT).astype(BF16)
    do_ref[0] = do
    product = do.astype(F32) * mixed.astype(F32)
    high = product.astype(BF16)
    rest = (product - high.astype(F32)).astype(BF16)
    head = lax.broadcasted_iota(jnp.int32, (HEADS, width), 0)
    column = lax.broadcasted_iota(jnp.int32, (HEADS, width), 1)
    pick = jnp.where(column // HEAD_DIM == head, 1.0, 0.0).astype(BF16)
    delta = dot(pick, high, NT) + dot(pick, rest, NT)
    tile = facing_first(step, steps, seqs)
    do_sent[sequence, tile] = do
    for pair in range(PAIRS):
        delta_ref[0, pair] = delta[2 * pair : 2 * pair + 2]
        delta_sent[sequence, tile, pair] = delta[2 * pair : 2 * pair + 2]
    for hop in hops:
        wanted, copies = sent(sequence, tile, hop)

        @pl.when(wanted)
        def _():
            for copy in copies:
                copy.start()

    @pl.when((step == steps - 1) & (sequence == batch - 1))
    def _():
        def settle(index, carry):
            which, tile = index // mine, lax.rem(index, mine)
            for hop in hops:
                wanted, copies = sent(which, tile, hop)

                @pl.when(wanted)
                def _():
                    for copy in copies:
                        copy.wait_send()

            return carry

        lax.fori_loop(0, batch * mine, settle, 0)

        def arrive(index, carry):
            which, slot = index // halo_tiles, lax.rem(index, halo_tiles)
            place = seq * mine + mine + slot
            if halo_tiles == REACH:
                place = jnp.where(seq == 0, place, place - tiles)
            else:
                place = jnp.where(slot < REACH, place, place - tiles)

            @pl.when((place >= 0) & (place < seqs * mine))
            def _():
                for copy in halo_copies(which, 0, slot, 0, seq):
                    copy.wait_recv()

            return carry

        lax.fori_loop(0, batch * halo_tiles, arrive, 0)


def facing_first(step, steps, seqs):
    if seqs != 2:
        return step
    return lax.rem(step + (1 - lax.axis_index("seq")) * (steps // 2), steps)


def feed(x, mixed, seeds, gain, w_rest, w_down, seqs, halo):
    batch, rows, width = x.shape
    steps = rows // TILE
    place = lambda i: facing_first(i, steps, seqs)
    block = lambda n: pl.BlockSpec((1, TILE, n), lambda i, b: (b, place(i), 0))
    turned = lambda n: pl.BlockSpec((n, TILE), lambda i, b: (0, b * steps + place(i)))
    fixed = lambda m, n: pl.BlockSpec((m, n), lambda i, b: (0, 0), pipeline_mode=pl.Buffered(1))
    shape = lambda n, t: jax.ShapeDtypeStruct((batch, rows, n), t)
    columns = w_rest.shape[1]
    padded = -(-columns // CUT) * CUT
    reach = -(-REACH // steps)
    return pl.pallas_call(
        functools.partial(feed_kernel, seqs, halo // TILE),
        grid=(steps, batch),
        in_specs=[
            block(width), block(width), block(width), fixed(1, width), fixed(width, columns), fixed(FF, width),
        ],
        out_specs=[
            block(width), turned(width), turned(FF), block(padded), block(width), block(width),
            pl.BlockSpec((1, PAIRS, 2, TILE), lambda i, b: (b, 0, 0, place(i))),
            pl.BlockSpec(memory_space=pl.ANY),
            pl.BlockSpec(memory_space=pl.ANY),
        ],
        out_shape=[
            shape(width, BF16),
            jax.ShapeDtypeStruct((width, batch * rows), BF16),
            jax.ShapeDtypeStruct((FF, batch * rows), BF16),
            shape(padded, BF16),
            shape(width, F32),
            shape(width, BF16),
            jax.ShapeDtypeStruct((batch, PAIRS, 2, rows), F32),
            jax.ShapeDtypeStruct((batch, halo, width), BF16),
            jax.ShapeDtypeStruct((batch, PAIRS, 2, halo), F32),
        ],
        scratch_shapes=[
            pltpu.VMEM((batch, steps, TILE, width), BF16),
            pltpu.VMEM((batch, steps, PAIRS, 2, TILE), F32),
            pltpu.SemaphoreType.DMA((2, batch, steps, 2 * reach)),
            pltpu.SemaphoreType.DMA((2, batch, halo // TILE)),
        ],
        compiler_params=params(collective_id=2, has_side_effects=True),
        cost_estimate=pl.CostEstimate(
            flops=2 * batch * rows * width * (6 * FF + 2 * width), bytes_accessed=64 * 1024 * 1024, transcendentals=0
        ),
        name="feed",
    )(x, mixed, seeds, gain, w_rest, w_down)


def weigh_kernel(blocks, share, held, turns, *refs):
    lefts, (right_ref, out_ref, prod, kept, sent, got, send_sem, recv_sem) = refs[:-8], refs[-8:]
    step = pl.program_id(0)
    dp = lax.axis_index("dp")
    core = lax.rem(dp, 2)
    mate = dp + 1 - 2 * core
    places = prod.shape[0] // (2 * share)

    def to_mate(n):
        return pltpu.make_async_remote_copy(
            src_ref=sent.at[n], dst_ref=got.at[n], send_sem=send_sem.at[n], recv_sem=recv_sem.at[n],
            device_id={"dp": mate}, device_id_type=MESH,
        )

    @pl.when(step == 0)
    def _():
        barrier = pltpu.get_barrier_semaphore()
        pl.semaphore_signal(barrier, inc=1, device_id={"dp": mate}, device_id_type=MESH)
        pl.semaphore_wait(barrier, 1)

    columns = right_ref.shape[1]
    for first, last, pieces in turns:

        @pl.when((step >= first) & (step < last))
        def _():
            start = 0
            for which, count in pieces:
                span = slice(start, start + count)
                prod[:, span] = dot(lefts[which][...], right_ref[:, span])
                start += count

    @pl.when(step < blocks)
    def _():
        for place in range(places):
            even = prod[2 * place * share : (2 * place + 1) * share, :]
            odd = prod[(2 * place + 1) * share : (2 * place + 2) * share, :]
            rows = slice(place * held, place * held + share)
            sent[step, rows, :] = jnp.where(core == 0, odd, even).astype(BF16)
            kept[step % 2, rows, :] = jnp.where(core == 0, even, odd)
            if held > share:
                rows = slice(place * held + share, (place + 1) * held)
                sent[step, rows, :] = jnp.zeros((held - share, columns), BF16)
                kept[step % 2, rows, :] = jnp.zeros((held - share, columns), F32)
        to_mate(step).start()

    @pl.when(step >= 1)
    def _():
        done = step - 1
        to_mate(done).wait()
        out_ref[...] = (kept[done % 2] + got[done].astype(F32)).astype(BF16)


def weigh(lefts, right, columns, blocks, turns, share, name, number):
    rows, tokens = lefts[0].shape
    total = blocks * columns
    held = -(-share // 16) * 16
    places = rows // (2 * share)
    fixed = pl.BlockSpec((rows, tokens), lambda n: (0, 0), pipeline_mode=pl.Buffered(1))
    return pl.pallas_call(
        functools.partial(weigh_kernel, blocks, share, held, turns),
        grid=(blocks + 1,),
        in_specs=[fixed] * len(lefts) + [pl.BlockSpec((tokens, columns), lambda n: (0, jnp.minimum(n, blocks - 1)))],
        out_specs=pl.BlockSpec((places * held, columns), lambda n: (0, jnp.maximum(n - 1, 0))),
        out_shape=jax.ShapeDtypeStruct((places * held, total), BF16),
        scratch_shapes=[
            pltpu.VMEM((rows, columns), F32),
            pltpu.VMEM((2, places * held, columns), F32),
            pltpu.VMEM((blocks, places * held, columns), BF16),
            pltpu.VMEM((blocks, places * held, columns), BF16),
            pltpu.SemaphoreType.DMA((blocks,)),
            pltpu.SemaphoreType.DMA((blocks,)),
        ],
        compiler_params=params(collective_id=number, has_side_effects=True),
        cost_estimate=pl.CostEstimate(
            flops=2 * rows * tokens * total, bytes_accessed=24 * 1024 * 1024, transcendentals=0
        ),
        name=name,
    )(*lefts, right)


LAGS = (1, 3, 5, 6, 7, 8)
RING, RING_XY, RING_LINE = 5, 2, 4
EARLY, DOWN_BLOCKS, LINE_LAG = 8, 4, 2


def close_kernel(blocks, rest_blocks, rest_edge, seqs, reps, h2t_ref, ot_ref, h1t_ref, rest_ref, right_ref, three_ref, w_ref, x_ref, dr_ref, gain_ref, early_ref, down_ref,
                 gi_ref, rest_sum, sum_ref, early_sum, down_sum,
                 prod, kept0, kept1x, kept1y, kept2, s0, r0, s1x, r1x, s1y, r1y, s2x, r2x, s2y, r2y,
                 mine, ends, others, early_ends, early_others, down_ends, down_others, send_sem, recv_sem, line_sem):
    step = pl.program_id(0)
    width = h1t_ref.shape[0]
    share = mine.shape[1]
    seq, dp, rep = lax.axis_index("seq"), lax.axis_index("dp"), lax.axis_index("rep")
    core, side = lax.rem(dp, 2), dp // 2
    mate, across = dp + 1 - 2 * core, lax.rem(dp + 2, 4)
    seq_peers = [lax.rem(seq + hop, seqs) for hop in range(1, seqs)]
    inner = (rep == 1) | (rep == 2)
    beside = rep + 1 - 2 * lax.rem(rep, 2)
    slot_seq, slot_side, slot_in = 1, seqs, seqs + 1

    def copy(source, target, n, slot, device):
        turn = lax.rem(n, 2 * RING_XY)
        return pltpu.make_async_remote_copy(
            src_ref=source, dst_ref=target, send_sem=send_sem.at[turn, slot], recv_sem=recv_sem.at[turn, slot],
            device_id=device, device_id_type=MESH,
        )

    def rows(first, count):
        return pl.ds(pl.multiple_of(first * share, share), count * share)

    def half(n):
        return lax.rem(n // 2, RING_XY)

    def to_mate(n):
        slot = lax.rem(n, RING)
        return [copy(s0.at[slot], r0.at[slot], n, 0, {"dp": mate})]

    def to_seq(n, source, target):
        return [
            copy(source.at[half(n), hop], target.at[half(n), hop], n, slot_seq + hop, {"seq": peer})
            for hop, peer in enumerate(seq_peers)
        ]

    def to_side(n, source, target):
        return [copy(source.at[half(n)], target.at[half(n)], n, slot_side, {"dp": across})]

    def line(which, source, first, second, sends, arrivals):
        start, target, device = (
            (source, first, beside), (first, second, reps - 1 - rep), (second, second, beside),
        )[which]
        return pltpu.make_async_remote_copy(
            src_ref=start, dst_ref=target, send_sem=sends, recv_sem=arrivals,
            device_id={"rep": device}, device_id_type=MESH,
        )

    def own_line(n, which):
        slot, turn = slot_in + which, lax.rem(n, RING_LINE)
        return line(which, mine.at[turn], ends.at[turn], others.at[turn], send_sem.at[turn, slot], recv_sem.at[turn, slot])

    early_columns, down_columns = early_ends.shape[2], down_ends.shape[2]
    extra = []
    for k in range(down_ends.shape[0]):
        extra.append((down_ref, down_ends, down_others, down_sum, k, slice(k * down_columns, (k + 1) * down_columns)))
    for k in range(early_ends.shape[0]):
        extra.append((early_ref, early_ends, early_others, early_sum, k, slice(k * early_columns, (k + 1) * early_columns)))

    def extra_line(index, which):
        source, first, second, _, k, columns = extra[index]
        return line(
            which, source.at[:, columns], first.at[k], second.at[k],
            line_sem.at[0, index, which], line_sem.at[1, index, which],
        )

    def start(copies):
        for each in copies:
            each.start()

    def wait(copies):
        for each in copies:
            each.wait()

    @pl.when(step == 0)
    def _():
        barrier = pltpu.get_barrier_semaphore()
        partners = [{"dp": mate}, {"dp": across}]
        partners += [{"seq": peer} for peer in seq_peers] + [{"rep": beside}]
        for partner in partners:
            pl.semaphore_signal(barrier, inc=1, device_id=partner, device_id_type=MESH)

        @pl.when(inner)
        def _():
            pl.semaphore_signal(barrier, inc=1, device_id={"rep": reps - 1 - rep}, device_id_type=MESH)
            pl.semaphore_wait(barrier, len(partners) + 1)

        @pl.when(jnp.logical_not(inner))
        def _():
            pl.semaphore_wait(barrier, len(partners))

    for index in range(len(extra)):
        @pl.when((step == index) & jnp.logical_not(inner))
        def _():
            extra_line(index, 0).start()

    whole_blocks, split = rest_edge // CUT, rest_edge % CUT

    @pl.when(step < whole_blocks)
    def _():
        prod[...] = dot(h2t_ref[...], rest_ref[...])

    @pl.when((step >= whole_blocks) & (step < rest_blocks))
    def _():
        if split:
            @pl.when(step == whole_blocks)
            def _():
                prod[:, :split] = dot(h2t_ref[...], rest_ref[:, :split])
                prod[:, split:] = dot(ot_ref[...], rest_ref[:, split:])

        @pl.when(step >= whole_blocks + (split > 0))
        def _():
            prod[...] = dot(ot_ref[...], rest_ref[...])

    @pl.when((step >= rest_blocks) & (step < blocks))
    def _():
        prod[...] = dot(h1t_ref[...], right_ref[0])

    @pl.when(step < blocks)
    def _():
        for place in range(2 * seqs):
            span = slice(place * share, (place + 1) * share)
            s0[lax.rem(step, RING), span, :] = prod[rows(2 * place + 1 - core, 1), :].astype(BF16)
        start(to_mate(step))
        for place in range(2 * seqs):
            span = slice(place * share, (place + 1) * share)
            kept0[step % 2, span, :] = prod[rows(2 * place + core, 1), :]

    @pl.when((step >= blocks) & (step < blocks + gi_steps(three_ref, right_ref)))
    def _():
        back = None
        for part in range(3):
            term = dot(three_ref[part], w_ref[:, part * width : (part + 1) * width], NT)
            back = term if back is None else back + term
        unit, inverse = normed(x_ref[...].astype(F32))
        gi_ref[...] = dr_ref[...] + norm_back(back * gain_ref[...], unit, inverse)

    for index, (source, first, second, total, k, columns) in enumerate(extra):
        meet, share_out, close_out = (index + LINE_LAG * hop for hop in (1, 2, 3))

        @pl.when((step == meet) & inner)
        def _():
            extra_line(index, 0).wait_recv()
            first[k] = (source[:, columns].astype(F32) + first[k].astype(F32)).astype(BF16)
            extra_line(index, 1).start()

        @pl.when((step == share_out) & inner)
        def _():
            extra_line(index, 1).wait()
            second[k] = (first[k].astype(F32) + second[k].astype(F32)).astype(BF16)
            extra_line(index, 2).start()

        @pl.when(step == close_out)
        def _():
            @pl.when(inner)
            def _():
                extra_line(index, 2).wait_send()

            @pl.when(jnp.logical_not(inner))
            def _():
                extra_line(index, 0).wait_send()
                extra_line(index, 2).wait_recv()

            total[:, columns] = second[k]

    n6 = step - LAGS[5]

    @pl.when((n6 >= 0) & (n6 < blocks))
    def _():
        @pl.when(inner)
        def _():
            own_line(n6, 2).wait_send()

        @pl.when(jnp.logical_not(inner))
        def _():
            own_line(n6, 2).wait_recv()

        total = others[lax.rem(n6, RING_LINE)]

        @pl.when(n6 < rest_blocks)
        def _():
            rest_sum[:, pl.ds(pl.multiple_of(n6 * CUT, CUT), CUT)] = total

        @pl.when(n6 >= rest_blocks)
        def _():
            sum_ref[:, pl.ds(pl.multiple_of((n6 - rest_blocks) * CUT, CUT), CUT)] = total

    n5 = step - LAGS[4]

    @pl.when((n5 >= 0) & (n5 < blocks) & inner)
    def _():
        own_line(n5, 1).wait()
        others[lax.rem(n5, RING_LINE)] = (ends[lax.rem(n5, RING_LINE)].astype(F32) + others[lax.rem(n5, RING_LINE)].astype(F32)).astype(BF16)
        own_line(n5, 2).start()

    n4 = step - LAGS[3]

    @pl.when((n4 >= 0) & (n4 < blocks) & inner)
    def _():
        own_line(n4, 0).wait_recv()
        ends[lax.rem(n4, RING_LINE)] = (mine[lax.rem(n4, RING_LINE)].astype(F32) + ends[lax.rem(n4, RING_LINE)].astype(F32)).astype(BF16)
        own_line(n4, 1).start()

    @pl.when((n4 >= 0) & (n4 < blocks) & jnp.logical_not(inner))
    def _():
        own_line(n4, 0).wait_send()

    n3 = step - LAGS[2]

    @pl.when((n3 >= 0) & (n3 < blocks))
    def _():
        total = kept2[n3 % 2]

        @pl.when(n3 % 2 == 0)
        def _():
            wait(to_side(n3, s2y, r2y))
            mine[lax.rem(n3, RING_LINE)] = (total + r2y[half(n3)].astype(F32)).astype(BF16)

        @pl.when(n3 % 2 == 1)
        def _():
            wait(to_seq(n3, s2x, r2x))
            added = total
            for hop in range(seqs - 1):
                added = added + r2x[half(n3), hop].astype(F32)
            mine[lax.rem(n3, RING_LINE)] = added.astype(BF16)

        @pl.when(jnp.logical_not(inner))
        def _():
            own_line(n3, 0).start()

    n2 = step - LAGS[1]

    @pl.when((n2 >= 0) & (n2 < blocks) & (n2 % 2 == 0))
    def _():
        wait(to_seq(n2, s1x, r1x))
        total = kept1x[...]
        for hop in range(seqs - 1):
            total = total + r1x[half(n2), hop].astype(F32)
        kept1x[...] = total
        s2y[half(n2)] = kept1x[rows(1 - side, 1), :].astype(BF16)
        start(to_side(n2, s2y, r2y))
        kept2[0] = kept1x[rows(side, 1), :]

    @pl.when((n2 >= 0) & (n2 < blocks) & (n2 % 2 == 1))
    def _():
        wait(to_side(n2, s1y, r1y))
        kept1y[...] = kept1y[...] + r1y[half(n2)].astype(F32)
        for hop, peer in enumerate(seq_peers):
            s2x[half(n2), hop] = kept1y[rows(peer, 1), :].astype(BF16)
        start(to_seq(n2, s2x, r2x))
        kept2[1] = kept1y[rows(seq, 1), :]

    n1 = step - LAGS[0]

    @pl.when((n1 >= 0) & (n1 < blocks))
    def _():
        wait(to_mate(n1))
        held = n1 % 2
        kept0[held] = kept0[held] + r0[lax.rem(n1, RING)].astype(F32)

        @pl.when(n1 % 2 == 0)
        def _():
            for hop, peer in enumerate(seq_peers):
                s1x[half(n1), hop] = kept0[held, rows(2 * peer, 2), :].astype(BF16)
            start(to_seq(n1, s1x, r1x))
            kept1x[...] = kept0[held, rows(2 * seq, 2), :]

        @pl.when(n1 % 2 == 1)
        def _():
            for place in range(seqs):
                s1y[half(n1), place * share : (place + 1) * share, :] = kept0[held, rows(2 * place + 1 - side, 1), :].astype(BF16)
            start(to_side(n1, s1y, r1y))
            for place in range(seqs):
                kept1y[place * share : (place + 1) * share, :] = kept0[held, rows(2 * place + side, 1), :]


def gi_steps(three_ref, right_ref):
    return right_ref.shape[1] // three_ref.shape[1]


def close(h2t, mixed_t, h1t, rest, rest_edge, slopes, weight, x, dr, gain, early, down, seqs, dps, reps):
    assert (dps, reps) == (4, 4)
    width, tokens = h1t.shape
    share = width // (seqs * dps)
    rest_blocks = rest.shape[1] // CUT - EARLY
    rest_edge = rest_edge - EARLY * CUT
    blocks_of = lambda array, count: (count, array.shape[0], array.shape[1] // count)
    blocks = rest_blocks + 3 * width // CUT
    halves = width // CUT
    token_blocks = tokens // TILE
    steps = max(blocks + token_blocks, blocks + LAGS[5], DOWN_BLOCKS + EARLY + 3 * LINE_LAG)
    late = lambda s: jnp.clip(s - blocks, 0, token_blocks - 1)
    turn_of = lambda s: jnp.clip(s - rest_blocks, 0, blocks - rest_blocks - 1)
    fixed = lambda m, n: pl.BlockSpec((m, n), lambda s: (0, 0), pipeline_mode=pl.Buffered(1))
    row = pl.BlockSpec((TILE, width), lambda s: (late(s), 0))
    half_rows = 2 * seqs * share
    buffers = lambda *shape: [pltpu.VMEM(shape + (CUT,), BF16)] * 2
    slots = seqs + 4
    return pl.pallas_call(
        functools.partial(close_kernel, blocks, rest_blocks, rest_edge, seqs, reps),
        grid=(steps,),
        in_specs=[
            fixed(width, tokens),
            fixed(width, tokens),
            fixed(width, tokens),
            pl.BlockSpec((tokens, CUT), lambda s: (0, EARLY + jnp.minimum(s, rest_blocks - 1))),
            pl.BlockSpec((1, tokens, CUT), lambda s: (turn_of(s) // halves, 0, turn_of(s) % halves)),
            pl.BlockSpec((3, TILE, width), lambda s: (0, late(s), 0)),
            fixed(*weight.shape),
            row,
            row,
            fixed(1, width),
            fixed(*early.shape),
            fixed(*down.shape),
        ],
        out_specs=[
            row, fixed(share, rest_blocks * CUT), fixed(share, 3 * width), fixed(*early.shape), fixed(*down.shape),
        ],
        out_shape=[
            jax.ShapeDtypeStruct((tokens, width), F32),
            jax.ShapeDtypeStruct((share, rest_blocks * CUT), BF16),
            jax.ShapeDtypeStruct((share, 3 * width), BF16),
            jax.ShapeDtypeStruct(early.shape, BF16),
            jax.ShapeDtypeStruct(down.shape, BF16),
        ],
        scratch_shapes=[
            pltpu.VMEM((width, CUT), F32),
            pltpu.VMEM((2, half_rows, CUT), F32),
            pltpu.VMEM((2 * share, CUT), F32),
            pltpu.VMEM((seqs * share, CUT), F32),
            pltpu.VMEM((2, share, CUT), F32),
            *buffers(RING, half_rows),
            *buffers(RING_XY, seqs - 1, 2 * share),
            *buffers(RING_XY, seqs * share),
            *buffers(RING_XY, seqs - 1, share),
            *buffers(RING_XY, share),
            *[pltpu.VMEM((RING_LINE, share, CUT), BF16)] * 3,
            *[pltpu.VMEM(blocks_of(early, EARLY), BF16)] * 2,
            *[pltpu.VMEM(blocks_of(down, DOWN_BLOCKS), BF16)] * 2,
            pltpu.SemaphoreType.DMA((max(2 * RING_XY, RING_LINE), slots)),
            pltpu.SemaphoreType.DMA((max(2 * RING_XY, RING_LINE), slots)),
            pltpu.SemaphoreType.DMA((2, EARLY + DOWN_BLOCKS, 3)),
        ],
        compiler_params=params(collective_id=1, has_side_effects=True),
        cost_estimate=pl.CostEstimate(
            flops=2 * tokens * width * (6 * width + rest.shape[1]), bytes_accessed=48 * 1024 * 1024, transcendentals=0
        ),
        name="close",
    )(h2t, mixed_t, h1t, rest, slopes, slopes, weight, x, dr, gain, early, down)


def neighbours(block, axis, along, after=None):
    count = lax.axis_size(axis)
    rows = block.shape[along]
    if count == 2:
        start = (1 - lax.axis_index(axis)) * (rows - HALF)
        facing = lax.dynamic_slice_in_dim(block, start, HALF, along)
        if after is not None:
            facing, _ = lax.optimization_barrier((facing, after))
        return lax.ppermute(facing, axis, [(0, 1), (1, 0)])
    step = min(rows, HALF)
    head = lax.slice_in_dim(block, 0, step, axis=along)
    tail = lax.slice_in_dim(block, rows - step, rows, axis=along)
    hops = range(1, HALF // step + 1)
    after = [lax.ppermute(head, axis, [(i + hop, i) for i in range(count - hop)]) for hop in hops]
    before = [lax.ppermute(tail, axis, [(i, i + hop) for i in range(count - hop)]) for hop in reversed(hops)]
    return jnp.concatenate(after + before, axis=along)


def survey(labels, stretch, extent, seq_index, seq_count):
    length = labels.shape[1]
    mem = jnp.arange(extent, dtype=jnp.int32)
    own_start = seq_index * stretch
    wraps = stretch + HALF if seq_count > 2 else jnp.where(seq_index == 0, extent, stretch)
    places = own_start + mem - jnp.where(mem >= wraps, extent, 0)
    padded = jnp.pad(labels, ((0, 0), (HALF, HALF)))
    cut = lambda first, size: lax.dynamic_slice_in_dim(padded, first + HALF, size, 1)
    parts = [cut(own_start, stretch)]
    if seq_count == 2:
        parts.append(cut(jnp.where(seq_index == 0, own_start + stretch, own_start - HALF), HALF))
    else:
        parts += [cut(own_start + stretch, HALF), cut(own_start - HALF, HALF)]
    near = jnp.concatenate(parts, axis=1)
    docs = jnp.arange(DOCS, dtype=jnp.int32)
    starts = jnp.sum(labels[:, :, None] < docs, axis=1, dtype=jnp.int32)
    stops = jnp.sum(labels[:, :, None] <= docs, axis=1, dtype=jnp.int32) - 1
    same = near[:, :, None] == docs
    positions = places - jnp.sum(jnp.where(same, starts[:, None, :], 0), axis=-1)
    lane = jnp.arange(LANES, dtype=jnp.int32)
    half_dim = HEAD_DIM // 2
    frequency = THETA ** (-((lane % half_dim).astype(F32) * 2.0 / HEAD_DIM))
    angles = positions.astype(F32)[:, :, None] * frequency
    cosines = jnp.cos(angles)
    sines = jnp.sin(angles) * jnp.where(lane % HEAD_DIM < half_dim, -1.0, 1.0)
    slot = lane % HEAD_DIM
    marks_k = jnp.where(
        slot < DOCS,
        jnp.where(near[:, :, None] == slot, 0.0, MASKED),
        jnp.where((slot >= 8) & (slot < 11), 1.0, 0.0),
    ).astype(BF16)
    kind = jnp.arange(HEAD_DIM, dtype=jnp.int32)[None, :, None]
    marks_q = jnp.where((kind < DOCS) & (near[:, None, :] == kind), 1.0, 0.0).astype(BF16)
    at = jnp.arange(length // TILE, dtype=jnp.int32) * TILE
    first_label, last_label = labels[:, ::TILE], labels[:, TILE - 1 :: TILE]
    pick = lambda table, which: jnp.sum(
        jnp.where(which[:, :, None] == docs, table[:, None, :], 0), axis=-1
    )
    lows = jnp.maximum(pick(starts, first_label), at - HALF) // TILE
    highs = jnp.minimum(pick(stops, last_label), at + TILE - 1 + HALF) // TILE + 1
    own = (own_start // TILE).astype(jnp.int32).reshape(1)
    return own, lows, highs, cosines, sines, marks_k, marks_q


def body(inputs, segments, cotangent, attn_gain, mlp_gain, w_qkv, w_out, w_in, w_down):
    stretch, width = inputs.shape[2:]
    length = segments.shape[2]
    x = inputs.reshape(-1, stretch, width)
    seeds = cotangent.reshape(-1, stretch, width)
    labels = segments.reshape(-1, length)
    batch = x.shape[0]
    group = ("seq", "dp")
    seq_index = lax.axis_index("seq")
    seq_count = lax.axis_size("seq")

    share = attn_gain.shape[0]
    shards = width // share
    gather = lambda shard: lax.all_gather(shard, group, axis=0, tiled=True)
    gain_rows = jnp.pad(jnp.stack([attn_gain, mlp_gain]), ((0, share - 2), (0, LANES - share)))
    qkv_full = gather(jnp.concatenate([w_qkv, gain_rows], axis=1))
    blank = jnp.zeros((share, FF_PAD - FF), BF16)
    x_halo = neighbours(x, "seq", 1, qkv_full)
    rest_full = gather(jnp.concatenate([w_in[:, :FF], blank, w_in[:, FF:], blank, w_out], axis=1))
    down_full = gather(w_down)
    gains = qkv_full[:, 3 * width : 3 * width + share].reshape(shards, share, share).astype(F32)
    gain_one, gain_two = gains[:, 0].reshape(1, width), gains[:, 1].reshape(1, width)

    halo = x_halo.shape[1]
    extent = stretch + halo
    own, lows, highs, cosines, sines, marks_k, marks_q = survey(labels, stretch, extent, seq_index, seq_count)

    h1t, qkv = project(x, qkv_full, cosines, sines, 0, None, extent, shards)
    qkv = project(x_halo, qkv_full, cosines, sines, stretch // TILE, qkv, extent, shards)
    mixed, mixed_t, lse = attend(own, lows, highs, qkv, marks_k, marks_q, stretch)
    lse_halo = neighbours(lse, "seq", 3)
    result, h2t, hidt, slopes, dr, do, delta, do_halo, delta_halo = feed(
        x, mixed, seeds, gain_two, rest_full, down_full, seq_count, halo
    )

    tokens = batch * stretch
    dps = lax.axis_size("dp")
    pairs = [list(range(core, seq_count * dps, 2)) for core in range(2)]
    scatter = lambda part: lax.psum_scatter(part, group, scatter_dimension=0, tiled=True, axis_index_groups=pairs)
    slopes = slopes.reshape(tokens, -1)
    part_down = weigh(
        [hidt], seeds.reshape(tokens, width), TILE, width // TILE, ((0, width // TILE, ((0, TILE),)),),
        w_down.shape[0], "weigh_down", 3,
    )
    shard_down = scatter(part_down)
    slopes, part_down = lax.optimization_barrier((slopes, part_down))
    part_early = weigh([h2t], slopes, CUT, EARLY, ((0, EARLY, ((0, CUT),)),), share, "weigh_early", 4)
    shard_early = scatter(part_early)
    do_halo, part_early = lax.optimization_barrier((do_halo, part_early))
    slopes_qkv = attend_back(
        own, lows, highs, qkv, do, do_halo, lse, lse_halo, delta, delta_halo, marks_k, marks_q, cosines, sines
    )
    grad_x, late_sum, grad_qkv, early_sum, down_sum = close(
        h2t, mixed_t, h1t, slopes, 2 * FF_PAD, slopes_qkv.reshape(3, tokens, width), qkv_full, x.reshape(tokens, width), dr.reshape(tokens, width),
        gain_one, shard_early, shard_down, seq_count, dps, lax.axis_size("rep"),
    )
    grad_qkv = grad_qkv.astype(F32)
    rest_sum = jnp.concatenate([early_sum, late_sum], axis=1).astype(F32)
    grad_in = jnp.concatenate([rest_sum[:, :FF], rest_sum[:, FF_PAD : FF_PAD + FF]], axis=1)
    grad_attn_gain = jnp.sum(grad_qkv * w_qkv.astype(F32), axis=1) / attn_gain.astype(F32)
    grad_mlp_gain = jnp.sum(grad_in * w_in.astype(F32), axis=1) / mlp_gain.astype(F32)
    return (
        result.reshape(cotangent.shape),
        grad_x.reshape(inputs.shape),
        grad_attn_gain,
        grad_mlp_gain,
        grad_qkv,
        rest_sum[:, 2 * FF_PAD : 2 * FF_PAD + width],
        grad_in,
        down_sum[: w_down.shape[0]].astype(F32),
    )


def solution(mesh):
    return jax.shard_map(
        body,
        mesh=mesh,
        in_specs=(
            P(None, ("dp", "rep"), "seq", None),
            P(None, ("dp", "rep"), None),
            P(None, ("dp", "rep"), "seq", None),
            P(("seq", "dp")),
            P(("seq", "dp")),
            P(("seq", "dp"), None),
            P(("seq", "dp"), None),
            P(("seq", "dp"), None),
            P(("seq", "dp"), None),
        ),
        out_specs=(
            P(None, ("dp", "rep"), "seq", None),
            P(None, ("dp", "rep"), "seq", None),
            P(("seq", "dp")),
            P(("seq", "dp")),
            P(("seq", "dp"), None),
            P(("seq", "dp"), None),
            P(("seq", "dp"), None),
            P(("seq", "dp"), None),
        ),
        check_vma=False,
    )
```

```python
import functools

import jax
import jax.numpy as jnp
from jax import lax
from jax.experimental import pallas as pl
from jax.experimental.pallas import tpu as pltpu
from jax.sharding import PartitionSpec as P

HEADS = 16
HEAD_DIM = 64
FF = 2624
HALF = 512
DOCS = 7

EPS = 1e-05
THETA = 10000.0
MASKED = -1e30

TILE = 256
CUT = 512
REACH = HALF // TILE
LANES = 128
FF_PAD = -(-FF // LANES) * LANES
PAIRS = HEADS // 2
WIDE = 4
WIDE_BACK = 2
VMEM = 60 * 1024 * 1024

F32 = jnp.float32
BF16 = jnp.bfloat16

MESH = pl.DeviceIdType.MESH

NN = (((1,), (0,)), ((), ()))
NT = (((1,), (1,)), ((), ()))


def dot(left, right, dims=NN):
    return lax.dot_general(left, right, dims, preferred_element_type=F32)


def params(**more):
    return pltpu.CompilerParams(vmem_limit_bytes=VMEM, **more)


def normed(values):
    centre = values - jnp.mean(values, axis=-1, keepdims=True)
    spread = jnp.mean(centre * centre, axis=-1, keepdims=True)
    inverse = lax.rsqrt(spread + EPS)
    return centre * inverse, inverse


def norm_back(grads, unit, inverse):
    first = jnp.mean(grads, axis=-1, keepdims=True)
    second = jnp.mean(grads * unit, axis=-1, keepdims=True)
    return (grads - first - unit * second) * inverse


def swapped(values):
    lane = lax.broadcasted_iota(jnp.int32, values.shape, 1)
    ahead = pltpu.roll(values, LANES - HEAD_DIM // 2, 1)
    behind = pltpu.roll(values, HEAD_DIM // 2, 1)
    return jnp.where(lane % HEAD_DIM < HEAD_DIM // 2, ahead, behind)


def project_kernel(keep, shards, x_ref, w_ref, cos_ref, sin_ref, *outs):
    qkv_ref = outs[-1]
    width = x_ref.shape[2]
    share = width // shards
    gain = jnp.concatenate(
        [w_ref[share * i : share * i + 1, 3 * width : 3 * width + share] for i in range(shards)], axis=1
    ).astype(F32)
    unit, _ = normed(x_ref[0].astype(F32))
    h1 = (unit * gain).astype(BF16)
    if keep:
        outs[0][...] = h1.T
    cosines, sines = cos_ref[0], sin_ref[0]
    for start in range(0, 3 * width, 512):
        part = dot(h1, w_ref[:, start : start + 512])
        for column in range(0, 512, LANES):
            piece = part[:, column : column + LANES]
            if start < 2 * width:
                piece = piece * cosines + swapped(piece) * sines
            if start < width:
                piece = piece * HEAD_DIM**-0.5
            qkv_ref[0, :, start + column : start + column + LANES] = piece.astype(BF16)


def project(x, weight, cosines, sines, first_tile, held, extent, shards):
    batch, rows, width = x.shape
    steps = rows // TILE
    grid = (batch, steps)
    keep = held is None
    block = lambda b, i: (b, i, 0)
    shifted = lambda b, i: (b, i + first_tile, 0)
    qkv_spec = pl.BlockSpec((1, TILE, 3 * width), shifted)
    qkv_shape = jax.ShapeDtypeStruct((batch, extent, 3 * width), BF16)
    in_specs = [
        pl.BlockSpec((1, TILE, width), block),
        pl.BlockSpec(weight.shape, lambda b, i: (0, 0), pipeline_mode=pl.Buffered(1)),
        pl.BlockSpec((1, TILE, LANES), shifted),
        pl.BlockSpec((1, TILE, LANES), shifted),
    ]
    cost = pl.CostEstimate(
        flops=2 * batch * rows * width * 3 * width,
        bytes_accessed=8 * batch * rows * width + 6 * width * width,
        transcendentals=0,
    )
    if keep:
        return pl.pallas_call(
            functools.partial(project_kernel, True, shards),
            grid=grid,
            in_specs=in_specs,
            out_specs=[pl.BlockSpec((width, TILE), lambda b, i: (0, b * steps + i)), qkv_spec],
            out_shape=[jax.ShapeDtypeStruct((width, batch * rows), BF16), qkv_shape],
            compiler_params=params(),
            cost_estimate=cost,
            name="project_own",
        )(x, weight, cosines, sines)

    def halo_kernel(x_ref, w_ref, cos_ref, sin_ref, held_ref, qkv_ref):
        project_kernel(False, shards, x_ref, w_ref, cos_ref, sin_ref, qkv_ref)

    return pl.pallas_call(
        halo_kernel,
        grid=grid,
        in_specs=in_specs + [pl.BlockSpec(memory_space=pl.ANY)],
        out_specs=qkv_spec,
        out_shape=qkv_shape,
        input_output_aliases={4: 0},
        compiler_params=params(),
        cost_estimate=cost,
        name="project_halo",
    )(x, weight, cosines, sines, held)


def edge_masks():
    key = lax.broadcasted_iota(jnp.int32, (TILE, TILE), 0)
    query = lax.broadcasted_iota(jnp.int32, (TILE, TILE), 1)
    return (
        jnp.where(key >= query, 0.0, MASKED).astype(F32),
        jnp.where(key <= query, 0.0, MASKED).astype(F32),
    )


def edge_of(key_tile, query_tile):
    gap = key_tile - query_tile
    return jnp.where(gap == -REACH, 0, jnp.where(gap == REACH, 2, 1))


def low_half(rows):
    return lax.broadcasted_iota(jnp.int32, (rows, LANES), 1) < HEAD_DIM


def split3(values):
    high = values.astype(BF16).astype(F32)
    rest = values - high
    middle = rest.astype(BF16).astype(F32)
    return high, middle, rest - middle


def attend_kernel(tiles, wide, own_ref, lo_ref, hi_ref, q_ref, k_ref, v_ref, ek_ref, eq_ref, o_ref, ot_ref, lse_ref,
                  kx, qx, vx, edges):
    batch = pl.program_id(0)
    stretch, extent = q_ref.shape[1], k_ref.shape[1]

    @pl.when((batch == 0) & (pl.program_id(1) == 0))
    def _():
        before, after = edge_masks()
        edges[0] = before
        edges[1] = jnp.zeros((TILE, TILE), F32)
        edges[2] = after

    low = low_half(extent)
    marks = ek_ref[0]
    ones = jnp.ones((16, extent), BF16)
    for pair in range(wide):
        span = slice(pair * LANES, (pair + 1) * LANES)
        keys = k_ref[0, :, span]
        kx[2 * pair] = jnp.where(low, keys, marks)
        kx[2 * pair + 1] = jnp.where(low, marks, keys)
        turned = q_ref[0, :, span].T
        qx[2 * pair] = jnp.concatenate([turned[:HEAD_DIM], eq_ref[0]], axis=0)
        qx[2 * pair + 1] = jnp.concatenate([eq_ref[0], turned[HEAD_DIM:]], axis=0)
        flipped = v_ref[0, :, span].T
        vx[2 * pair] = jnp.concatenate([flipped[:HEAD_DIM], ones], axis=0)
        vx[2 * pair + 1] = jnp.concatenate([flipped[HEAD_DIM:], ones], axis=0)
    own = own_ref[0]

    def one_tile(index, carry):
        query_tile = own + index
        first, last = lo_ref[batch, query_tile], hi_ref[batch, query_tile]
        columns = pl.ds(pl.multiple_of(index * TILE, TILE), TILE)

        def some(count):
            places, masks = [], []
            for step in range(count):
                key_tile = first + step
                places.append(pl.multiple_of(lax.rem(key_tile - own + tiles, tiles) * TILE, TILE))
                masks.append(edge_of(key_tile, query_tile))

            def score(head):
                return [
                    dot(kx[head, pl.ds(place, TILE), :], qx[head, :, columns]) + edges[mask]
                    for place, mask in zip(places, masks)
                ]

            heads = 2 * wide
            scores = {head: score(head) for head in range(min(1, heads))}
            mixed, waiting = [], []

            def close_head(head, top, powers):
                sums = dot(
                    jnp.concatenate([vx[head, :, pl.ds(place, TILE)] for place in places], axis=1),
                    jnp.concatenate(powers, axis=0),
                )
                total = sums[HEAD_DIM : HEAD_DIM + 1]
                mixed.append(sums[:HEAD_DIM] * (1.0 / total))
                lse_ref[0, head // 2, head % 2 : head % 2 + 1, columns] = top + jnp.log(total)
                if head % 2 == 1:
                    both = jnp.concatenate(mixed[-2:], axis=0)
                    span = slice(head // 2 * LANES, (head // 2 + 1) * LANES)
                    ot_ref[span, columns] = both.astype(BF16)
                    o_ref[0, columns, span] = both.T.astype(BF16)

            for head in range(heads):
                if head + 1 < heads:
                    scores[head + 1] = score(head + 1)
                parts = scores.pop(head)
                top = parts[0]
                for part in parts[1:]:
                    top = jnp.maximum(top, part)
                top = jnp.max(top, axis=0, keepdims=True)
                powers = [jnp.exp(part - top).astype(BF16) for part in parts]
                waiting.append((head, top, powers))
                if len(waiting) > 1:
                    close_head(*waiting.pop(0))
            for item in waiting:
                close_head(*item)

        for count in range(1, 2 * REACH + 2):
            pl.when(last - first == count)(functools.partial(some, count))
        return carry

    lax.fori_loop(0, stretch // TILE, one_tile, 0)


def attend(own, lows, highs, qkv, marks_k, marks_q, stretch):
    batch, extent, _ = qkv.shape
    tiles = extent // TILE
    width = PAIRS * LANES
    wide = WIDE
    groups = PAIRS // wide
    spec = lambda rows, offset: pl.BlockSpec((1, rows, wide * LANES), lambda b, p, *_: (b, 0, p + offset))
    per = pl.BlockSpec((1, extent, LANES), lambda b, p, *_: (b, 0, 0))
    return pl.pallas_call(
        functools.partial(attend_kernel, tiles, wide),
        grid_spec=pltpu.PrefetchScalarGridSpec(
            num_scalar_prefetch=3,
            grid=(batch, groups),
            in_specs=[
                spec(stretch, 0),
                spec(extent, groups),
                spec(extent, 2 * groups),
                per,
                pl.BlockSpec((1, HEAD_DIM, stretch), lambda b, p, *_: (b, 0, 0)),
            ],
            out_specs=[
                spec(stretch, 0),
                pl.BlockSpec((wide * LANES, stretch), lambda b, p, *_: (p, b)),
                pl.BlockSpec((1, wide, 2, stretch), lambda b, p, *_: (b, p, 0, 0)),
            ],
            scratch_shapes=[
                pltpu.VMEM((2 * wide, extent, LANES), BF16),
                pltpu.VMEM((2 * wide, LANES, stretch), BF16),
                pltpu.VMEM((2 * wide, HEAD_DIM + 16, extent), BF16),
                pltpu.VMEM((3, TILE, TILE), F32),
            ],
        ),
        out_shape=[
            jax.ShapeDtypeStruct((batch, stretch, width), BF16),
            jax.ShapeDtypeStruct((width, batch * stretch), BF16),
            jax.ShapeDtypeStruct((batch, PAIRS, 2, stretch), F32),
        ],
        compiler_params=params(),
        cost_estimate=pl.CostEstimate(
            flops=2 * 2 * HEADS * batch * stretch * extent * 128, bytes_accessed=32 * 1024 * 1024, transcendentals=0
        ),
        name="attend",
    )(own, lows, highs, qkv, qkv, qkv, marks_k, marks_q)


def attend_back_kernel(tiles, wide, first_batch, own_ref, lo_ref, hi_ref, q_ref, k_ref, v_ref, do_ref, doh_ref, lse_ref, lseh_ref,
                       delta_ref, deltah_ref, ek_ref, eq_ref, cos_ref, sin_ref, *refs):
    out_ref, kx, vx, qx, dx, dn, kt, dqt, edges = refs[-9:]
    batch = pl.program_id(0) + first_batch
    extent = k_ref.shape[1]
    stretch = do_ref.shape[1]
    mine = stretch // TILE
    heads = 2 * wide

    @pl.when((pl.program_id(0) == 0) & (pl.program_id(1) == 0))
    def _():
        before, after = edge_masks()
        edges[0] = before
        edges[1] = jnp.zeros((TILE, TILE), F32)
        edges[2] = after

    low = low_half(extent)
    marks = ek_ref[0]
    lane = lax.broadcasted_iota(jnp.int32, (extent, LANES), 1) % HEAD_DIM
    units = jnp.where((lane >= 8) & (lane < 11), 1.0, 0.0).astype(BF16)
    row = lax.broadcasted_iota(jnp.int32, (HEAD_DIM, extent), 0)
    label_rows = eq_ref[0].astype(F32)
    dn[:stretch] = do_ref[0]
    dn[stretch:] = doh_ref[0]
    for pair in range(wide):
        span = slice(pair * LANES, (pair + 1) * LANES)
        keys, values = k_ref[0, :, span], v_ref[0, :, span]
        kx[2 * pair] = jnp.where(low, keys, marks)
        kx[2 * pair + 1] = jnp.where(low, marks, keys)
        kt[span] = keys.T
        vx[2 * pair] = jnp.where(low, values, units)
        vx[2 * pair + 1] = jnp.where(low, units, values)
        turned, flipped = q_ref[0, :, span].T, dn[:, span].T
        lses = jnp.concatenate([lse_ref[0, pair], lseh_ref[0, pair]], axis=1)
        deltas = jnp.concatenate([delta_ref[0, pair], deltah_ref[0, pair]], axis=1)
        for half in range(2):
            lse = split3(lses[half : half + 1])
            delta = split3(deltas[half : half + 1])
            mark, shift = label_rows, jnp.zeros((HEAD_DIM, extent), F32)
            for place in range(3):
                mark = jnp.where(row == 8 + place, -lse[place], mark)
                shift = jnp.where(row == 8 + place, -delta[place], shift)
            mark, shift = mark.astype(BF16), shift.astype(BF16)
            rows = slice(half * HEAD_DIM, (half + 1) * HEAD_DIM)
            order = (lambda a, b: [a, b]) if half == 0 else (lambda a, b: [b, a])
            qx[2 * pair + half] = jnp.concatenate(order(turned[rows], mark), axis=0)
            dx[2 * pair + half] = jnp.concatenate(order(flipped[rows], shift), axis=0)

    own = own_ref[0]
    dqt[...] = jnp.zeros_like(dqt)
    low_tile = low_half(TILE)

    def place(tile):
        return pl.ds(pl.multiple_of(lax.rem(tile - own + tiles, tiles) * TILE, TILE), TILE)

    def some(key_tile, begin, count, key_grad, out_rows):
        rows = place(key_tile)
        columns = [place(begin + step) for step in range(count)]
        masks = [edge_of(key_tile, begin + step) for step in range(count)]
        items = [(head, step) for head in range(heads) for step in range(count)]
        powers, slopes, sums = {}, {}, {}

        def first_products(head, step):
            score = dot(kx[head, rows, :], qx[head, :, columns[step]]) + edges[masks[step]]
            return score, dot(vx[head, rows, :], dx[head, :, columns[step]])

        def last_products(head, step):
            span = slice(head * HEAD_DIM, (head + 1) * HEAD_DIM)
            dqt[span, columns[step]] += dot(kt[span, rows], slopes[head][step])
            if not key_grad or step + 1 < count:
                return
            pair = slice(head // 2 * LANES, (head // 2 + 1) * LANES)
            grads = jnp.concatenate([dn[column, pair] for column in columns], axis=0)
            queries = jnp.concatenate([q_ref[0, column, pair] for column in columns], axis=0)
            sums[head] = (
                dot(jnp.concatenate(slopes.pop(head), axis=1), queries),
                dot(jnp.concatenate(powers.pop(head), axis=1), grads),
            )
            if head % 2 == 1:
                key_sum, value_sum = (jnp.where(low_tile, a, b) for a, b in zip(sums[head - 1], sums[head]))
                cosines, sines = cos_ref[0, out_rows, :], sin_ref[0, out_rows, :]
                out_ref[1, 0, out_rows, pair] = (key_sum * cosines - swapped(key_sum) * sines).astype(BF16)
                out_ref[2, 0, out_rows, pair] = value_sum.astype(BF16)

        ahead = [first_products(*items[0])]
        for index, (head, step) in enumerate(items):
            if index + 1 < len(items):
                ahead.append(first_products(*items[index + 1]))
            score, slope = ahead.pop(0)
            power = jnp.exp(score)
            powers.setdefault(head, []).append(power.astype(BF16))
            slopes.setdefault(head, []).append((power * slope).astype(BF16))
            if index >= 1:
                last_products(*items[index - 1])
        last_products(*items[-1])

    def own_keys(index, carry):
        key_tile = own + index
        first, last = lo_ref[batch, key_tile], hi_ref[batch, key_tile]
        out_rows = pl.ds(pl.multiple_of(index * TILE, TILE), TILE)
        for count in range(1, 2 * REACH + 2):
            pl.when(last - first == count)(functools.partial(some, key_tile, first, count, True, out_rows))
        return carry

    lax.fori_loop(0, mine, own_keys, 0)

    def other_keys(mem, carry):
        ahead = own + mem
        key_tile = jnp.where(ahead < own + mine + REACH, ahead, ahead - tiles)
        if tiles == mine + REACH:
            key_tile = jnp.where(own == 0, ahead, ahead - tiles)
        valid = (key_tile >= 0) & (key_tile < lo_ref.shape[1])
        safe = jnp.where(valid, key_tile, 0)
        begin = jnp.maximum(lo_ref[batch, safe], own)
        end = jnp.where(valid, jnp.minimum(hi_ref[batch, safe], own + mine), begin)
        for count in range(1, min(REACH, mine) + 1):
            pl.when(end - begin == count)(functools.partial(some, safe, begin, count, False, None))
        return carry

    lax.fori_loop(mine, tiles, other_keys, 0)
    for pair in range(wide):
        span = slice(pair * LANES, (pair + 1) * LANES)
        raw = dqt[span, :stretch].T * HEAD_DIM**-0.5
        out_ref[0, 0, :, span] = (raw * cos_ref[0] - swapped(raw) * sin_ref[0]).astype(BF16)


def attend_back(own, lows, highs, qkv, grads, grads_halo, lse, lse_halo, delta, delta_halo, marks_k, marks_q,
                cosines, sines, first_batch, count, held):
    batch, extent, _ = qkv.shape
    stretch, width = grads.shape[1:]
    halo = extent - stretch
    tiles = extent // TILE
    wide = WIDE_BACK
    groups = PAIRS // wide
    spec = lambda rows, offset: pl.BlockSpec((1, rows, wide * LANES), lambda b, p, *_: (b + first_batch, 0, p + offset))
    per = lambda rows: pl.BlockSpec((1, rows, LANES), lambda b, p, *_: (b + first_batch, 0, 0))
    numbers = lambda rows: pl.BlockSpec((1, wide, 2, rows), lambda b, p, *_: (b + first_batch, p, 0, 0))
    return pl.pallas_call(
        functools.partial(attend_back_kernel, tiles, wide, first_batch),
        grid_spec=pltpu.PrefetchScalarGridSpec(
            num_scalar_prefetch=3,
            grid=(count, groups),
            in_specs=[
                spec(extent, 0),
                spec(extent, groups),
                spec(extent, 2 * groups),
                spec(stretch, 0),
                spec(halo, 0),
                numbers(stretch),
                numbers(halo),
                numbers(stretch),
                numbers(halo),
                per(extent),
                pl.BlockSpec((1, HEAD_DIM, extent), lambda b, p, *_: (b + first_batch, 0, 0)),
                per(stretch),
                per(stretch),
            ]
            + ([] if held is None else [pl.BlockSpec(memory_space=pl.ANY)]),
            out_specs=pl.BlockSpec((3, 1, stretch, wide * LANES), lambda b, p, *_: (0, b + first_batch, 0, p)),
            scratch_shapes=[
                pltpu.VMEM((2 * wide, extent, LANES), BF16),
                pltpu.VMEM((2 * wide, extent, LANES), BF16),
                pltpu.VMEM((2 * wide, LANES, extent), BF16),
                pltpu.VMEM((2 * wide, LANES, extent), BF16),
                pltpu.VMEM((extent, wide * LANES), BF16),
                pltpu.VMEM((wide * LANES, extent), BF16),
                pltpu.VMEM((wide * LANES, extent), F32),
                pltpu.VMEM((3, TILE, TILE), F32),
            ],
        ),
        input_output_aliases={} if held is None else {16: 0},
        out_shape=jax.ShapeDtypeStruct((3, batch, stretch, width), BF16),
        compiler_params=params(),
        cost_estimate=pl.CostEstimate(
            flops=5 * 2 * HEADS * count * stretch * extent * 128, bytes_accessed=64 * 1024 * 1024, transcendentals=0
        ),
        name="attend_back",
    )(own, lows, highs, qkv, qkv, qkv, grads, grads_halo, lse, lse_halo, delta, delta_halo, marks_k, marks_q,
      cosines, sines, *([] if held is None else [held]))


def feed_kernel(seqs, halo_tiles, x_ref, o_ref, g_ref, gain_ref, w_ref, wd_ref,
                out_ref, h2t_ref, hidt_ref, slopes_ref, dr_ref, do_ref, delta_ref, do_halo, delta_halo,
                do_sent, delta_sent, send_sem, recv_sem):
    batch, steps = pl.num_programs(1), pl.num_programs(0)
    step, sequence = pl.program_id(0), pl.program_id(1)
    seq = lax.axis_index("seq")
    mine, tiles = steps, steps + halo_tiles
    reach = -(-REACH // mine)
    hops = [hop for hop in range(-reach, reach + 1) if hop != 0]

    def exists(hop):
        return (seq + hop >= 0) & (seq + hop < seqs)

    def sent(which, tile, hop):
        peer = seq + hop
        place = seq * mine + tile
        wanted = exists(hop) & (place >= peer * mine - REACH) & (place < (peer + 1) * mine + REACH)
        slot = lax.rem(place - peer * mine + tiles, tiles) - mine
        slot = jnp.where(wanted, slot, 0)
        return wanted, halo_copies(which, tile, slot, hops.index(hop), peer)

    def halo_copies(which, tile, slot, hop, peer):
        span = pl.ds(pl.multiple_of(slot * TILE, TILE), TILE)
        pieces = [
            (do_sent.at[which, tile], do_halo.at[which, span]),
            (delta_sent.at[which, tile], delta_halo.at[which, :, :, span]),
        ]
        return [
            pltpu.make_async_remote_copy(
                src_ref=source, dst_ref=target, send_sem=send_sem.at[kind, which, tile, hop],
                recv_sem=recv_sem.at[kind, which, slot], device_id={"seq": peer}, device_id_type=MESH,
            )
            for kind, (source, target) in enumerate(pieces)
        ]

    @pl.when((step == 0) & (sequence == 0))
    def _():
        barrier = pltpu.get_barrier_semaphore()
        for hop in hops:
            @pl.when(exists(hop))
            def _():
                pl.semaphore_signal(barrier, inc=1, device_id={"seq": seq + hop}, device_id_type=MESH)

        for hop in hops:
            @pl.when(exists(hop))
            def _():
                pl.semaphore_wait(barrier, 1)

    mixed = o_ref[0]
    seeds = g_ref[0]
    gain = gain_ref[...]
    width = mixed.shape[1]
    w_out = slice(2 * FF_PAD, 2 * FF_PAD + width)
    r1 = x_ref[0].astype(F32) + dot(mixed, w_ref[:, w_out])
    unit, inverse = normed(r1)
    h2 = (unit * gain).astype(BF16)
    h2t_ref[...] = h2.T
    total = r1
    back = jnp.zeros_like(r1)
    edges = list(range(0, FF - 511, 512))
    for start, stop in zip(edges, edges[1:] + [FF]):
        gates, ups = slice(start, stop), slice(FF_PAD + start, FF_PAD + stop)
        gate = dot(h2, w_ref[:, gates])
        up = dot(h2, w_ref[:, ups])
        grad = dot(seeds, wd_ref[start:stop, :], NT)
        phi = 0.5 + 0.5 * lax.erf(gate * (0.5**0.5))
        bell = jnp.exp(gate * gate * -0.5) * 0.3989422804014327
        act = gate * phi
        hid = (act * up).astype(BF16)
        grad_gate = (grad * up * (phi + gate * bell)).astype(BF16)
        grad_up = (grad * act).astype(BF16)
        hidt_ref[start:stop, :] = hid.T
        slopes_ref[0, :, gates] = grad_gate
        slopes_ref[0, :, ups] = grad_up
        total = total + dot(hid, wd_ref[start:stop, :])
        back = back + dot(grad_gate, w_ref[:, gates], NT) + dot(grad_up, w_ref[:, ups], NT)
    blank = jnp.zeros((TILE, FF_PAD - FF), BF16)
    slopes_ref[0, :, 2 * FF_PAD + width :] = jnp.zeros((TILE, slopes_ref.shape[2] - 2 * FF_PAD - width), BF16)
    slopes_ref[0, :, FF:FF_PAD] = blank
    slopes_ref[0, :, FF_PAD + FF : 2 * FF_PAD] = blank
    out_ref[0] = total.astype(BF16)
    dr = seeds.astype(F32) + norm_back(back * gain, unit, inverse)
    dr_ref[0] = dr
    da = dr.astype(BF16)
    slopes_ref[0, :, w_out] = da
    do = dot(da, w_ref[:, w_out], NT).astype(BF16)
    do_ref[0] = do
    product = do.astype(F32) * mixed.astype(F32)
    high = product.astype(BF16)
    rest = (product - high.astype(F32)).astype(BF16)
    head = lax.broadcasted_iota(jnp.int32, (HEADS, width), 0)
    column = lax.broadcasted_iota(jnp.int32, (HEADS, width), 1)
    pick = jnp.where(column // HEAD_DIM == head, 1.0, 0.0).astype(BF16)
    delta = dot(pick, high, NT) + dot(pick, rest, NT)
    tile = facing_first(step, steps, seqs)
    do_sent[sequence, tile] = do
    for pair in range(PAIRS):
        delta_ref[0, pair] = delta[2 * pair : 2 * pair + 2]
        delta_sent[sequence, tile, pair] = delta[2 * pair : 2 * pair + 2]
    for hop in hops:
        wanted, copies = sent(sequence, tile, hop)

        @pl.when(wanted)
        def _():
            for copy in copies:
                copy.start()

    @pl.when((step == steps - 1) & (sequence == batch - 1))
    def _():
        def settle(index, carry):
            which, tile = index // mine, lax.rem(index, mine)
            for hop in hops:
                wanted, copies = sent(which, tile, hop)

                @pl.when(wanted)
                def _():
                    for copy in copies:
                        copy.wait_send()

            return carry

        lax.fori_loop(0, batch * mine, settle, 0)

        def arrive(index, carry):
            which, slot = index // halo_tiles, lax.rem(index, halo_tiles)
            place = seq * mine + mine + slot
            if halo_tiles == REACH:
                place = jnp.where(seq == 0, place, place - tiles)
            else:
                place = jnp.where(slot < REACH, place, place - tiles)

            @pl.when((place >= 0) & (place < seqs * mine))
            def _():
                for copy in halo_copies(which, 0, slot, 0, seq):
                    copy.wait_recv()

            return carry

        lax.fori_loop(0, batch * halo_tiles, arrive, 0)


def facing_first(step, steps, seqs):
    if seqs != 2:
        return step
    return lax.rem(step + (1 - lax.axis_index("seq")) * (steps // 2), steps)


def feed(x, mixed, seeds, gain, w_rest, w_down, seqs, halo):
    batch, rows, width = x.shape
    steps = rows // TILE
    place = lambda i: facing_first(i, steps, seqs)
    block = lambda n: pl.BlockSpec((1, TILE, n), lambda i, b: (b, place(i), 0))
    turned = lambda n: pl.BlockSpec((n, TILE), lambda i, b: (0, b * steps + place(i)))
    fixed = lambda m, n: pl.BlockSpec((m, n), lambda i, b: (0, 0), pipeline_mode=pl.Buffered(1))
    shape = lambda n, t: jax.ShapeDtypeStruct((batch, rows, n), t)
    columns = w_rest.shape[1]
    padded = -(-columns // CUT) * CUT
    reach = -(-REACH // steps)
    return pl.pallas_call(
        functools.partial(feed_kernel, seqs, halo // TILE),
        grid=(steps, batch),
        in_specs=[
            block(width), block(width), block(width), fixed(1, width), fixed(width, columns), fixed(FF, width),
        ],
        out_specs=[
            block(width), turned(width), turned(FF), block(padded), block(width), block(width),
            pl.BlockSpec((1, PAIRS, 2, TILE), lambda i, b: (b, 0, 0, place(i))),
            pl.BlockSpec(memory_space=pl.ANY),
            pl.BlockSpec(memory_space=pl.ANY),
        ],
        out_shape=[
            shape(width, BF16),
            jax.ShapeDtypeStruct((width, batch * rows), BF16),
            jax.ShapeDtypeStruct((FF, batch * rows), BF16),
            shape(padded, BF16),
            shape(width, F32),
            shape(width, BF16),
            jax.ShapeDtypeStruct((batch, PAIRS, 2, rows), F32),
            jax.ShapeDtypeStruct((batch, halo, width), BF16),
            jax.ShapeDtypeStruct((batch, PAIRS, 2, halo), F32),
        ],
        scratch_shapes=[
            pltpu.VMEM((batch, steps, TILE, width), BF16),
            pltpu.VMEM((batch, steps, PAIRS, 2, TILE), F32),
            pltpu.SemaphoreType.DMA((2, batch, steps, 2 * reach)),
            pltpu.SemaphoreType.DMA((2, batch, halo // TILE)),
        ],
        compiler_params=params(collective_id=2, has_side_effects=True),
        cost_estimate=pl.CostEstimate(
            flops=2 * batch * rows * width * (6 * FF + 2 * width), bytes_accessed=64 * 1024 * 1024, transcendentals=0
        ),
        name="feed",
    )(x, mixed, seeds, gain, w_rest, w_down)


def weigh_kernel(blocks, share, held, turns, *refs):
    lefts, (right_ref, out_ref, prod, kept, sent, got, send_sem, recv_sem) = refs[:-8], refs[-8:]
    step = pl.program_id(0)
    dp = lax.axis_index("dp")
    core = lax.rem(dp, 2)
    mate = dp + 1 - 2 * core
    places = prod.shape[0] // (2 * share)

    def to_mate(n):
        return pltpu.make_async_remote_copy(
            src_ref=sent.at[n], dst_ref=got.at[n], send_sem=send_sem.at[n], recv_sem=recv_sem.at[n],
            device_id={"dp": mate}, device_id_type=MESH,
        )

    @pl.when(step == 0)
    def _():
        barrier = pltpu.get_barrier_semaphore()
        pl.semaphore_signal(barrier, inc=1, device_id={"dp": mate}, device_id_type=MESH)
        pl.semaphore_wait(barrier, 1)

    columns = right_ref.shape[1]
    for first, last, pieces in turns:

        @pl.when((step >= first) & (step < last))
        def _():
            start = 0
            for which, count in pieces:
                span = slice(start, start + count)
                prod[:, span] = dot(lefts[which][...], right_ref[:, span])
                start += count

    @pl.when(step < blocks)
    def _():
        for place in range(places):
            even = prod[2 * place * share : (2 * place + 1) * share, :]
            odd = prod[(2 * place + 1) * share : (2 * place + 2) * share, :]
            rows = slice(place * held, place * held + share)
            sent[step, rows, :] = jnp.where(core == 0, odd, even).astype(BF16)
            kept[step % 2, rows, :] = jnp.where(core == 0, even, odd)
            if held > share:
                rows = slice(place * held + share, (place + 1) * held)
                sent[step, rows, :] = jnp.zeros((held - share, columns), BF16)
                kept[step % 2, rows, :] = jnp.zeros((held - share, columns), F32)
        to_mate(step).start()

    @pl.when(step >= 1)
    def _():
        done = step - 1
        to_mate(done).wait()
        out_ref[...] = (kept[done % 2] + got[done].astype(F32)).astype(BF16)


def weigh(lefts, right, columns, blocks, turns, share, name, number):
    rows, tokens = lefts[0].shape
    total = blocks * columns
    held = -(-share // 16) * 16
    places = rows // (2 * share)
    fixed = pl.BlockSpec((rows, tokens), lambda n: (0, 0), pipeline_mode=pl.Buffered(1))
    return pl.pallas_call(
        functools.partial(weigh_kernel, blocks, share, held, turns),
        grid=(blocks + 1,),
        in_specs=[fixed] * len(lefts) + [pl.BlockSpec((tokens, columns), lambda n: (0, jnp.minimum(n, blocks - 1)))],
        out_specs=pl.BlockSpec((places * held, columns), lambda n: (0, jnp.maximum(n - 1, 0))),
        out_shape=jax.ShapeDtypeStruct((places * held, total), BF16),
        scratch_shapes=[
            pltpu.VMEM((rows, columns), F32),
            pltpu.VMEM((2, places * held, columns), F32),
            pltpu.VMEM((blocks, places * held, columns), BF16),
            pltpu.VMEM((blocks, places * held, columns), BF16),
            pltpu.SemaphoreType.DMA((blocks,)),
            pltpu.SemaphoreType.DMA((blocks,)),
        ],
        compiler_params=params(collective_id=number, has_side_effects=True),
        cost_estimate=pl.CostEstimate(
            flops=2 * rows * tokens * total, bytes_accessed=24 * 1024 * 1024, transcendentals=0
        ),
        name=name,
    )(*lefts, right)


LAGS = (1, 3, 5, 6, 7, 8)
RING, RING_XY, RING_LINE = 5, 2, 4
EARLY = 8


def close_kernel(blocks, rest_blocks, rest_edge, seqs, reps, h2t_ref, ot_ref, h1t_ref, rest_ref, right_ref, three_ref, w_ref, x_ref, dr_ref, gain_ref, gi_ref, rest_sum, sum_ref,
                 prod, kept0, kept1x, kept1y, kept2, s0, r0, s1x, r1x, s1y, r1y, s2x, r2x, s2y, r2y,
                 mine, ends, others, send_sem, recv_sem):
    step = pl.program_id(0)
    width = h1t_ref.shape[0]
    share = mine.shape[1]
    seq, dp, rep = lax.axis_index("seq"), lax.axis_index("dp"), lax.axis_index("rep")
    core, side = lax.rem(dp, 2), dp // 2
    mate, across = dp + 1 - 2 * core, lax.rem(dp + 2, 4)
    seq_peers = [lax.rem(seq + hop, seqs) for hop in range(1, seqs)]
    inner = (rep == 1) | (rep == 2)
    beside = rep + 1 - 2 * lax.rem(rep, 2)
    slot_seq, slot_side, slot_in = 1, seqs, seqs + 1

    def copy(source, target, n, slot, device):
        turn = lax.rem(n, 2 * RING_XY)
        return pltpu.make_async_remote_copy(
            src_ref=source, dst_ref=target, send_sem=send_sem.at[turn, slot], recv_sem=recv_sem.at[turn, slot],
            device_id=device, device_id_type=MESH,
        )

    def rows(first, count):
        return pl.ds(pl.multiple_of(first * share, share), count * share)

    def half(n):
        return lax.rem(n // 2, RING_XY)

    def to_mate(n):
        slot = lax.rem(n, RING)
        return [copy(s0.at[slot], r0.at[slot], n, 0, {"dp": mate})]

    def to_seq(n, source, target):
        return [
            copy(source.at[half(n), hop], target.at[half(n), hop], n, slot_seq + hop, {"seq": peer})
            for hop, peer in enumerate(seq_peers)
        ]

    def to_side(n, source, target):
        return [copy(source.at[half(n)], target.at[half(n)], n, slot_side, {"dp": across})]

    def line(which, source, first, second, sends, arrivals):
        start, target, device = (
            (source, first, beside), (first, second, reps - 1 - rep), (second, second, beside),
        )[which]
        return pltpu.make_async_remote_copy(
            src_ref=start, dst_ref=target, send_sem=sends, recv_sem=arrivals,
            device_id={"rep": device}, device_id_type=MESH,
        )

    def own_line(n, which):
        slot, turn = slot_in + which, lax.rem(n, RING_LINE)
        return line(which, mine.at[turn], ends.at[turn], others.at[turn], send_sem.at[turn, slot], recv_sem.at[turn, slot])

    def start(copies):
        for each in copies:
            each.start()

    def wait(copies):
        for each in copies:
            each.wait()

    @pl.when(step == 0)
    def _():
        barrier = pltpu.get_barrier_semaphore()
        partners = [{"dp": mate}, {"dp": across}]
        partners += [{"seq": peer} for peer in seq_peers] + [{"rep": beside}]
        for partner in partners:
            pl.semaphore_signal(barrier, inc=1, device_id=partner, device_id_type=MESH)

        @pl.when(inner)
        def _():
            pl.semaphore_signal(barrier, inc=1, device_id={"rep": reps - 1 - rep}, device_id_type=MESH)
            pl.semaphore_wait(barrier, len(partners) + 1)

        @pl.when(jnp.logical_not(inner))
        def _():
            pl.semaphore_wait(barrier, len(partners))

    whole_blocks, split = rest_edge // CUT, rest_edge % CUT

    @pl.when(step < whole_blocks)
    def _():
        prod[...] = dot(h2t_ref[...], rest_ref[...])

    @pl.when((step >= whole_blocks) & (step < rest_blocks))
    def _():
        if split:
            @pl.when(step == whole_blocks)
            def _():
                prod[:, :split] = dot(h2t_ref[...], rest_ref[:, :split])
                prod[:, split:] = dot(ot_ref[...], rest_ref[:, split:])

        @pl.when(step >= whole_blocks + (split > 0))
        def _():
            prod[...] = dot(ot_ref[...], rest_ref[...])

    @pl.when((step >= rest_blocks) & (step < blocks))
    def _():
        prod[...] = dot(h1t_ref[...], right_ref[0])

    @pl.when(step < blocks)
    def _():
        for place in range(2 * seqs):
            span = slice(place * share, (place + 1) * share)
            s0[lax.rem(step, RING), span, :] = prod[rows(2 * place + 1 - core, 1), :].astype(BF16)
        start(to_mate(step))
        for place in range(2 * seqs):
            span = slice(place * share, (place + 1) * share)
            kept0[step % 2, span, :] = prod[rows(2 * place + core, 1), :]

    @pl.when((step >= blocks) & (step < blocks + gi_steps(three_ref, right_ref)))
    def _():
        back = None
        for part in range(3):
            term = dot(three_ref[part], w_ref[:, part * width : (part + 1) * width], NT)
            back = term if back is None else back + term
        unit, inverse = normed(x_ref[...].astype(F32))
        gi_ref[...] = dr_ref[...] + norm_back(back * gain_ref[...], unit, inverse)

    n6 = step - LAGS[5]

    @pl.when((n6 >= 0) & (n6 < blocks))
    def _():
        @pl.when(inner)
        def _():
            own_line(n6, 2).wait_send()

        @pl.when(jnp.logical_not(inner))
        def _():
            own_line(n6, 2).wait_recv()

        total = others[lax.rem(n6, RING_LINE)]

        @pl.when(n6 < rest_blocks)
        def _():
            rest_sum[:, pl.ds(pl.multiple_of(n6 * CUT, CUT), CUT)] = total

        @pl.when(n6 >= rest_blocks)
        def _():
            sum_ref[:, pl.ds(pl.multiple_of((n6 - rest_blocks) * CUT, CUT), CUT)] = total

    n5 = step - LAGS[4]

    @pl.when((n5 >= 0) & (n5 < blocks) & inner)
    def _():
        own_line(n5, 1).wait()
        others[lax.rem(n5, RING_LINE)] = (ends[lax.rem(n5, RING_LINE)].astype(F32) + others[lax.rem(n5, RING_LINE)].astype(F32)).astype(BF16)
        own_line(n5, 2).start()

    n4 = step - LAGS[3]

    @pl.when((n4 >= 0) & (n4 < blocks) & inner)
    def _():
        own_line(n4, 0).wait_recv()
        ends[lax.rem(n4, RING_LINE)] = (mine[lax.rem(n4, RING_LINE)].astype(F32) + ends[lax.rem(n4, RING_LINE)].astype(F32)).astype(BF16)
        own_line(n4, 1).start()

    @pl.when((n4 >= 0) & (n4 < blocks) & jnp.logical_not(inner))
    def _():
        own_line(n4, 0).wait_send()

    n3 = step - LAGS[2]

    @pl.when((n3 >= 0) & (n3 < blocks))
    def _():
        total = kept2[n3 % 2]

        @pl.when(n3 % 2 == 0)
        def _():
            wait(to_side(n3, s2y, r2y))
            mine[lax.rem(n3, RING_LINE)] = (total + r2y[half(n3)].astype(F32)).astype(BF16)

        @pl.when(n3 % 2 == 1)
        def _():
            wait(to_seq(n3, s2x, r2x))
            added = total
            for hop in range(seqs - 1):
                added = added + r2x[half(n3), hop].astype(F32)
            mine[lax.rem(n3, RING_LINE)] = added.astype(BF16)

        @pl.when(jnp.logical_not(inner))
        def _():
            own_line(n3, 0).start()

    n2 = step - LAGS[1]

    @pl.when((n2 >= 0) & (n2 < blocks) & (n2 % 2 == 0))
    def _():
        wait(to_seq(n2, s1x, r1x))
        total = kept1x[...]
        for hop in range(seqs - 1):
            total = total + r1x[half(n2), hop].astype(F32)
        kept1x[...] = total
        s2y[half(n2)] = kept1x[rows(1 - side, 1), :].astype(BF16)
        start(to_side(n2, s2y, r2y))
        kept2[0] = kept1x[rows(side, 1), :]

    @pl.when((n2 >= 0) & (n2 < blocks) & (n2 % 2 == 1))
    def _():
        wait(to_side(n2, s1y, r1y))
        kept1y[...] = kept1y[...] + r1y[half(n2)].astype(F32)
        for hop, peer in enumerate(seq_peers):
            s2x[half(n2), hop] = kept1y[rows(peer, 1), :].astype(BF16)
        start(to_seq(n2, s2x, r2x))
        kept2[1] = kept1y[rows(seq, 1), :]

    n1 = step - LAGS[0]

    @pl.when((n1 >= 0) & (n1 < blocks))
    def _():
        wait(to_mate(n1))
        held = n1 % 2
        kept0[held] = kept0[held] + r0[lax.rem(n1, RING)].astype(F32)

        @pl.when(n1 % 2 == 0)
        def _():
            for hop, peer in enumerate(seq_peers):
                s1x[half(n1), hop] = kept0[held, rows(2 * peer, 2), :].astype(BF16)
            start(to_seq(n1, s1x, r1x))
            kept1x[...] = kept0[held, rows(2 * seq, 2), :]

        @pl.when(n1 % 2 == 1)
        def _():
            for place in range(seqs):
                s1y[half(n1), place * share : (place + 1) * share, :] = kept0[held, rows(2 * place + 1 - side, 1), :].astype(BF16)
            start(to_side(n1, s1y, r1y))
            for place in range(seqs):
                kept1y[place * share : (place + 1) * share, :] = kept0[held, rows(2 * place + side, 1), :]


def gi_steps(three_ref, right_ref):
    return right_ref.shape[1] // three_ref.shape[1]


def close(h2t, mixed_t, h1t, rest, rest_edge, slopes, weight, x, dr, gain, seqs, dps, reps):
    assert (dps, reps) == (4, 4)
    width, tokens = h1t.shape
    share = width // (seqs * dps)
    rest_blocks = rest.shape[1] // CUT - EARLY
    rest_edge = rest_edge - EARLY * CUT
    blocks = rest_blocks + 3 * width // CUT
    halves = width // CUT
    token_blocks = tokens // TILE
    steps = max(blocks + token_blocks, blocks + LAGS[5])
    late = lambda s: jnp.clip(s - blocks, 0, token_blocks - 1)
    turn_of = lambda s: jnp.clip(s - rest_blocks, 0, blocks - rest_blocks - 1)
    fixed = lambda m, n: pl.BlockSpec((m, n), lambda s: (0, 0), pipeline_mode=pl.Buffered(1))
    row = pl.BlockSpec((TILE, width), lambda s: (late(s), 0))
    half_rows = 2 * seqs * share
    buffers = lambda *shape: [pltpu.VMEM(shape + (CUT,), BF16)] * 2
    slots = seqs + 4
    return pl.pallas_call(
        functools.partial(close_kernel, blocks, rest_blocks, rest_edge, seqs, reps),
        grid=(steps,),
        in_specs=[
            fixed(width, tokens),
            fixed(width, tokens),
            fixed(width, tokens),
            pl.BlockSpec((tokens, CUT), lambda s: (0, EARLY + jnp.minimum(s, rest_blocks - 1))),
            pl.BlockSpec((1, tokens, CUT), lambda s: (turn_of(s) // halves, 0, turn_of(s) % halves)),
            pl.BlockSpec((3, TILE, width), lambda s: (0, late(s), 0)),
            fixed(*weight.shape),
            row,
            row,
            fixed(1, width),
        ],
        out_specs=[row, fixed(share, rest_blocks * CUT), fixed(share, 3 * width)],
        out_shape=[
            jax.ShapeDtypeStruct((tokens, width), F32),
            jax.ShapeDtypeStruct((share, rest_blocks * CUT), BF16),
            jax.ShapeDtypeStruct((share, 3 * width), BF16),
        ],
        scratch_shapes=[
            pltpu.VMEM((width, CUT), F32),
            pltpu.VMEM((2, half_rows, CUT), F32),
            pltpu.VMEM((2 * share, CUT), F32),
            pltpu.VMEM((seqs * share, CUT), F32),
            pltpu.VMEM((2, share, CUT), F32),
            *buffers(RING, half_rows),
            *buffers(RING_XY, seqs - 1, 2 * share),
            *buffers(RING_XY, seqs * share),
            *buffers(RING_XY, seqs - 1, share),
            *buffers(RING_XY, share),
            *[pltpu.VMEM((RING_LINE, share, CUT), BF16)] * 3,
            pltpu.SemaphoreType.DMA((max(2 * RING_XY, RING_LINE), slots)),
            pltpu.SemaphoreType.DMA((max(2 * RING_XY, RING_LINE), slots)),
        ],
        compiler_params=params(collective_id=1, has_side_effects=True),
        cost_estimate=pl.CostEstimate(
            flops=2 * tokens * width * (6 * width + rest.shape[1]), bytes_accessed=48 * 1024 * 1024, transcendentals=0
        ),
        name="close",
    )(h2t, mixed_t, h1t, rest, slopes, slopes, weight, x, dr, gain)


def neighbours(block, axis, along, after=None):
    count = lax.axis_size(axis)
    rows = block.shape[along]
    if count == 2:
        start = (1 - lax.axis_index(axis)) * (rows - HALF)
        facing = lax.dynamic_slice_in_dim(block, start, HALF, along)
        if after is not None:
            facing, _ = lax.optimization_barrier((facing, after))
        return lax.ppermute(facing, axis, [(0, 1), (1, 0)])
    step = min(rows, HALF)
    head = lax.slice_in_dim(block, 0, step, axis=along)
    tail = lax.slice_in_dim(block, rows - step, rows, axis=along)
    hops = range(1, HALF // step + 1)
    after = [lax.ppermute(head, axis, [(i + hop, i) for i in range(count - hop)]) for hop in hops]
    before = [lax.ppermute(tail, axis, [(i, i + hop) for i in range(count - hop)]) for hop in reversed(hops)]
    return jnp.concatenate(after + before, axis=along)


def survey(labels, stretch, extent, seq_index, seq_count):
    length = labels.shape[1]
    mem = jnp.arange(extent, dtype=jnp.int32)
    own_start = seq_index * stretch
    wraps = stretch + HALF if seq_count > 2 else jnp.where(seq_index == 0, extent, stretch)
    places = own_start + mem - jnp.where(mem >= wraps, extent, 0)
    padded = jnp.pad(labels, ((0, 0), (HALF, HALF)))
    cut = lambda first, size: lax.dynamic_slice_in_dim(padded, first + HALF, size, 1)
    parts = [cut(own_start, stretch)]
    if seq_count == 2:
        parts.append(cut(jnp.where(seq_index == 0, own_start + stretch, own_start - HALF), HALF))
    else:
        parts += [cut(own_start + stretch, HALF), cut(own_start - HALF, HALF)]
    near = jnp.concatenate(parts, axis=1)
    docs = jnp.arange(DOCS, dtype=jnp.int32)
    starts = jnp.sum(labels[:, :, None] < docs, axis=1, dtype=jnp.int32)
    stops = jnp.sum(labels[:, :, None] <= docs, axis=1, dtype=jnp.int32) - 1
    same = near[:, :, None] == docs
    positions = places - jnp.sum(jnp.where(same, starts[:, None, :], 0), axis=-1)
    lane = jnp.arange(LANES, dtype=jnp.int32)
    half_dim = HEAD_DIM // 2
    frequency = THETA ** (-((lane % half_dim).astype(F32) * 2.0 / HEAD_DIM))
    angles = positions.astype(F32)[:, :, None] * frequency
    cosines = jnp.cos(angles)
    sines = jnp.sin(angles) * jnp.where(lane % HEAD_DIM < half_dim, -1.0, 1.0)
    slot = lane % HEAD_DIM
    marks_k = jnp.where(
        slot < DOCS,
        jnp.where(near[:, :, None] == slot, 0.0, MASKED),
        jnp.where((slot >= 8) & (slot < 11), 1.0, 0.0),
    ).astype(BF16)
    kind = jnp.arange(HEAD_DIM, dtype=jnp.int32)[None, :, None]
    marks_q = jnp.where((kind < DOCS) & (near[:, None, :] == kind), 1.0, 0.0).astype(BF16)
    at = jnp.arange(length // TILE, dtype=jnp.int32) * TILE
    first_label, last_label = labels[:, ::TILE], labels[:, TILE - 1 :: TILE]
    pick = lambda table, which: jnp.sum(
        jnp.where(which[:, :, None] == docs, table[:, None, :], 0), axis=-1
    )
    lows = jnp.maximum(pick(starts, first_label), at - HALF) // TILE
    highs = jnp.minimum(pick(stops, last_label), at + TILE - 1 + HALF) // TILE + 1
    own = (own_start // TILE).astype(jnp.int32).reshape(1)
    return own, lows, highs, cosines, sines, marks_k, marks_q


def body(inputs, segments, cotangent, attn_gain, mlp_gain, w_qkv, w_out, w_in, w_down):
    stretch, width = inputs.shape[2:]
    length = segments.shape[2]
    x = inputs.reshape(-1, stretch, width)
    seeds = cotangent.reshape(-1, stretch, width)
    labels = segments.reshape(-1, length)
    batch = x.shape[0]
    group = ("seq", "dp")
    seq_index = lax.axis_index("seq")
    seq_count = lax.axis_size("seq")

    share = attn_gain.shape[0]
    shards = width // share
    gather = lambda shard: lax.all_gather(shard, group, axis=0, tiled=True)
    gain_rows = jnp.pad(jnp.stack([attn_gain, mlp_gain]), ((0, share - 2), (0, LANES - share)))
    qkv_full = gather(jnp.concatenate([w_qkv, gain_rows], axis=1))
    blank = jnp.zeros((share, FF_PAD - FF), BF16)
    halo = HALF * (1 if seq_count == 2 else 2)
    extent = stretch + halo
    own, lows, highs, cosines, sines, marks_k, marks_q = survey(labels, stretch, extent, seq_index, seq_count)
    x_halo = neighbours(x, "seq", 1, (qkv_full, cosines, sines, marks_k))
    rest_full = gather(jnp.concatenate([w_in[:, :FF], blank, w_in[:, FF:], blank, w_out], axis=1))
    down_full = gather(w_down)
    gains = qkv_full[:, 3 * width : 3 * width + share].reshape(shards, share, share).astype(F32)
    gain_one, gain_two = gains[:, 0].reshape(1, width), gains[:, 1].reshape(1, width)

    h1t, qkv = project(x, qkv_full, cosines, sines, 0, None, extent, shards)
    qkv = project(x_halo, qkv_full, cosines, sines, stretch // TILE, qkv, extent, shards)
    mixed, mixed_t, lse = attend(own, lows, highs, qkv, marks_k, marks_q, stretch)
    lse_halo = neighbours(lse, "seq", 3)
    result, h2t, hidt, slopes, dr, do, delta, do_halo, delta_halo = feed(
        x, mixed, seeds, gain_two, rest_full, down_full, seq_count, halo
    )

    tokens = batch * stretch
    dps = lax.axis_size("dp")
    pairs = [list(range(core, seq_count * dps, 2)) for core in range(2)]
    scatter = lambda part: lax.psum_scatter(part, group, scatter_dimension=0, tiled=True, axis_index_groups=pairs)
    slopes = slopes.reshape(tokens, -1)
    part_down = weigh(
        [hidt], seeds.reshape(tokens, width), TILE, width // TILE, ((0, width // TILE, ((0, TILE),)),),
        w_down.shape[0], "weigh_down", 3,
    )
    shard_down = scatter(part_down)
    slopes, part_down = lax.optimization_barrier((slopes, part_down))
    part_early = weigh([h2t], slopes, CUT, EARLY, ((0, EARLY, ((0, CUT),)),), share, "weigh_early", 4)
    shard_early = scatter(part_early)
    do_halo, part_early = lax.optimization_barrier((do_halo, part_early))
    def back(first_batch, count, held):
        return attend_back(
            own, lows, highs, qkv, do, do_halo, lse, lse_halo, delta, delta_halo, marks_k, marks_q, cosines, sines,
            first_batch, count, held,
        )

    slopes_qkv = back(0, batch // 2, None)
    slopes_qkv, shard_early, shard_down = lax.optimization_barrier((slopes_qkv, shard_early, shard_down))
    early_sum, down_sum = lax.psum((shard_early, shard_down), "rep")
    slopes_qkv = back(batch // 2, batch - batch // 2, slopes_qkv)
    grad_x, late_sum, grad_qkv = close(
        h2t, mixed_t, h1t, slopes, 2 * FF_PAD, slopes_qkv.reshape(3, tokens, width), qkv_full, x.reshape(tokens, width), dr.reshape(tokens, width),
        gain_one, seq_count, dps, lax.axis_size("rep"),
    )
    grad_qkv = grad_qkv.astype(F32)
    rest_sum = jnp.concatenate([early_sum, late_sum], axis=1).astype(F32)
    grad_in = jnp.concatenate([rest_sum[:, :FF], rest_sum[:, FF_PAD : FF_PAD + FF]], axis=1)
    grad_attn_gain = jnp.sum(grad_qkv * w_qkv.astype(F32), axis=1) / attn_gain.astype(F32)
    grad_mlp_gain = jnp.sum(grad_in * w_in.astype(F32), axis=1) / mlp_gain.astype(F32)
    return (
        result.reshape(cotangent.shape),
        grad_x.reshape(inputs.shape),
        grad_attn_gain,
        grad_mlp_gain,
        grad_qkv,
        rest_sum[:, 2 * FF_PAD : 2 * FF_PAD + width],
        grad_in,
        down_sum[: w_down.shape[0]].astype(F32),
    )


def solution(mesh):
    return jax.shard_map(
        body,
        mesh=mesh,
        in_specs=(
            P(None, ("dp", "rep"), "seq", None),
            P(None, ("dp", "rep"), None),
            P(None, ("dp", "rep"), "seq", None),
            P(("seq", "dp")),
            P(("seq", "dp")),
            P(("seq", "dp"), None),
            P(("seq", "dp"), None),
            P(("seq", "dp"), None),
            P(("seq", "dp"), None),
        ),
        out_specs=(
            P(None, ("dp", "rep"), "seq", None),
            P(None, ("dp", "rep"), "seq", None),
            P(("seq", "dp")),
            P(("seq", "dp")),
            P(("seq", "dp"), None),
            P(("seq", "dp"), None),
            P(("seq", "dp"), None),
            P(("seq", "dp"), None),
        ),
        check_vma=False,
    )
```

```python
import functools

import jax
import jax.numpy as jnp
from jax import lax
from jax.experimental import pallas as pl
from jax.experimental.pallas import tpu as pltpu
from jax.sharding import PartitionSpec as P

HEADS = 16
HEAD_DIM = 64
FF = 2624
HALF = 512
DOCS = 7

EPS = 1e-05
THETA = 10000.0
MASKED = -1e30

TILE = 256
CUT = 512
REACH = HALF // TILE
LANES = 128
FF_PAD = -(-FF // LANES) * LANES
PAIRS = HEADS // 2
WIDE = 4
WIDE_BACK = 2
VMEM = 60 * 1024 * 1024

F32 = jnp.float32
BF16 = jnp.bfloat16

MESH = pl.DeviceIdType.MESH

NN = (((1,), (0,)), ((), ()))
NT = (((1,), (1,)), ((), ()))


def dot(left, right, dims=NN):
    return lax.dot_general(left, right, dims, preferred_element_type=F32)


def params(**more):
    return pltpu.CompilerParams(vmem_limit_bytes=VMEM, **more)


def normed(values):
    centre = values - jnp.mean(values, axis=-1, keepdims=True)
    spread = jnp.mean(centre * centre, axis=-1, keepdims=True)
    inverse = lax.rsqrt(spread + EPS)
    return centre * inverse, inverse


def norm_back(grads, unit, inverse):
    first = jnp.mean(grads, axis=-1, keepdims=True)
    second = jnp.mean(grads * unit, axis=-1, keepdims=True)
    return (grads - first - unit * second) * inverse


def swapped(values):
    lane = lax.broadcasted_iota(jnp.int32, values.shape, 1)
    ahead = pltpu.roll(values, LANES - HEAD_DIM // 2, 1)
    behind = pltpu.roll(values, HEAD_DIM // 2, 1)
    return jnp.where(lane % HEAD_DIM < HEAD_DIM // 2, ahead, behind)


def project_kernel(keep, shards, x_ref, w_ref, cos_ref, sin_ref, *outs):
    qkv_ref = outs[-1]
    width = x_ref.shape[2]
    share = width // shards
    gain = jnp.concatenate(
        [w_ref[share * i : share * i + 1, 3 * width : 3 * width + share] for i in range(shards)], axis=1
    ).astype(F32)
    unit, _ = normed(x_ref[0].astype(F32))
    h1 = (unit * gain).astype(BF16)
    if keep:
        outs[0][...] = h1.T
    cosines, sines = cos_ref[0], sin_ref[0]
    for start in range(0, 3 * width, 512):
        part = dot(h1, w_ref[:, start : start + 512])
        for column in range(0, 512, LANES):
            piece = part[:, column : column + LANES]
            if start < 2 * width:
                piece = piece * cosines + swapped(piece) * sines
            if start < width:
                piece = piece * HEAD_DIM**-0.5
            qkv_ref[0, :, start + column : start + column + LANES] = piece.astype(BF16)


def project(x, weight, cosines, sines, first_tile, held, extent, shards):
    batch, rows, width = x.shape
    steps = rows // TILE
    grid = (batch, steps)
    keep = held is None
    block = lambda b, i: (b, i, 0)
    shifted = lambda b, i: (b, i + first_tile, 0)
    qkv_spec = pl.BlockSpec((1, TILE, 3 * width), shifted)
    qkv_shape = jax.ShapeDtypeStruct((batch, extent, 3 * width), BF16)
    in_specs = [
        pl.BlockSpec((1, TILE, width), block),
        pl.BlockSpec(weight.shape, lambda b, i: (0, 0), pipeline_mode=pl.Buffered(1)),
        pl.BlockSpec((1, TILE, LANES), shifted),
        pl.BlockSpec((1, TILE, LANES), shifted),
    ]
    cost = pl.CostEstimate(
        flops=2 * batch * rows * width * 3 * width,
        bytes_accessed=8 * batch * rows * width + 6 * width * width,
        transcendentals=0,
    )
    if keep:
        return pl.pallas_call(
            functools.partial(project_kernel, True, shards),
            grid=grid,
            in_specs=in_specs,
            out_specs=[pl.BlockSpec((width, TILE), lambda b, i: (0, b * steps + i)), qkv_spec],
            out_shape=[jax.ShapeDtypeStruct((width, batch * rows), BF16), qkv_shape],
            compiler_params=params(),
            cost_estimate=cost,
            name="project_own",
        )(x, weight, cosines, sines)

    def halo_kernel(x_ref, w_ref, cos_ref, sin_ref, held_ref, qkv_ref):
        project_kernel(False, shards, x_ref, w_ref, cos_ref, sin_ref, qkv_ref)

    return pl.pallas_call(
        halo_kernel,
        grid=grid,
        in_specs=in_specs + [pl.BlockSpec(memory_space=pl.ANY)],
        out_specs=qkv_spec,
        out_shape=qkv_shape,
        input_output_aliases={4: 0},
        compiler_params=params(),
        cost_estimate=cost,
        name="project_halo",
    )(x, weight, cosines, sines, held)


def edge_masks():
    key = lax.broadcasted_iota(jnp.int32, (TILE, TILE), 0)
    query = lax.broadcasted_iota(jnp.int32, (TILE, TILE), 1)
    return (
        jnp.where(key >= query, 0.0, MASKED).astype(F32),
        jnp.where(key <= query, 0.0, MASKED).astype(F32),
    )


def edge_of(key_tile, query_tile):
    gap = key_tile - query_tile
    return jnp.where(gap == -REACH, 0, jnp.where(gap == REACH, 2, 1))


def low_half(rows):
    return lax.broadcasted_iota(jnp.int32, (rows, LANES), 1) < HEAD_DIM


def split3(values):
    high = values.astype(BF16).astype(F32)
    rest = values - high
    middle = rest.astype(BF16).astype(F32)
    return high, middle, rest - middle


def attend_kernel(tiles, wide, own_ref, lo_ref, hi_ref, q_ref, k_ref, v_ref, ek_ref, eq_ref, o_ref, ot_ref, lse_ref,
                  kx, qx, vx, edges):
    batch = pl.program_id(0)
    stretch, extent = q_ref.shape[1], k_ref.shape[1]

    @pl.when((batch == 0) & (pl.program_id(1) == 0))
    def _():
        before, after = edge_masks()
        edges[0] = before
        edges[1] = jnp.zeros((TILE, TILE), F32)
        edges[2] = after

    low = low_half(extent)
    marks = ek_ref[0]
    ones = jnp.ones((16, extent), BF16)
    for pair in range(wide):
        span = slice(pair * LANES, (pair + 1) * LANES)
        keys = k_ref[0, :, span]
        kx[2 * pair] = jnp.where(low, keys, marks)
        kx[2 * pair + 1] = jnp.where(low, marks, keys)
        turned = q_ref[0, :, span].T
        qx[2 * pair] = jnp.concatenate([turned[:HEAD_DIM], eq_ref[0]], axis=0)
        qx[2 * pair + 1] = jnp.concatenate([eq_ref[0], turned[HEAD_DIM:]], axis=0)
        flipped = v_ref[0, :, span].T
        vx[2 * pair] = jnp.concatenate([flipped[:HEAD_DIM], ones], axis=0)
        vx[2 * pair + 1] = jnp.concatenate([flipped[HEAD_DIM:], ones], axis=0)
    own = own_ref[0]

    def one_tile(index, carry):
        query_tile = own + index
        first, last = lo_ref[batch, query_tile], hi_ref[batch, query_tile]
        columns = pl.ds(pl.multiple_of(index * TILE, TILE), TILE)

        def some(count):
            places, masks = [], []
            for step in range(count):
                key_tile = first + step
                places.append(pl.multiple_of(lax.rem(key_tile - own + tiles, tiles) * TILE, TILE))
                masks.append(edge_of(key_tile, query_tile))

            def score(head):
                return [
                    dot(kx[head, pl.ds(place, TILE), :], qx[head, :, columns]) + edges[mask]
                    for place, mask in zip(places, masks)
                ]

            heads = 2 * wide
            scores = {head: score(head) for head in range(min(1, heads))}
            mixed, waiting = [], []

            def close_head(head, top, powers):
                sums = dot(
                    jnp.concatenate([vx[head, :, pl.ds(place, TILE)] for place in places], axis=1),
                    jnp.concatenate(powers, axis=0),
                )
                total = sums[HEAD_DIM : HEAD_DIM + 1]
                mixed.append(sums[:HEAD_DIM] * (1.0 / total))
                lse_ref[0, head // 2, head % 2 : head % 2 + 1, columns] = top + jnp.log(total)
                if head % 2 == 1:
                    both = jnp.concatenate(mixed[-2:], axis=0)
                    span = slice(head // 2 * LANES, (head // 2 + 1) * LANES)
                    ot_ref[span, columns] = both.astype(BF16)
                    o_ref[0, columns, span] = both.T.astype(BF16)

            for head in range(heads):
                if head + 1 < heads:
                    scores[head + 1] = score(head + 1)
                parts = scores.pop(head)
                top = parts[0]
                for part in parts[1:]:
                    top = jnp.maximum(top, part)
                top = jnp.max(top, axis=0, keepdims=True)
                powers = [jnp.exp(part - top).astype(BF16) for part in parts]
                waiting.append((head, top, powers))
                if len(waiting) > 1:
                    close_head(*waiting.pop(0))
            for item in waiting:
                close_head(*item)

        for count in range(1, 2 * REACH + 2):
            pl.when(last - first == count)(functools.partial(some, count))
        return carry

    lax.fori_loop(0, stretch // TILE, one_tile, 0)


def attend(own, lows, highs, qkv, marks_k, marks_q, stretch):
    batch, extent, _ = qkv.shape
    tiles = extent // TILE
    width = PAIRS * LANES
    wide = WIDE
    groups = PAIRS // wide
    spec = lambda rows, offset: pl.BlockSpec((1, rows, wide * LANES), lambda b, p, *_: (b, 0, p + offset))
    per = pl.BlockSpec((1, extent, LANES), lambda b, p, *_: (b, 0, 0))
    return pl.pallas_call(
        functools.partial(attend_kernel, tiles, wide),
        grid_spec=pltpu.PrefetchScalarGridSpec(
            num_scalar_prefetch=3,
            grid=(batch, groups),
            in_specs=[
                spec(stretch, 0),
                spec(extent, groups),
                spec(extent, 2 * groups),
                per,
                pl.BlockSpec((1, HEAD_DIM, stretch), lambda b, p, *_: (b, 0, 0)),
            ],
            out_specs=[
                spec(stretch, 0),
                pl.BlockSpec((wide * LANES, stretch), lambda b, p, *_: (p, b)),
                pl.BlockSpec((1, wide, 2, stretch), lambda b, p, *_: (b, p, 0, 0)),
            ],
            scratch_shapes=[
                pltpu.VMEM((2 * wide, extent, LANES), BF16),
                pltpu.VMEM((2 * wide, LANES, stretch), BF16),
                pltpu.VMEM((2 * wide, HEAD_DIM + 16, extent), BF16),
                pltpu.VMEM((3, TILE, TILE), F32),
            ],
        ),
        out_shape=[
            jax.ShapeDtypeStruct((batch, stretch, width), BF16),
            jax.ShapeDtypeStruct((width, batch * stretch), BF16),
            jax.ShapeDtypeStruct((batch, PAIRS, 2, stretch), F32),
        ],
        compiler_params=params(),
        cost_estimate=pl.CostEstimate(
            flops=2 * 2 * HEADS * batch * stretch * extent * 128, bytes_accessed=32 * 1024 * 1024, transcendentals=0
        ),
        name="attend",
    )(own, lows, highs, qkv, qkv, qkv, marks_k, marks_q)


def attend_back_kernel(tiles, wide, first_batch, own_ref, lo_ref, hi_ref, q_ref, k_ref, v_ref, do_ref, doh_ref, lse_ref, lseh_ref,
                       delta_ref, deltah_ref, ek_ref, eq_ref, cos_ref, sin_ref, *refs):
    out_ref, kx, vx, qx, dx, dn, kt, dqt, edges = refs[-9:]
    batch = pl.program_id(0) + first_batch
    extent = k_ref.shape[1]
    stretch = do_ref.shape[1]
    mine = stretch // TILE
    heads = 2 * wide

    @pl.when((pl.program_id(0) == 0) & (pl.program_id(1) == 0))
    def _():
        before, after = edge_masks()
        edges[0] = before
        edges[1] = jnp.zeros((TILE, TILE), F32)
        edges[2] = after

    low = low_half(extent)
    marks = ek_ref[0]
    lane = lax.broadcasted_iota(jnp.int32, (extent, LANES), 1) % HEAD_DIM
    units = jnp.where((lane >= 8) & (lane < 11), 1.0, 0.0).astype(BF16)
    row = lax.broadcasted_iota(jnp.int32, (HEAD_DIM, extent), 0)
    label_rows = eq_ref[0].astype(F32)
    dn[:stretch] = do_ref[0]
    dn[stretch:] = doh_ref[0]
    for pair in range(wide):
        span = slice(pair * LANES, (pair + 1) * LANES)
        keys, values = k_ref[0, :, span], v_ref[0, :, span]
        kx[2 * pair] = jnp.where(low, keys, marks)
        kx[2 * pair + 1] = jnp.where(low, marks, keys)
        kt[span] = keys.T
        vx[2 * pair] = jnp.where(low, values, units)
        vx[2 * pair + 1] = jnp.where(low, units, values)
        turned, flipped = q_ref[0, :, span].T, dn[:, span].T
        lses = jnp.concatenate([lse_ref[0, pair], lseh_ref[0, pair]], axis=1)
        deltas = jnp.concatenate([delta_ref[0, pair], deltah_ref[0, pair]], axis=1)
        for half in range(2):
            lse = split3(lses[half : half + 1])
            delta = split3(deltas[half : half + 1])
            mark, shift = label_rows, jnp.zeros((HEAD_DIM, extent), F32)
            for place in range(3):
                mark = jnp.where(row == 8 + place, -lse[place], mark)
                shift = jnp.where(row == 8 + place, -delta[place], shift)
            mark, shift = mark.astype(BF16), shift.astype(BF16)
            rows = slice(half * HEAD_DIM, (half + 1) * HEAD_DIM)
            order = (lambda a, b: [a, b]) if half == 0 else (lambda a, b: [b, a])
            qx[2 * pair + half] = jnp.concatenate(order(turned[rows], mark), axis=0)
            dx[2 * pair + half] = jnp.concatenate(order(flipped[rows], shift), axis=0)

    own = own_ref[0]
    dqt[...] = jnp.zeros_like(dqt)
    low_tile = low_half(TILE)

    def place(tile):
        return pl.ds(pl.multiple_of(lax.rem(tile - own + tiles, tiles) * TILE, TILE), TILE)

    def some(key_tile, begin, count, key_grad, out_rows):
        rows = place(key_tile)
        columns = [place(begin + step) for step in range(count)]
        masks = [edge_of(key_tile, begin + step) for step in range(count)]
        items = [(head, step) for head in range(heads) for step in range(count)]
        powers, slopes, sums = {}, {}, {}

        def first_products(head, step):
            score = dot(kx[head, rows, :], qx[head, :, columns[step]]) + edges[masks[step]]
            return score, dot(vx[head, rows, :], dx[head, :, columns[step]])

        def last_products(head, step):
            span = slice(head * HEAD_DIM, (head + 1) * HEAD_DIM)
            dqt[span, columns[step]] += dot(kt[span, rows], slopes[head][step])
            if not key_grad or step + 1 < count:
                return
            pair = slice(head // 2 * LANES, (head // 2 + 1) * LANES)
            grads = jnp.concatenate([dn[column, pair] for column in columns], axis=0)
            queries = jnp.concatenate([q_ref[0, column, pair] for column in columns], axis=0)
            sums[head] = (
                dot(jnp.concatenate(slopes.pop(head), axis=1), queries),
                dot(jnp.concatenate(powers.pop(head), axis=1), grads),
            )
            if head % 2 == 1:
                key_sum, value_sum = (jnp.where(low_tile, a, b) for a, b in zip(sums[head - 1], sums[head]))
                cosines, sines = cos_ref[0, out_rows, :], sin_ref[0, out_rows, :]
                out_ref[1, 0, out_rows, pair] = (key_sum * cosines - swapped(key_sum) * sines).astype(BF16)
                out_ref[2, 0, out_rows, pair] = value_sum.astype(BF16)

        ahead = [first_products(*items[0])]
        for index, (head, step) in enumerate(items):
            if index + 1 < len(items):
                ahead.append(first_products(*items[index + 1]))
            score, slope = ahead.pop(0)
            power = jnp.exp(score)
            powers.setdefault(head, []).append(power.astype(BF16))
            slopes.setdefault(head, []).append((power * slope).astype(BF16))
            if index >= 1:
                last_products(*items[index - 1])
        last_products(*items[-1])

    def own_keys(index, carry):
        key_tile = own + index
        first, last = lo_ref[batch, key_tile], hi_ref[batch, key_tile]
        out_rows = pl.ds(pl.multiple_of(index * TILE, TILE), TILE)
        for count in range(1, 2 * REACH + 2):
            pl.when(last - first == count)(functools.partial(some, key_tile, first, count, True, out_rows))
        return carry

    lax.fori_loop(0, mine, own_keys, 0)

    def other_keys(mem, carry):
        ahead = own + mem
        key_tile = jnp.where(ahead < own + mine + REACH, ahead, ahead - tiles)
        if tiles == mine + REACH:
            key_tile = jnp.where(own == 0, ahead, ahead - tiles)
        valid = (key_tile >= 0) & (key_tile < lo_ref.shape[1])
        safe = jnp.where(valid, key_tile, 0)
        begin = jnp.maximum(lo_ref[batch, safe], own)
        end = jnp.where(valid, jnp.minimum(hi_ref[batch, safe], own + mine), begin)
        for count in range(1, min(REACH, mine) + 1):
            pl.when(end - begin == count)(functools.partial(some, safe, begin, count, False, None))
        return carry

    lax.fori_loop(mine, tiles, other_keys, 0)
    for pair in range(wide):
        span = slice(pair * LANES, (pair + 1) * LANES)
        raw = dqt[span, :stretch].T * HEAD_DIM**-0.5
        out_ref[0, 0, :, span] = (raw * cos_ref[0] - swapped(raw) * sin_ref[0]).astype(BF16)


def attend_back(own, lows, highs, qkv, grads, grads_halo, lse, lse_halo, delta, delta_halo, marks_k, marks_q,
                cosines, sines, first_batch, count, held):
    batch, extent, _ = qkv.shape
    stretch, width = grads.shape[1:]
    halo = extent - stretch
    tiles = extent // TILE
    wide = WIDE_BACK
    groups = PAIRS // wide
    spec = lambda rows, offset: pl.BlockSpec((1, rows, wide * LANES), lambda b, p, *_: (b + first_batch, 0, p + offset))
    per = lambda rows: pl.BlockSpec((1, rows, LANES), lambda b, p, *_: (b + first_batch, 0, 0))
    numbers = lambda rows: pl.BlockSpec((1, wide, 2, rows), lambda b, p, *_: (b + first_batch, p, 0, 0))
    return pl.pallas_call(
        functools.partial(attend_back_kernel, tiles, wide, first_batch),
        grid_spec=pltpu.PrefetchScalarGridSpec(
            num_scalar_prefetch=3,
            grid=(count, groups),
            in_specs=[
                spec(extent, 0),
                spec(extent, groups),
                spec(extent, 2 * groups),
                spec(stretch, 0),
                spec(halo, 0),
                numbers(stretch),
                numbers(halo),
                numbers(stretch),
                numbers(halo),
                per(extent),
                pl.BlockSpec((1, HEAD_DIM, extent), lambda b, p, *_: (b + first_batch, 0, 0)),
                per(stretch),
                per(stretch),
            ]
            + ([] if held is None else [pl.BlockSpec(memory_space=pl.ANY)]),
            out_specs=pl.BlockSpec((3, 1, stretch, wide * LANES), lambda b, p, *_: (0, b + first_batch, 0, p)),
            scratch_shapes=[
                pltpu.VMEM((2 * wide, extent, LANES), BF16),
                pltpu.VMEM((2 * wide, extent, LANES), BF16),
                pltpu.VMEM((2 * wide, LANES, extent), BF16),
                pltpu.VMEM((2 * wide, LANES, extent), BF16),
                pltpu.VMEM((extent, wide * LANES), BF16),
                pltpu.VMEM((wide * LANES, extent), BF16),
                pltpu.VMEM((wide * LANES, extent), F32),
                pltpu.VMEM((3, TILE, TILE), F32),
            ],
        ),
        input_output_aliases={} if held is None else {16: 0},
        out_shape=jax.ShapeDtypeStruct((3, batch, stretch, width), BF16),
        compiler_params=params(),
        cost_estimate=pl.CostEstimate(
            flops=5 * 2 * HEADS * count * stretch * extent * 128, bytes_accessed=64 * 1024 * 1024, transcendentals=0
        ),
        name="attend_back",
    )(own, lows, highs, qkv, qkv, qkv, grads, grads_halo, lse, lse_halo, delta, delta_halo, marks_k, marks_q,
      cosines, sines, *([] if held is None else [held]))


def feed_kernel(seqs, halo_tiles, x_ref, o_ref, g_ref, gain_ref, w_ref, wd_ref,
                out_ref, h2t_ref, hidt_ref, slopes_ref, dr_ref, do_ref, delta_ref, do_halo, delta_halo,
                do_sent, delta_sent, send_sem, recv_sem):
    batch, steps = pl.num_programs(1), pl.num_programs(0)
    step, sequence = pl.program_id(0), pl.program_id(1)
    seq = lax.axis_index("seq")
    mine, tiles = steps, steps + halo_tiles
    reach = -(-REACH // mine)
    hops = [hop for hop in range(-reach, reach + 1) if hop != 0]

    def exists(hop):
        return (seq + hop >= 0) & (seq + hop < seqs)

    def sent(which, tile, hop):
        peer = seq + hop
        place = seq * mine + tile
        wanted = exists(hop) & (place >= peer * mine - REACH) & (place < (peer + 1) * mine + REACH)
        slot = lax.rem(place - peer * mine + tiles, tiles) - mine
        slot = jnp.where(wanted, slot, 0)
        return wanted, halo_copies(which, tile, slot, hops.index(hop), peer)

    def halo_copies(which, tile, slot, hop, peer):
        span = pl.ds(pl.multiple_of(slot * TILE, TILE), TILE)
        pieces = [
            (do_sent.at[which, tile], do_halo.at[which, span]),
            (delta_sent.at[which, tile], delta_halo.at[which, :, :, span]),
        ]
        return [
            pltpu.make_async_remote_copy(
                src_ref=source, dst_ref=target, send_sem=send_sem.at[kind, which, tile, hop],
                recv_sem=recv_sem.at[kind, which, slot], device_id={"seq": peer}, device_id_type=MESH,
            )
            for kind, (source, target) in enumerate(pieces)
        ]

    @pl.when((step == 0) & (sequence == 0))
    def _():
        barrier = pltpu.get_barrier_semaphore()
        for hop in hops:
            @pl.when(exists(hop))
            def _():
                pl.semaphore_signal(barrier, inc=1, device_id={"seq": seq + hop}, device_id_type=MESH)

        for hop in hops:
            @pl.when(exists(hop))
            def _():
                pl.semaphore_wait(barrier, 1)

    mixed = o_ref[0]
    seeds = g_ref[0]
    gain = gain_ref[...]
    width = mixed.shape[1]
    w_out = slice(2 * FF_PAD, 2 * FF_PAD + width)
    r1 = x_ref[0].astype(F32) + dot(mixed, w_ref[:, w_out])
    unit, inverse = normed(r1)
    h2 = (unit * gain).astype(BF16)
    h2t_ref[...] = h2.T
    total = r1
    back = jnp.zeros_like(r1)
    edges = list(range(0, FF - 511, 512))
    for start, stop in zip(edges, edges[1:] + [FF]):
        gates, ups = slice(start, stop), slice(FF_PAD + start, FF_PAD + stop)
        gate = dot(h2, w_ref[:, gates])
        up = dot(h2, w_ref[:, ups])
        grad = dot(seeds, wd_ref[start:stop, :], NT)
        phi = 0.5 + 0.5 * lax.erf(gate * (0.5**0.5))
        bell = jnp.exp(gate * gate * -0.5) * 0.3989422804014327
        act = gate * phi
        hid = (act * up).astype(BF16)
        grad_gate = (grad * up * (phi + gate * bell)).astype(BF16)
        grad_up = (grad * act).astype(BF16)
        hidt_ref[start:stop, :] = hid.T
        slopes_ref[0, :, gates] = grad_gate
        slopes_ref[0, :, ups] = grad_up
        total = total + dot(hid, wd_ref[start:stop, :])
        back = back + dot(grad_gate, w_ref[:, gates], NT) + dot(grad_up, w_ref[:, ups], NT)
    blank = jnp.zeros((TILE, FF_PAD - FF), BF16)
    slopes_ref[0, :, 2 * FF_PAD + width :] = jnp.zeros((TILE, slopes_ref.shape[2] - 2 * FF_PAD - width), BF16)
    slopes_ref[0, :, FF:FF_PAD] = blank
    slopes_ref[0, :, FF_PAD + FF : 2 * FF_PAD] = blank
    out_ref[0] = total.astype(BF16)
    dr = seeds.astype(F32) + norm_back(back * gain, unit, inverse)
    dr_ref[0] = dr
    da = dr.astype(BF16)
    slopes_ref[0, :, w_out] = da
    do = dot(da, w_ref[:, w_out], NT).astype(BF16)
    do_ref[0] = do
    product = do.astype(F32) * mixed.astype(F32)
    high = product.astype(BF16)
    rest = (product - high.astype(F32)).astype(BF16)
    head = lax.broadcasted_iota(jnp.int32, (HEADS, width), 0)
    column = lax.broadcasted_iota(jnp.int32, (HEADS, width), 1)
    pick = jnp.where(column // HEAD_DIM == head, 1.0, 0.0).astype(BF16)
    delta = dot(pick, high, NT) + dot(pick, rest, NT)
    tile = facing_first(step, steps, seqs)
    do_sent[sequence, tile] = do
    for pair in range(PAIRS):
        delta_ref[0, pair] = delta[2 * pair : 2 * pair + 2]
        delta_sent[sequence, tile, pair] = delta[2 * pair : 2 * pair + 2]
    for hop in hops:
        wanted, copies = sent(sequence, tile, hop)

        @pl.when(wanted)
        def _():
            for copy in copies:
                copy.start()

    @pl.when((step == steps - 1) & (sequence == batch - 1))
    def _():
        def settle(index, carry):
            which, tile = index // mine, lax.rem(index, mine)
            for hop in hops:
                wanted, copies = sent(which, tile, hop)

                @pl.when(wanted)
                def _():
                    for copy in copies:
                        copy.wait_send()

            return carry

        lax.fori_loop(0, batch * mine, settle, 0)

        def arrive(index, carry):
            which, slot = index // halo_tiles, lax.rem(index, halo_tiles)
            place = seq * mine + mine + slot
            if halo_tiles == REACH:
                place = jnp.where(seq == 0, place, place - tiles)
            else:
                place = jnp.where(slot < REACH, place, place - tiles)

            @pl.when((place >= 0) & (place < seqs * mine))
            def _():
                for copy in halo_copies(which, 0, slot, 0, seq):
                    copy.wait_recv()

            return carry

        lax.fori_loop(0, batch * halo_tiles, arrive, 0)


def facing_first(step, steps, seqs):
    if seqs != 2:
        return step
    return lax.rem(step + (1 - lax.axis_index("seq")) * (steps // 2), steps)


def feed(x, mixed, seeds, gain, w_rest, w_down, seqs, halo):
    batch, rows, width = x.shape
    steps = rows // TILE
    place = lambda i: facing_first(i, steps, seqs)
    block = lambda n: pl.BlockSpec((1, TILE, n), lambda i, b: (b, place(i), 0))
    turned = lambda n: pl.BlockSpec((n, TILE), lambda i, b: (0, b * steps + place(i)))
    fixed = lambda m, n: pl.BlockSpec((m, n), lambda i, b: (0, 0), pipeline_mode=pl.Buffered(1))
    shape = lambda n, t: jax.ShapeDtypeStruct((batch, rows, n), t)
    columns = w_rest.shape[1]
    padded = -(-columns // CUT) * CUT
    reach = -(-REACH // steps)
    return pl.pallas_call(
        functools.partial(feed_kernel, seqs, halo // TILE),
        grid=(steps, batch),
        in_specs=[
            block(width), block(width), block(width), fixed(1, width), fixed(width, columns), fixed(FF, width),
        ],
        out_specs=[
            block(width), turned(width), turned(FF), block(padded), block(width), block(width),
            pl.BlockSpec((1, PAIRS, 2, TILE), lambda i, b: (b, 0, 0, place(i))),
            pl.BlockSpec(memory_space=pl.ANY),
            pl.BlockSpec(memory_space=pl.ANY),
        ],
        out_shape=[
            shape(width, BF16),
            jax.ShapeDtypeStruct((width, batch * rows), BF16),
            jax.ShapeDtypeStruct((FF, batch * rows), BF16),
            shape(padded, BF16),
            shape(width, F32),
            shape(width, BF16),
            jax.ShapeDtypeStruct((batch, PAIRS, 2, rows), F32),
            jax.ShapeDtypeStruct((batch, halo, width), BF16),
            jax.ShapeDtypeStruct((batch, PAIRS, 2, halo), F32),
        ],
        scratch_shapes=[
            pltpu.VMEM((batch, steps, TILE, width), BF16),
            pltpu.VMEM((batch, steps, PAIRS, 2, TILE), F32),
            pltpu.SemaphoreType.DMA((2, batch, steps, 2 * reach)),
            pltpu.SemaphoreType.DMA((2, batch, halo // TILE)),
        ],
        compiler_params=params(collective_id=2, has_side_effects=True),
        cost_estimate=pl.CostEstimate(
            flops=2 * batch * rows * width * (6 * FF + 2 * width), bytes_accessed=64 * 1024 * 1024, transcendentals=0
        ),
        name="feed",
    )(x, mixed, seeds, gain, w_rest, w_down)


def weigh_kernel(blocks, share, held, turns, *refs):
    lefts, (right_ref, out_ref, prod, kept, sent, got, send_sem, recv_sem) = refs[:-8], refs[-8:]
    step = pl.program_id(0)
    dp = lax.axis_index("dp")
    core = lax.rem(dp, 2)
    mate = dp + 1 - 2 * core
    places = prod.shape[0] // (2 * share)

    def to_mate(n):
        return pltpu.make_async_remote_copy(
            src_ref=sent.at[n], dst_ref=got.at[n], send_sem=send_sem.at[n], recv_sem=recv_sem.at[n],
            device_id={"dp": mate}, device_id_type=MESH,
        )

    @pl.when(step == 0)
    def _():
        barrier = pltpu.get_barrier_semaphore()
        pl.semaphore_signal(barrier, inc=1, device_id={"dp": mate}, device_id_type=MESH)
        pl.semaphore_wait(barrier, 1)

    columns = right_ref.shape[1]
    for first, last, pieces in turns:

        @pl.when((step >= first) & (step < last))
        def _():
            start = 0
            for which, count in pieces:
                span = slice(start, start + count)
                prod[:, span] = dot(lefts[which][...], right_ref[:, span])
                start += count

    @pl.when(step < blocks)
    def _():
        for place in range(places):
            even = prod[2 * place * share : (2 * place + 1) * share, :]
            odd = prod[(2 * place + 1) * share : (2 * place + 2) * share, :]
            rows = slice(place * held, place * held + share)
            sent[step, rows, :] = jnp.where(core == 0, odd, even).astype(BF16)
            kept[step % 2, rows, :] = jnp.where(core == 0, even, odd)
            if held > share:
                rows = slice(place * held + share, (place + 1) * held)
                sent[step, rows, :] = jnp.zeros((held - share, columns), BF16)
                kept[step % 2, rows, :] = jnp.zeros((held - share, columns), F32)
        to_mate(step).start()

    @pl.when(step >= 1)
    def _():
        done = step - 1
        to_mate(done).wait()
        out_ref[...] = (kept[done % 2] + got[done].astype(F32)).astype(BF16)


def weigh(lefts, right, columns, blocks, turns, share, name, number):
    rows, tokens = lefts[0].shape
    total = blocks * columns
    held = -(-share // 16) * 16
    places = rows // (2 * share)
    fixed = pl.BlockSpec((rows, tokens), lambda n: (0, 0), pipeline_mode=pl.Buffered(1))
    return pl.pallas_call(
        functools.partial(weigh_kernel, blocks, share, held, turns),
        grid=(blocks + 1,),
        in_specs=[fixed] * len(lefts) + [pl.BlockSpec((tokens, columns), lambda n: (0, jnp.minimum(n, blocks - 1)))],
        out_specs=pl.BlockSpec((places * held, columns), lambda n: (0, jnp.maximum(n - 1, 0))),
        out_shape=jax.ShapeDtypeStruct((places * held, total), BF16),
        scratch_shapes=[
            pltpu.VMEM((rows, columns), F32),
            pltpu.VMEM((2, places * held, columns), F32),
            pltpu.VMEM((blocks, places * held, columns), BF16),
            pltpu.VMEM((blocks, places * held, columns), BF16),
            pltpu.SemaphoreType.DMA((blocks,)),
            pltpu.SemaphoreType.DMA((blocks,)),
        ],
        compiler_params=params(collective_id=number, has_side_effects=True),
        cost_estimate=pl.CostEstimate(
            flops=2 * rows * tokens * total, bytes_accessed=24 * 1024 * 1024, transcendentals=0
        ),
        name=name,
    )(*lefts, right)


LAGS = (1, 3, 5, 7, 9, 11)
RING, RING_XY, RING_LINE = 5, 2, 8
EARLY = 7


def close_kernel(blocks, rest_blocks, rest_edge, seqs, reps, h2t_ref, ot_ref, h1t_ref, rest_ref, right_ref, three_ref, w_ref, x_ref, dr_ref, gain_ref, gi_ref, rest_sum, sum_ref,
                 prod, kept0, kept1x, kept1y, kept2, s0, r0, s1x, r1x, s1y, r1y, s2x, r2x, s2y, r2y,
                 mine, ends, others, send_sem, recv_sem):
    step = pl.program_id(0)
    width = h1t_ref.shape[0]
    share = mine.shape[1]
    seq, dp, rep = lax.axis_index("seq"), lax.axis_index("dp"), lax.axis_index("rep")
    core, side = lax.rem(dp, 2), dp // 2
    mate, across = dp + 1 - 2 * core, lax.rem(dp + 2, 4)
    seq_peers = [lax.rem(seq + hop, seqs) for hop in range(1, seqs)]
    inner = (rep == 1) | (rep == 2)
    beside = rep + 1 - 2 * lax.rem(rep, 2)
    slot_seq, slot_side, slot_in = 1, seqs, seqs + 1

    def copy(source, target, n, slot, device):
        turn = lax.rem(n, 2 * RING_XY)
        return pltpu.make_async_remote_copy(
            src_ref=source, dst_ref=target, send_sem=send_sem.at[turn, slot], recv_sem=recv_sem.at[turn, slot],
            device_id=device, device_id_type=MESH,
        )

    def rows(first, count):
        return pl.ds(pl.multiple_of(first * share, share), count * share)

    def half(n):
        return lax.rem(n // 2, RING_XY)

    def to_mate(n):
        slot = lax.rem(n, RING)
        return [copy(s0.at[slot], r0.at[slot], n, 0, {"dp": mate})]

    def to_seq(n, source, target):
        return [
            copy(source.at[half(n), hop], target.at[half(n), hop], n, slot_seq + hop, {"seq": peer})
            for hop, peer in enumerate(seq_peers)
        ]

    def to_side(n, source, target):
        return [copy(source.at[half(n)], target.at[half(n)], n, slot_side, {"dp": across})]

    def line(which, source, first, second, sends, arrivals):
        start, target, device = (
            (source, first, beside), (first, second, reps - 1 - rep), (second, second, beside),
        )[which]
        return pltpu.make_async_remote_copy(
            src_ref=start, dst_ref=target, send_sem=sends, recv_sem=arrivals,
            device_id={"rep": device}, device_id_type=MESH,
        )

    def own_line(n, which):
        slot, turn = slot_in + which, lax.rem(n, RING_LINE)
        return line(which, mine.at[turn], ends.at[turn], others.at[turn], send_sem.at[turn, slot], recv_sem.at[turn, slot])

    def start(copies):
        for each in copies:
            each.start()

    def wait(copies):
        for each in copies:
            each.wait()

    @pl.when(step == 0)
    def _():
        barrier = pltpu.get_barrier_semaphore()
        partners = [{"dp": mate}, {"dp": across}]
        partners += [{"seq": peer} for peer in seq_peers] + [{"rep": beside}]
        for partner in partners:
            pl.semaphore_signal(barrier, inc=1, device_id=partner, device_id_type=MESH)

        @pl.when(inner)
        def _():
            pl.semaphore_signal(barrier, inc=1, device_id={"rep": reps - 1 - rep}, device_id_type=MESH)
            pl.semaphore_wait(barrier, len(partners) + 1)

        @pl.when(jnp.logical_not(inner))
        def _():
            pl.semaphore_wait(barrier, len(partners))

    whole_blocks, split = rest_edge // CUT, rest_edge % CUT

    @pl.when(step < whole_blocks)
    def _():
        prod[...] = dot(h2t_ref[...], rest_ref[...])

    @pl.when((step >= whole_blocks) & (step < rest_blocks))
    def _():
        if split:
            @pl.when(step == whole_blocks)
            def _():
                prod[:, :split] = dot(h2t_ref[...], rest_ref[:, :split])
                prod[:, split:] = dot(ot_ref[...], rest_ref[:, split:])

        @pl.when(step >= whole_blocks + (split > 0))
        def _():
            prod[...] = dot(ot_ref[...], rest_ref[...])

    @pl.when((step >= rest_blocks) & (step < blocks))
    def _():
        prod[...] = dot(h1t_ref[...], right_ref[0])

    @pl.when(step < blocks)
    def _():
        for place in range(2 * seqs):
            span = slice(place * share, (place + 1) * share)
            s0[lax.rem(step, RING), span, :] = prod[rows(2 * place + 1 - core, 1), :].astype(BF16)
        start(to_mate(step))
        for place in range(2 * seqs):
            span = slice(place * share, (place + 1) * share)
            kept0[step % 2, span, :] = prod[rows(2 * place + core, 1), :]

    @pl.when((step >= blocks) & (step < blocks + gi_steps(three_ref, right_ref)))
    def _():
        back = None
        for part in range(3):
            term = dot(three_ref[part], w_ref[:, part * width : (part + 1) * width], NT)
            back = term if back is None else back + term
        unit, inverse = normed(x_ref[...].astype(F32))
        gi_ref[...] = dr_ref[...] + norm_back(back * gain_ref[...], unit, inverse)

    n6 = step - LAGS[5]

    @pl.when((n6 >= 0) & (n6 < blocks))
    def _():
        @pl.when(inner)
        def _():
            own_line(n6, 2).wait_send()

        @pl.when(jnp.logical_not(inner))
        def _():
            own_line(n6, 2).wait_recv()

        total = others[lax.rem(n6, RING_LINE)]

        @pl.when(n6 < rest_blocks)
        def _():
            rest_sum[:, pl.ds(pl.multiple_of(n6 * CUT, CUT), CUT)] = total

        @pl.when(n6 >= rest_blocks)
        def _():
            sum_ref[:, pl.ds(pl.multiple_of((n6 - rest_blocks) * CUT, CUT), CUT)] = total

    n5 = step - LAGS[4]

    @pl.when((n5 >= 0) & (n5 < blocks) & inner)
    def _():
        own_line(n5, 1).wait()
        others[lax.rem(n5, RING_LINE)] = (ends[lax.rem(n5, RING_LINE)].astype(F32) + others[lax.rem(n5, RING_LINE)].astype(F32)).astype(BF16)
        own_line(n5, 2).start()

    n4 = step - LAGS[3]

    @pl.when((n4 >= 0) & (n4 < blocks) & inner)
    def _():
        own_line(n4, 0).wait_recv()
        ends[lax.rem(n4, RING_LINE)] = (mine[lax.rem(n4, RING_LINE)].astype(F32) + ends[lax.rem(n4, RING_LINE)].astype(F32)).astype(BF16)
        own_line(n4, 1).start()

    @pl.when((n4 >= 0) & (n4 < blocks) & jnp.logical_not(inner))
    def _():
        own_line(n4, 0).wait_send()

    n3 = step - LAGS[2]

    @pl.when((n3 >= 0) & (n3 < blocks))
    def _():
        total = kept2[n3 % 2]

        @pl.when(n3 % 2 == 0)
        def _():
            wait(to_side(n3, s2y, r2y))
            mine[lax.rem(n3, RING_LINE)] = (total + r2y[half(n3)].astype(F32)).astype(BF16)

        @pl.when(n3 % 2 == 1)
        def _():
            wait(to_seq(n3, s2x, r2x))
            added = total
            for hop in range(seqs - 1):
                added = added + r2x[half(n3), hop].astype(F32)
            mine[lax.rem(n3, RING_LINE)] = added.astype(BF16)

        @pl.when(jnp.logical_not(inner))
        def _():
            own_line(n3, 0).start()

    n2 = step - LAGS[1]

    @pl.when((n2 >= 0) & (n2 < blocks) & (n2 % 2 == 0))
    def _():
        wait(to_seq(n2, s1x, r1x))
        total = kept1x[...]
        for hop in range(seqs - 1):
            total = total + r1x[half(n2), hop].astype(F32)
        kept1x[...] = total
        s2y[half(n2)] = kept1x[rows(1 - side, 1), :].astype(BF16)
        start(to_side(n2, s2y, r2y))
        kept2[0] = kept1x[rows(side, 1), :]

    @pl.when((n2 >= 0) & (n2 < blocks) & (n2 % 2 == 1))
    def _():
        wait(to_side(n2, s1y, r1y))
        kept1y[...] = kept1y[...] + r1y[half(n2)].astype(F32)
        for hop, peer in enumerate(seq_peers):
            s2x[half(n2), hop] = kept1y[rows(peer, 1), :].astype(BF16)
        start(to_seq(n2, s2x, r2x))
        kept2[1] = kept1y[rows(seq, 1), :]

    n1 = step - LAGS[0]

    @pl.when((n1 >= 0) & (n1 < blocks))
    def _():
        wait(to_mate(n1))
        held = n1 % 2
        kept0[held] = kept0[held] + r0[lax.rem(n1, RING)].astype(F32)

        @pl.when(n1 % 2 == 0)
        def _():
            for hop, peer in enumerate(seq_peers):
                s1x[half(n1), hop] = kept0[held, rows(2 * peer, 2), :].astype(BF16)
            start(to_seq(n1, s1x, r1x))
            kept1x[...] = kept0[held, rows(2 * seq, 2), :]

        @pl.when(n1 % 2 == 1)
        def _():
            for place in range(seqs):
                s1y[half(n1), place * share : (place + 1) * share, :] = kept0[held, rows(2 * place + 1 - side, 1), :].astype(BF16)
            start(to_side(n1, s1y, r1y))
            for place in range(seqs):
                kept1y[place * share : (place + 1) * share, :] = kept0[held, rows(2 * place + side, 1), :]


def gi_steps(three_ref, right_ref):
    return right_ref.shape[1] // three_ref.shape[1]


def close(h2t, mixed_t, h1t, rest, rest_edge, slopes, weight, x, dr, gain, seqs, dps, reps):
    assert (dps, reps) == (4, 4)
    width, tokens = h1t.shape
    share = width // (seqs * dps)
    rest_blocks = rest.shape[1] // CUT - EARLY
    rest_edge = rest_edge - EARLY * CUT
    blocks = rest_blocks + 3 * width // CUT
    halves = width // CUT
    token_blocks = tokens // TILE
    steps = max(blocks + token_blocks, blocks + LAGS[5])
    late = lambda s: jnp.clip(s - blocks, 0, token_blocks - 1)
    turn_of = lambda s: jnp.clip(s - rest_blocks, 0, blocks - rest_blocks - 1)
    fixed = lambda m, n: pl.BlockSpec((m, n), lambda s: (0, 0), pipeline_mode=pl.Buffered(1))
    row = pl.BlockSpec((TILE, width), lambda s: (late(s), 0))
    half_rows = 2 * seqs * share
    buffers = lambda *shape: [pltpu.VMEM(shape + (CUT,), BF16)] * 2
    slots = seqs + 4
    return pl.pallas_call(
        functools.partial(close_kernel, blocks, rest_blocks, rest_edge, seqs, reps),
        grid=(steps,),
        in_specs=[
            fixed(width, tokens),
            fixed(width, tokens),
            fixed(width, tokens),
            pl.BlockSpec((tokens, CUT), lambda s: (0, EARLY + jnp.minimum(s, rest_blocks - 1))),
            pl.BlockSpec((1, tokens, CUT), lambda s: (turn_of(s) // halves, 0, turn_of(s) % halves)),
            pl.BlockSpec((3, TILE, width), lambda s: (0, late(s), 0)),
            fixed(*weight.shape),
            row,
            row,
            fixed(1, width),
        ],
        out_specs=[row, fixed(share, rest_blocks * CUT), fixed(share, 3 * width)],
        out_shape=[
            jax.ShapeDtypeStruct((tokens, width), F32),
            jax.ShapeDtypeStruct((share, rest_blocks * CUT), BF16),
            jax.ShapeDtypeStruct((share, 3 * width), BF16),
        ],
        scratch_shapes=[
            pltpu.VMEM((width, CUT), F32),
            pltpu.VMEM((2, half_rows, CUT), F32),
            pltpu.VMEM((2 * share, CUT), F32),
            pltpu.VMEM((seqs * share, CUT), F32),
            pltpu.VMEM((2, share, CUT), F32),
            *buffers(RING, half_rows),
            *buffers(RING_XY, seqs - 1, 2 * share),
            *buffers(RING_XY, seqs * share),
            *buffers(RING_XY, seqs - 1, share),
            *buffers(RING_XY, share),
            *[pltpu.VMEM((RING_LINE, share, CUT), BF16)] * 3,
            pltpu.SemaphoreType.DMA((max(2 * RING_XY, RING_LINE), slots)),
            pltpu.SemaphoreType.DMA((max(2 * RING_XY, RING_LINE), slots)),
        ],
        compiler_params=params(collective_id=1, has_side_effects=True),
        cost_estimate=pl.CostEstimate(
            flops=2 * tokens * width * (6 * width + rest.shape[1]), bytes_accessed=48 * 1024 * 1024, transcendentals=0
        ),
        name="close",
    )(h2t, mixed_t, h1t, rest, slopes, slopes, weight, x, dr, gain)


def neighbours(block, axis, along, after=None):
    count = lax.axis_size(axis)
    rows = block.shape[along]
    if count == 2:
        start = (1 - lax.axis_index(axis)) * (rows - HALF)
        facing = lax.dynamic_slice_in_dim(block, start, HALF, along)
        if after is not None:
            facing, _ = lax.optimization_barrier((facing, after))
        return lax.ppermute(facing, axis, [(0, 1), (1, 0)])
    step = min(rows, HALF)
    head = lax.slice_in_dim(block, 0, step, axis=along)
    tail = lax.slice_in_dim(block, rows - step, rows, axis=along)
    hops = range(1, HALF // step + 1)
    after = [lax.ppermute(head, axis, [(i + hop, i) for i in range(count - hop)]) for hop in hops]
    before = [lax.ppermute(tail, axis, [(i, i + hop) for i in range(count - hop)]) for hop in reversed(hops)]
    return jnp.concatenate(after + before, axis=along)


def survey(labels, stretch, extent, seq_index, seq_count):
    length = labels.shape[1]
    mem = jnp.arange(extent, dtype=jnp.int32)
    own_start = seq_index * stretch
    wraps = stretch + HALF if seq_count > 2 else jnp.where(seq_index == 0, extent, stretch)
    places = own_start + mem - jnp.where(mem >= wraps, extent, 0)
    padded = jnp.pad(labels, ((0, 0), (HALF, HALF)))
    cut = lambda first, size: lax.dynamic_slice_in_dim(padded, first + HALF, size, 1)
    parts = [cut(own_start, stretch)]
    if seq_count == 2:
        parts.append(cut(jnp.where(seq_index == 0, own_start + stretch, own_start - HALF), HALF))
    else:
        parts += [cut(own_start + stretch, HALF), cut(own_start - HALF, HALF)]
    near = jnp.concatenate(parts, axis=1)
    docs = jnp.arange(DOCS, dtype=jnp.int32)
    starts = jnp.sum(labels[:, :, None] < docs, axis=1, dtype=jnp.int32)
    stops = jnp.sum(labels[:, :, None] <= docs, axis=1, dtype=jnp.int32) - 1
    same = near[:, :, None] == docs
    positions = places - jnp.sum(jnp.where(same, starts[:, None, :], 0), axis=-1)
    lane = jnp.arange(LANES, dtype=jnp.int32)
    half_dim = HEAD_DIM // 2
    frequency = THETA ** (-((lane % half_dim).astype(F32) * 2.0 / HEAD_DIM))
    angles = positions.astype(F32)[:, :, None] * frequency
    cosines = jnp.cos(angles)
    sines = jnp.sin(angles) * jnp.where(lane % HEAD_DIM < half_dim, -1.0, 1.0)
    slot = lane % HEAD_DIM
    marks_k = jnp.where(
        slot < DOCS,
        jnp.where(near[:, :, None] == slot, 0.0, MASKED),
        jnp.where((slot >= 8) & (slot < 11), 1.0, 0.0),
    ).astype(BF16)
    kind = jnp.arange(HEAD_DIM, dtype=jnp.int32)[None, :, None]
    marks_q = jnp.where((kind < DOCS) & (near[:, None, :] == kind), 1.0, 0.0).astype(BF16)
    at = jnp.arange(length // TILE, dtype=jnp.int32) * TILE
    first_label, last_label = labels[:, ::TILE], labels[:, TILE - 1 :: TILE]
    pick = lambda table, which: jnp.sum(
        jnp.where(which[:, :, None] == docs, table[:, None, :], 0), axis=-1
    )
    lows = jnp.maximum(pick(starts, first_label), at - HALF) // TILE
    highs = jnp.minimum(pick(stops, last_label), at + TILE - 1 + HALF) // TILE + 1
    own = (own_start // TILE).astype(jnp.int32).reshape(1)
    return own, lows, highs, cosines, sines, marks_k, marks_q


def body(inputs, segments, cotangent, attn_gain, mlp_gain, w_qkv, w_out, w_in, w_down):
    stretch, width = inputs.shape[2:]
    length = segments.shape[2]
    x = inputs.reshape(-1, stretch, width)
    seeds = cotangent.reshape(-1, stretch, width)
    labels = segments.reshape(-1, length)
    batch = x.shape[0]
    group = ("seq", "dp")
    seq_index = lax.axis_index("seq")
    seq_count = lax.axis_size("seq")

    share = attn_gain.shape[0]
    shards = width // share
    gather = lambda shard: lax.all_gather(shard, group, axis=0, tiled=True)
    gain_rows = jnp.pad(jnp.stack([attn_gain, mlp_gain]), ((0, share - 2), (0, LANES - share)))
    qkv_full = gather(jnp.concatenate([w_qkv, gain_rows], axis=1))
    blank = jnp.zeros((share, FF_PAD - FF), BF16)
    halo = HALF * (1 if seq_count == 2 else 2)
    extent = stretch + halo
    own, lows, highs, cosines, sines, marks_k, marks_q = survey(labels, stretch, extent, seq_index, seq_count)
    x_halo = neighbours(x, "seq", 1, (qkv_full, cosines, sines, marks_k))
    rest_full = gather(jnp.concatenate([w_in[:, :FF], blank, w_in[:, FF:], blank, w_out], axis=1))
    down_full = gather(w_down)

    h1t, qkv = project(x, qkv_full, cosines, sines, 0, None, extent, shards)
    qkv = project(x_halo, qkv_full, cosines, sines, stretch // TILE, qkv, extent, shards)
    mixed, mixed_t, lse = attend(own, lows, highs, qkv, marks_k, marks_q, stretch)
    lse_halo = neighbours(lse, "seq", 3)
    late_full, mixed, lse_halo = lax.optimization_barrier((qkv_full, mixed, lse_halo))
    gains = late_full[:, 3 * width : 3 * width + share].reshape(shards, share, share).astype(F32)
    gain_one, gain_two = gains[:, 0].reshape(1, width), gains[:, 1].reshape(1, width)
    result, h2t, hidt, slopes, dr, do, delta, do_halo, delta_halo = feed(
        x, mixed, seeds, gain_two, rest_full, down_full, seq_count, halo
    )

    tokens = batch * stretch
    dps = lax.axis_size("dp")
    pairs = [list(range(core, seq_count * dps, 2)) for core in range(2)]
    scatter = lambda part: lax.psum_scatter(part, group, scatter_dimension=0, tiled=True, axis_index_groups=pairs)
    slopes = slopes.reshape(tokens, -1)
    part_down = weigh(
        [hidt], seeds.reshape(tokens, width), TILE, width // TILE, ((0, width // TILE, ((0, TILE),)),),
        w_down.shape[0], "weigh_down", 3,
    )
    shard_down = scatter(part_down)
    slopes, part_down = lax.optimization_barrier((slopes, part_down))
    part_early = weigh([h2t], slopes, CUT, EARLY, ((0, EARLY, ((0, CUT),)),), share, "weigh_early", 4)
    shard_early = scatter(part_early)
    do_halo, part_early = lax.optimization_barrier((do_halo, part_early))
    def back(first_batch, count, held):
        return attend_back(
            own, lows, highs, qkv, do, do_halo, lse, lse_halo, delta, delta_halo, marks_k, marks_q, cosines, sines,
            first_batch, count, held,
        )

    slopes_qkv = back(0, batch // 2, None)
    slopes_qkv, shard_early, shard_down = lax.optimization_barrier((slopes_qkv, shard_early, shard_down))
    early_sum, down_sum = lax.psum((shard_early, shard_down), "rep")
    slopes_qkv = back(batch // 2, batch - batch // 2, slopes_qkv)
    grad_x, late_sum, grad_qkv = close(
        h2t, mixed_t, h1t, slopes, 2 * FF_PAD, slopes_qkv.reshape(3, tokens, width), qkv_full, x.reshape(tokens, width), dr.reshape(tokens, width),
        gain_one, seq_count, dps, lax.axis_size("rep"),
    )
    grad_qkv = grad_qkv.astype(F32)
    rest_sum = jnp.concatenate([early_sum, late_sum], axis=1).astype(F32)
    grad_in = jnp.concatenate([rest_sum[:, :FF], rest_sum[:, FF_PAD : FF_PAD + FF]], axis=1)
    grad_attn_gain = jnp.sum(grad_qkv * w_qkv.astype(F32), axis=1) / attn_gain.astype(F32)
    grad_mlp_gain = jnp.sum(grad_in * w_in.astype(F32), axis=1) / mlp_gain.astype(F32)
    return (
        result.reshape(cotangent.shape),
        grad_x.reshape(inputs.shape),
        grad_attn_gain,
        grad_mlp_gain,
        grad_qkv,
        rest_sum[:, 2 * FF_PAD : 2 * FF_PAD + width],
        grad_in,
        down_sum[: w_down.shape[0]].astype(F32),
    )


def solution(mesh):
    return jax.shard_map(
        body,
        mesh=mesh,
        in_specs=(
            P(None, ("dp", "rep"), "seq", None),
            P(None, ("dp", "rep"), None),
            P(None, ("dp", "rep"), "seq", None),
            P(("seq", "dp")),
            P(("seq", "dp")),
            P(("seq", "dp"), None),
            P(("seq", "dp"), None),
            P(("seq", "dp"), None),
            P(("seq", "dp"), None),
        ),
        out_specs=(
            P(None, ("dp", "rep"), "seq", None),
            P(None, ("dp", "rep"), "seq", None),
            P(("seq", "dp")),
            P(("seq", "dp")),
            P(("seq", "dp"), None),
            P(("seq", "dp"), None),
            P(("seq", "dp"), None),
            P(("seq", "dp"), None),
        ),
        check_vma=False,
    )
```

```python
import functools

import jax
import jax.numpy as jnp
from jax import lax
from jax.experimental import pallas as pl
from jax.experimental.pallas import tpu as pltpu
from jax.sharding import PartitionSpec as P

HEADS = 16
HEAD_DIM = 64
FF = 2624
HALF = 512
DOCS = 7

EPS = 1e-05
THETA = 10000.0
MASKED = -1e30

TILE = 256
CUT = 512
REACH = HALF // TILE
LANES = 128
FF_PAD = -(-FF // LANES) * LANES
PAIRS = HEADS // 2
WIDE = 4
WIDE_BACK = 2
VMEM = 60 * 1024 * 1024

F32 = jnp.float32
BF16 = jnp.bfloat16

MESH = pl.DeviceIdType.MESH

NN = (((1,), (0,)), ((), ()))
NT = (((1,), (1,)), ((), ()))


def dot(left, right, dims=NN):
    return lax.dot_general(left, right, dims, preferred_element_type=F32)


def params(**more):
    return pltpu.CompilerParams(vmem_limit_bytes=VMEM, **more)


def normed(values):
    centre = values - jnp.mean(values, axis=-1, keepdims=True)
    spread = jnp.mean(centre * centre, axis=-1, keepdims=True)
    inverse = lax.rsqrt(spread + EPS)
    return centre * inverse, inverse


def norm_back(grads, unit, inverse):
    first = jnp.mean(grads, axis=-1, keepdims=True)
    second = jnp.mean(grads * unit, axis=-1, keepdims=True)
    return (grads - first - unit * second) * inverse


def swapped(values):
    lane = lax.broadcasted_iota(jnp.int32, values.shape, 1)
    ahead = pltpu.roll(values, LANES - HEAD_DIM // 2, 1)
    behind = pltpu.roll(values, HEAD_DIM // 2, 1)
    return jnp.where(lane % HEAD_DIM < HEAD_DIM // 2, ahead, behind)


def project_kernel(keep, shards, x_ref, w_ref, cos_ref, sin_ref, *outs):
    qkv_ref = outs[-1]
    width = x_ref.shape[2]
    share = width // shards
    gain = jnp.concatenate(
        [w_ref[share * i : share * i + 1, 3 * width : 3 * width + share] for i in range(shards)], axis=1
    ).astype(F32)
    unit, _ = normed(x_ref[0].astype(F32))
    h1 = (unit * gain).astype(BF16)
    if keep:
        outs[0][...] = h1.T
    cosines, sines = cos_ref[0], sin_ref[0]
    for start in range(0, 3 * width, 512):
        part = dot(h1, w_ref[:, start : start + 512])
        for column in range(0, 512, LANES):
            piece = part[:, column : column + LANES]
            if start < 2 * width:
                piece = piece * cosines + swapped(piece) * sines
            if start < width:
                piece = piece * HEAD_DIM**-0.5
            qkv_ref[0, :, start + column : start + column + LANES] = piece.astype(BF16)


def project(x, weight, cosines, sines, first_tile, held, extent, shards):
    batch, rows, width = x.shape
    steps = rows // TILE
    grid = (batch, steps)
    keep = held is None
    block = lambda b, i: (b, i, 0)
    shifted = lambda b, i: (b, i + first_tile, 0)
    qkv_spec = pl.BlockSpec((1, TILE, 3 * width), shifted)
    qkv_shape = jax.ShapeDtypeStruct((batch, extent, 3 * width), BF16)
    in_specs = [
        pl.BlockSpec((1, TILE, width), block),
        pl.BlockSpec(weight.shape, lambda b, i: (0, 0), pipeline_mode=pl.Buffered(1)),
        pl.BlockSpec((1, TILE, LANES), shifted),
        pl.BlockSpec((1, TILE, LANES), shifted),
    ]
    cost = pl.CostEstimate(
        flops=2 * batch * rows * width * 3 * width,
        bytes_accessed=8 * batch * rows * width + 6 * width * width,
        transcendentals=0,
    )
    if keep:
        return pl.pallas_call(
            functools.partial(project_kernel, True, shards),
            grid=grid,
            in_specs=in_specs,
            out_specs=[pl.BlockSpec((width, TILE), lambda b, i: (0, b * steps + i)), qkv_spec],
            out_shape=[jax.ShapeDtypeStruct((width, batch * rows), BF16), qkv_shape],
            compiler_params=params(),
            cost_estimate=cost,
            name="project_own",
        )(x, weight, cosines, sines)

    def halo_kernel(x_ref, w_ref, cos_ref, sin_ref, held_ref, qkv_ref):
        project_kernel(False, shards, x_ref, w_ref, cos_ref, sin_ref, qkv_ref)

    return pl.pallas_call(
        halo_kernel,
        grid=grid,
        in_specs=in_specs + [pl.BlockSpec(memory_space=pl.ANY)],
        out_specs=qkv_spec,
        out_shape=qkv_shape,
        input_output_aliases={4: 0},
        compiler_params=params(),
        cost_estimate=cost,
        name="project_halo",
    )(x, weight, cosines, sines, held)


def edge_masks():
    key = lax.broadcasted_iota(jnp.int32, (TILE, TILE), 0)
    query = lax.broadcasted_iota(jnp.int32, (TILE, TILE), 1)
    return (
        jnp.where(key >= query, 0.0, MASKED).astype(F32),
        jnp.where(key <= query, 0.0, MASKED).astype(F32),
    )


def edge_of(key_tile, query_tile):
    gap = key_tile - query_tile
    return jnp.where(gap == -REACH, 0, jnp.where(gap == REACH, 2, 1))


def low_half(rows):
    return lax.broadcasted_iota(jnp.int32, (rows, LANES), 1) < HEAD_DIM


def split3(values):
    high = values.astype(BF16).astype(F32)
    rest = values - high
    middle = rest.astype(BF16).astype(F32)
    return high, middle, rest - middle


def attend_kernel(tiles, wide, own_ref, lo_ref, hi_ref, q_ref, k_ref, v_ref, ek_ref, eq_ref, o_ref, ot_ref, lse_ref,
                  kx, qx, vx, edges):
    batch = pl.program_id(0)
    stretch, extent = q_ref.shape[1], k_ref.shape[1]

    @pl.when((batch == 0) & (pl.program_id(1) == 0))
    def _():
        before, after = edge_masks()
        edges[0] = before
        edges[1] = jnp.zeros((TILE, TILE), F32)
        edges[2] = after

    low = low_half(extent)
    marks = ek_ref[0]
    ones = jnp.ones((16, extent), BF16)
    for pair in range(wide):
        span = slice(pair * LANES, (pair + 1) * LANES)
        keys = k_ref[0, :, span]
        kx[2 * pair] = jnp.where(low, keys, marks)
        kx[2 * pair + 1] = jnp.where(low, marks, keys)
        turned = q_ref[0, :, span].T
        qx[2 * pair] = jnp.concatenate([turned[:HEAD_DIM], eq_ref[0]], axis=0)
        qx[2 * pair + 1] = jnp.concatenate([eq_ref[0], turned[HEAD_DIM:]], axis=0)
        flipped = v_ref[0, :, span].T
        vx[2 * pair] = jnp.concatenate([flipped[:HEAD_DIM], ones], axis=0)
        vx[2 * pair + 1] = jnp.concatenate([flipped[HEAD_DIM:], ones], axis=0)
    own = own_ref[0]

    def one_tile(index, carry):
        query_tile = own + index
        first, last = lo_ref[batch, query_tile], hi_ref[batch, query_tile]
        columns = pl.ds(pl.multiple_of(index * TILE, TILE), TILE)

        def some(count):
            places, masks = [], []
            for step in range(count):
                key_tile = first + step
                places.append(pl.multiple_of(lax.rem(key_tile - own + tiles, tiles) * TILE, TILE))
                masks.append(edge_of(key_tile, query_tile))

            def score(head):
                return [
                    dot(kx[head, pl.ds(place, TILE), :], qx[head, :, columns]) + edges[mask]
                    for place, mask in zip(places, masks)
                ]

            heads = 2 * wide
            scores = {head: score(head) for head in range(min(1, heads))}
            mixed, waiting = [], []

            def close_head(head, top, powers):
                sums = dot(
                    jnp.concatenate([vx[head, :, pl.ds(place, TILE)] for place in places], axis=1),
                    jnp.concatenate(powers, axis=0),
                )
                total = sums[HEAD_DIM : HEAD_DIM + 1]
                mixed.append(sums[:HEAD_DIM] * (1.0 / total))
                lse_ref[0, head // 2, head % 2 : head % 2 + 1, columns] = top + jnp.log(total)
                if head % 2 == 1:
                    both = jnp.concatenate(mixed[-2:], axis=0)
                    span = slice(head // 2 * LANES, (head // 2 + 1) * LANES)
                    ot_ref[span, columns] = both.astype(BF16)
                    o_ref[0, columns, span] = both.T.astype(BF16)

            for head in range(heads):
                if head + 1 < heads:
                    scores[head + 1] = score(head + 1)
                parts = scores.pop(head)
                top = parts[0]
                for part in parts[1:]:
                    top = jnp.maximum(top, part)
                top = jnp.max(top, axis=0, keepdims=True)
                powers = [jnp.exp(part - top).astype(BF16) for part in parts]
                waiting.append((head, top, powers))
                if len(waiting) > 1:
                    close_head(*waiting.pop(0))
            for item in waiting:
                close_head(*item)

        for count in range(1, 2 * REACH + 2):
            pl.when(last - first == count)(functools.partial(some, count))
        return carry

    lax.fori_loop(0, stretch // TILE, one_tile, 0)


def attend(own, lows, highs, qkv, marks_k, marks_q, stretch):
    batch, extent, _ = qkv.shape
    tiles = extent // TILE
    width = PAIRS * LANES
    wide = WIDE
    groups = PAIRS // wide
    spec = lambda rows, offset: pl.BlockSpec((1, rows, wide * LANES), lambda b, p, *_: (b, 0, p + offset))
    per = pl.BlockSpec((1, extent, LANES), lambda b, p, *_: (b, 0, 0))
    return pl.pallas_call(
        functools.partial(attend_kernel, tiles, wide),
        grid_spec=pltpu.PrefetchScalarGridSpec(
            num_scalar_prefetch=3,
            grid=(batch, groups),
            in_specs=[
                spec(stretch, 0),
                spec(extent, groups),
                spec(extent, 2 * groups),
                per,
                pl.BlockSpec((1, HEAD_DIM, stretch), lambda b, p, *_: (b, 0, 0)),
            ],
            out_specs=[
                spec(stretch, 0),
                pl.BlockSpec((wide * LANES, stretch), lambda b, p, *_: (p, b)),
                pl.BlockSpec((1, wide, 2, stretch), lambda b, p, *_: (b, p, 0, 0)),
            ],
            scratch_shapes=[
                pltpu.VMEM((2 * wide, extent, LANES), BF16),
                pltpu.VMEM((2 * wide, LANES, stretch), BF16),
                pltpu.VMEM((2 * wide, HEAD_DIM + 16, extent), BF16),
                pltpu.VMEM((3, TILE, TILE), F32),
            ],
        ),
        out_shape=[
            jax.ShapeDtypeStruct((batch, stretch, width), BF16),
            jax.ShapeDtypeStruct((width, batch * stretch), BF16),
            jax.ShapeDtypeStruct((batch, PAIRS, 2, stretch), F32),
        ],
        compiler_params=params(),
        cost_estimate=pl.CostEstimate(
            flops=2 * 2 * HEADS * batch * stretch * extent * 128, bytes_accessed=32 * 1024 * 1024, transcendentals=0
        ),
        name="attend",
    )(own, lows, highs, qkv, qkv, qkv, marks_k, marks_q)


def attend_back_kernel(tiles, wide, first_batch, own_ref, lo_ref, hi_ref, q_ref, k_ref, v_ref, do_ref, doh_ref, lse_ref, lseh_ref,
                       delta_ref, deltah_ref, ek_ref, eq_ref, cos_ref, sin_ref, *refs):
    out_ref, kx, vx, qx, dx, dn, kt, dqt, edges = refs[-9:]
    batch = pl.program_id(0) + first_batch
    extent = k_ref.shape[1]
    stretch = do_ref.shape[1]
    mine = stretch // TILE
    heads = 2 * wide

    @pl.when((pl.program_id(0) == 0) & (pl.program_id(1) == 0))
    def _():
        before, after = edge_masks()
        edges[0] = before
        edges[1] = jnp.zeros((TILE, TILE), F32)
        edges[2] = after

    low = low_half(extent)
    marks = ek_ref[0]
    lane = lax.broadcasted_iota(jnp.int32, (extent, LANES), 1) % HEAD_DIM
    units = jnp.where((lane >= 8) & (lane < 11), 1.0, 0.0).astype(BF16)
    row = lax.broadcasted_iota(jnp.int32, (HEAD_DIM, extent), 0)
    label_rows = eq_ref[0].astype(F32)
    dn[:stretch] = do_ref[0]
    dn[stretch:] = doh_ref[0]
    for pair in range(wide):
        span = slice(pair * LANES, (pair + 1) * LANES)
        keys, values = k_ref[0, :, span], v_ref[0, :, span]
        kx[2 * pair] = jnp.where(low, keys, marks)
        kx[2 * pair + 1] = jnp.where(low, marks, keys)
        kt[span] = keys.T
        vx[2 * pair] = jnp.where(low, values, units)
        vx[2 * pair + 1] = jnp.where(low, units, values)
        turned, flipped = q_ref[0, :, span].T, dn[:, span].T
        lses = jnp.concatenate([lse_ref[0, pair], lseh_ref[0, pair]], axis=1)
        deltas = jnp.concatenate([delta_ref[0, pair], deltah_ref[0, pair]], axis=1)
        for half in range(2):
            lse = split3(lses[half : half + 1])
            delta = split3(deltas[half : half + 1])
            mark, shift = label_rows, jnp.zeros((HEAD_DIM, extent), F32)
            for place in range(3):
                mark = jnp.where(row == 8 + place, -lse[place], mark)
                shift = jnp.where(row == 8 + place, -delta[place], shift)
            mark, shift = mark.astype(BF16), shift.astype(BF16)
            rows = slice(half * HEAD_DIM, (half + 1) * HEAD_DIM)
            order = (lambda a, b: [a, b]) if half == 0 else (lambda a, b: [b, a])
            qx[2 * pair + half] = jnp.concatenate(order(turned[rows], mark), axis=0)
            dx[2 * pair + half] = jnp.concatenate(order(flipped[rows], shift), axis=0)

    own = own_ref[0]
    dqt[...] = jnp.zeros_like(dqt)
    low_tile = low_half(TILE)

    def place(tile):
        return pl.ds(pl.multiple_of(lax.rem(tile - own + tiles, tiles) * TILE, TILE), TILE)

    def some(key_tile, begin, count, key_grad, out_rows):
        rows = place(key_tile)
        columns = [place(begin + step) for step in range(count)]
        masks = [edge_of(key_tile, begin + step) for step in range(count)]
        items = [(head, step) for head in range(heads) for step in range(count)]
        powers, slopes, sums = {}, {}, {}

        def first_products(head, step):
            score = dot(kx[head, rows, :], qx[head, :, columns[step]]) + edges[masks[step]]
            return score, dot(vx[head, rows, :], dx[head, :, columns[step]])

        def last_products(head, step):
            span = slice(head * HEAD_DIM, (head + 1) * HEAD_DIM)
            dqt[span, columns[step]] += dot(kt[span, rows], slopes[head][step])
            if not key_grad or step + 1 < count:
                return
            pair = slice(head // 2 * LANES, (head // 2 + 1) * LANES)
            grads = jnp.concatenate([dn[column, pair] for column in columns], axis=0)
            queries = jnp.concatenate([q_ref[0, column, pair] for column in columns], axis=0)
            sums[head] = (
                dot(jnp.concatenate(slopes.pop(head), axis=1), queries),
                dot(jnp.concatenate(powers.pop(head), axis=1), grads),
            )
            if head % 2 == 1:
                key_sum, value_sum = (jnp.where(low_tile, a, b) for a, b in zip(sums[head - 1], sums[head]))
                cosines, sines = cos_ref[0, out_rows, :], sin_ref[0, out_rows, :]
                out_ref[1, 0, out_rows, pair] = (key_sum * cosines - swapped(key_sum) * sines).astype(BF16)
                out_ref[2, 0, out_rows, pair] = value_sum.astype(BF16)

        ahead = [first_products(*items[0])]
        for index, (head, step) in enumerate(items):
            if index + 1 < len(items):
                ahead.append(first_products(*items[index + 1]))
            score, slope = ahead.pop(0)
            power = jnp.exp(score)
            powers.setdefault(head, []).append(power.astype(BF16))
            slopes.setdefault(head, []).append((power * slope).astype(BF16))
            if index >= 1:
                last_products(*items[index - 1])
        last_products(*items[-1])

    def own_keys(index, carry):
        key_tile = own + index
        first, last = lo_ref[batch, key_tile], hi_ref[batch, key_tile]
        out_rows = pl.ds(pl.multiple_of(index * TILE, TILE), TILE)
        for count in range(1, 2 * REACH + 2):
            pl.when(last - first == count)(functools.partial(some, key_tile, first, count, True, out_rows))
        return carry

    lax.fori_loop(0, mine, own_keys, 0)

    def other_keys(mem, carry):
        ahead = own + mem
        key_tile = jnp.where(ahead < own + mine + REACH, ahead, ahead - tiles)
        if tiles == mine + REACH:
            key_tile = jnp.where(own == 0, ahead, ahead - tiles)
        valid = (key_tile >= 0) & (key_tile < lo_ref.shape[1])
        safe = jnp.where(valid, key_tile, 0)
        begin = jnp.maximum(lo_ref[batch, safe], own)
        end = jnp.where(valid, jnp.minimum(hi_ref[batch, safe], own + mine), begin)
        for count in range(1, min(REACH, mine) + 1):
            pl.when(end - begin == count)(functools.partial(some, safe, begin, count, False, None))
        return carry

    lax.fori_loop(mine, tiles, other_keys, 0)
    for pair in range(wide):
        span = slice(pair * LANES, (pair + 1) * LANES)
        raw = dqt[span, :stretch].T * HEAD_DIM**-0.5
        out_ref[0, 0, :, span] = (raw * cos_ref[0] - swapped(raw) * sin_ref[0]).astype(BF16)


def attend_back(own, lows, highs, qkv, grads, grads_halo, lse, lse_halo, delta, delta_halo, marks_k, marks_q,
                cosines, sines, first_batch, count, held):
    batch, extent, _ = qkv.shape
    stretch, width = grads.shape[1:]
    halo = extent - stretch
    tiles = extent // TILE
    wide = WIDE_BACK
    groups = PAIRS // wide
    spec = lambda rows, offset: pl.BlockSpec((1, rows, wide * LANES), lambda b, p, *_: (b + first_batch, 0, p + offset))
    per = lambda rows: pl.BlockSpec((1, rows, LANES), lambda b, p, *_: (b + first_batch, 0, 0))
    numbers = lambda rows: pl.BlockSpec((1, wide, 2, rows), lambda b, p, *_: (b + first_batch, p, 0, 0))
    return pl.pallas_call(
        functools.partial(attend_back_kernel, tiles, wide, first_batch),
        grid_spec=pltpu.PrefetchScalarGridSpec(
            num_scalar_prefetch=3,
            grid=(count, groups),
            in_specs=[
                spec(extent, 0),
                spec(extent, groups),
                spec(extent, 2 * groups),
                spec(stretch, 0),
                spec(halo, 0),
                numbers(stretch),
                numbers(halo),
                numbers(stretch),
                numbers(halo),
                per(extent),
                pl.BlockSpec((1, HEAD_DIM, extent), lambda b, p, *_: (b + first_batch, 0, 0)),
                per(stretch),
                per(stretch),
            ]
            + ([] if held is None else [pl.BlockSpec(memory_space=pl.ANY)]),
            out_specs=pl.BlockSpec((3, 1, stretch, wide * LANES), lambda b, p, *_: (0, b + first_batch, 0, p)),
            scratch_shapes=[
                pltpu.VMEM((2 * wide, extent, LANES), BF16),
                pltpu.VMEM((2 * wide, extent, LANES), BF16),
                pltpu.VMEM((2 * wide, LANES, extent), BF16),
                pltpu.VMEM((2 * wide, LANES, extent), BF16),
                pltpu.VMEM((extent, wide * LANES), BF16),
                pltpu.VMEM((wide * LANES, extent), BF16),
                pltpu.VMEM((wide * LANES, extent), F32),
                pltpu.VMEM((3, TILE, TILE), F32),
            ],
        ),
        input_output_aliases={} if held is None else {16: 0},
        out_shape=jax.ShapeDtypeStruct((3, batch, stretch, width), BF16),
        compiler_params=params(),
        cost_estimate=pl.CostEstimate(
            flops=5 * 2 * HEADS * count * stretch * extent * 128, bytes_accessed=64 * 1024 * 1024, transcendentals=0
        ),
        name="attend_back",
    )(own, lows, highs, qkv, qkv, qkv, grads, grads_halo, lse, lse_halo, delta, delta_halo, marks_k, marks_q,
      cosines, sines, *([] if held is None else [held]))


def feed_kernel(seqs, halo_tiles, x_ref, o_ref, g_ref, gain_ref, w_ref, wd_ref,
                out_ref, h2t_ref, hidt_ref, slopes_ref, dr_ref, do_ref, delta_ref, do_halo, delta_halo,
                do_sent, delta_sent, send_sem, recv_sem):
    batch, steps = pl.num_programs(1), pl.num_programs(0)
    step, sequence = pl.program_id(0), pl.program_id(1)
    seq = lax.axis_index("seq")
    mine, tiles = steps, steps + halo_tiles
    reach = -(-REACH // mine)
    hops = [hop for hop in range(-reach, reach + 1) if hop != 0]

    def exists(hop):
        return (seq + hop >= 0) & (seq + hop < seqs)

    def sent(which, tile, hop):
        peer = seq + hop
        place = seq * mine + tile
        wanted = exists(hop) & (place >= peer * mine - REACH) & (place < (peer + 1) * mine + REACH)
        slot = lax.rem(place - peer * mine + tiles, tiles) - mine
        slot = jnp.where(wanted, slot, 0)
        return wanted, halo_copies(which, tile, slot, hops.index(hop), peer)

    def halo_copies(which, tile, slot, hop, peer):
        span = pl.ds(pl.multiple_of(slot * TILE, TILE), TILE)
        pieces = [
            (do_sent.at[which, tile], do_halo.at[which, span]),
            (delta_sent.at[which, tile], delta_halo.at[which, :, :, span]),
        ]
        return [
            pltpu.make_async_remote_copy(
                src_ref=source, dst_ref=target, send_sem=send_sem.at[kind, which, tile, hop],
                recv_sem=recv_sem.at[kind, which, slot], device_id={"seq": peer}, device_id_type=MESH,
            )
            for kind, (source, target) in enumerate(pieces)
        ]

    @pl.when((step == 0) & (sequence == 0))
    def _():
        barrier = pltpu.get_barrier_semaphore()
        for hop in hops:
            @pl.when(exists(hop))
            def _():
                pl.semaphore_signal(barrier, inc=1, device_id={"seq": seq + hop}, device_id_type=MESH)

        for hop in hops:
            @pl.when(exists(hop))
            def _():
                pl.semaphore_wait(barrier, 1)

    mixed = o_ref[0]
    seeds = g_ref[0]
    gain = gain_ref[...]
    width = mixed.shape[1]
    w_out = slice(2 * FF_PAD, 2 * FF_PAD + width)
    r1 = x_ref[0].astype(F32) + dot(mixed, w_ref[:, w_out])
    unit, inverse = normed(r1)
    h2 = (unit * gain).astype(BF16)
    h2t_ref[...] = h2.T
    total = r1
    back = jnp.zeros_like(r1)
    edges = list(range(0, FF - 511, 512))
    for start, stop in zip(edges, edges[1:] + [FF]):
        gates, ups = slice(start, stop), slice(FF_PAD + start, FF_PAD + stop)
        gate = dot(h2, w_ref[:, gates])
        up = dot(h2, w_ref[:, ups])
        grad = dot(seeds, wd_ref[start:stop, :], NT)
        phi = 0.5 + 0.5 * lax.erf(gate * (0.5**0.5))
        bell = jnp.exp(gate * gate * -0.5) * 0.3989422804014327
        act = gate * phi
        hid = (act * up).astype(BF16)
        grad_gate = (grad * up * (phi + gate * bell)).astype(BF16)
        grad_up = (grad * act).astype(BF16)
        hidt_ref[start:stop, :] = hid.T
        slopes_ref[0, :, gates] = grad_gate
        slopes_ref[0, :, ups] = grad_up
        total = total + dot(hid, wd_ref[start:stop, :])
        back = back + dot(grad_gate, w_ref[:, gates], NT) + dot(grad_up, w_ref[:, ups], NT)
    blank = jnp.zeros((TILE, FF_PAD - FF), BF16)
    slopes_ref[0, :, 2 * FF_PAD + width :] = jnp.zeros((TILE, slopes_ref.shape[2] - 2 * FF_PAD - width), BF16)
    slopes_ref[0, :, FF:FF_PAD] = blank
    slopes_ref[0, :, FF_PAD + FF : 2 * FF_PAD] = blank
    out_ref[0] = total.astype(BF16)
    dr = seeds.astype(F32) + norm_back(back * gain, unit, inverse)
    dr_ref[0] = dr
    da = dr.astype(BF16)
    slopes_ref[0, :, w_out] = da
    do = dot(da, w_ref[:, w_out], NT).astype(BF16)
    do_ref[0] = do
    product = do.astype(F32) * mixed.astype(F32)
    high = product.astype(BF16)
    rest = (product - high.astype(F32)).astype(BF16)
    head = lax.broadcasted_iota(jnp.int32, (HEADS, width), 0)
    column = lax.broadcasted_iota(jnp.int32, (HEADS, width), 1)
    pick = jnp.where(column // HEAD_DIM == head, 1.0, 0.0).astype(BF16)
    delta = dot(pick, high, NT) + dot(pick, rest, NT)
    tile = facing_first(step, steps, seqs)
    do_sent[sequence, tile] = do
    for pair in range(PAIRS):
        delta_ref[0, pair] = delta[2 * pair : 2 * pair + 2]
        delta_sent[sequence, tile, pair] = delta[2 * pair : 2 * pair + 2]
    for hop in hops:
        wanted, copies = sent(sequence, tile, hop)

        @pl.when(wanted)
        def _():
            for copy in copies:
                copy.start()

    @pl.when((step == steps - 1) & (sequence == batch - 1))
    def _():
        def settle(index, carry):
            which, tile = index // mine, lax.rem(index, mine)
            for hop in hops:
                wanted, copies = sent(which, tile, hop)

                @pl.when(wanted)
                def _():
                    for copy in copies:
                        copy.wait_send()

            return carry

        lax.fori_loop(0, batch * mine, settle, 0)

        def arrive(index, carry):
            which, slot = index // halo_tiles, lax.rem(index, halo_tiles)
            place = seq * mine + mine + slot
            if halo_tiles == REACH:
                place = jnp.where(seq == 0, place, place - tiles)
            else:
                place = jnp.where(slot < REACH, place, place - tiles)

            @pl.when((place >= 0) & (place < seqs * mine))
            def _():
                for copy in halo_copies(which, 0, slot, 0, seq):
                    copy.wait_recv()

            return carry

        lax.fori_loop(0, batch * halo_tiles, arrive, 0)


def facing_first(step, steps, seqs):
    if seqs != 2:
        return step
    return lax.rem(step + (1 - lax.axis_index("seq")) * (steps // 2), steps)


def feed(x, mixed, seeds, gain, w_rest, w_down, seqs, halo):
    batch, rows, width = x.shape
    steps = rows // TILE
    place = lambda i: facing_first(i, steps, seqs)
    block = lambda n: pl.BlockSpec((1, TILE, n), lambda i, b: (b, place(i), 0))
    turned = lambda n: pl.BlockSpec((n, TILE), lambda i, b: (0, b * steps + place(i)))
    fixed = lambda m, n: pl.BlockSpec((m, n), lambda i, b: (0, 0), pipeline_mode=pl.Buffered(1))
    shape = lambda n, t: jax.ShapeDtypeStruct((batch, rows, n), t)
    columns = w_rest.shape[1]
    padded = -(-columns // CUT) * CUT
    reach = -(-REACH // steps)
    return pl.pallas_call(
        functools.partial(feed_kernel, seqs, halo // TILE),
        grid=(steps, batch),
        in_specs=[
            block(width), block(width), block(width), fixed(1, width), fixed(width, columns), fixed(FF, width),
        ],
        out_specs=[
            block(width), turned(width), turned(FF), block(padded), block(width), block(width),
            pl.BlockSpec((1, PAIRS, 2, TILE), lambda i, b: (b, 0, 0, place(i))),
            pl.BlockSpec(memory_space=pl.ANY),
            pl.BlockSpec(memory_space=pl.ANY),
        ],
        out_shape=[
            shape(width, BF16),
            jax.ShapeDtypeStruct((width, batch * rows), BF16),
            jax.ShapeDtypeStruct((FF, batch * rows), BF16),
            shape(padded, BF16),
            shape(width, F32),
            shape(width, BF16),
            jax.ShapeDtypeStruct((batch, PAIRS, 2, rows), F32),
            jax.ShapeDtypeStruct((batch, halo, width), BF16),
            jax.ShapeDtypeStruct((batch, PAIRS, 2, halo), F32),
        ],
        scratch_shapes=[
            pltpu.VMEM((batch, steps, TILE, width), BF16),
            pltpu.VMEM((batch, steps, PAIRS, 2, TILE), F32),
            pltpu.SemaphoreType.DMA((2, batch, steps, 2 * reach)),
            pltpu.SemaphoreType.DMA((2, batch, halo // TILE)),
        ],
        compiler_params=params(collective_id=2, has_side_effects=True),
        cost_estimate=pl.CostEstimate(
            flops=2 * batch * rows * width * (6 * FF + 2 * width), bytes_accessed=64 * 1024 * 1024, transcendentals=0
        ),
        name="feed",
    )(x, mixed, seeds, gain, w_rest, w_down)


def weigh_kernel(blocks, share, held, turns, *refs):
    lefts, (right_ref, out_ref, prod, kept, sent, got, send_sem, recv_sem) = refs[:-8], refs[-8:]
    step = pl.program_id(0)
    dp = lax.axis_index("dp")
    core = lax.rem(dp, 2)
    mate = dp + 1 - 2 * core
    places = prod.shape[0] // (2 * share)

    def to_mate(n):
        return pltpu.make_async_remote_copy(
            src_ref=sent.at[n], dst_ref=got.at[n], send_sem=send_sem.at[n], recv_sem=recv_sem.at[n],
            device_id={"dp": mate}, device_id_type=MESH,
        )

    @pl.when(step == 0)
    def _():
        barrier = pltpu.get_barrier_semaphore()
        pl.semaphore_signal(barrier, inc=1, device_id={"dp": mate}, device_id_type=MESH)
        pl.semaphore_wait(barrier, 1)

    columns = right_ref.shape[1]
    for first, last, pieces in turns:

        @pl.when((step >= first) & (step < last))
        def _():
            start = 0
            for which, count in pieces:
                span = slice(start, start + count)
                prod[:, span] = dot(lefts[which][...], right_ref[:, span])
                start += count

    @pl.when(step < blocks)
    def _():
        for place in range(places):
            even = prod[2 * place * share : (2 * place + 1) * share, :]
            odd = prod[(2 * place + 1) * share : (2 * place + 2) * share, :]
            rows = slice(place * held, place * held + share)
            sent[step, rows, :] = jnp.where(core == 0, odd, even).astype(BF16)
            kept[step % 2, rows, :] = jnp.where(core == 0, even, odd)
            if held > share:
                rows = slice(place * held + share, (place + 1) * held)
                sent[step, rows, :] = jnp.zeros((held - share, columns), BF16)
                kept[step % 2, rows, :] = jnp.zeros((held - share, columns), F32)
        to_mate(step).start()

    @pl.when(step >= 1)
    def _():
        done = step - 1
        to_mate(done).wait()
        out_ref[...] = (kept[done % 2] + got[done].astype(F32)).astype(BF16)


def weigh(lefts, right, columns, blocks, turns, share, name, number):
    rows, tokens = lefts[0].shape
    total = blocks * columns
    held = -(-share // 16) * 16
    places = rows // (2 * share)
    fixed = pl.BlockSpec((rows, tokens), lambda n: (0, 0), pipeline_mode=pl.Buffered(1))
    return pl.pallas_call(
        functools.partial(weigh_kernel, blocks, share, held, turns),
        grid=(blocks + 1,),
        in_specs=[fixed] * len(lefts) + [pl.BlockSpec((tokens, columns), lambda n: (0, jnp.minimum(n, blocks - 1)))],
        out_specs=pl.BlockSpec((places * held, columns), lambda n: (0, jnp.maximum(n - 1, 0))),
        out_shape=jax.ShapeDtypeStruct((places * held, total), BF16),
        scratch_shapes=[
            pltpu.VMEM((rows, columns), F32),
            pltpu.VMEM((2, places * held, columns), F32),
            pltpu.VMEM((blocks, places * held, columns), BF16),
            pltpu.VMEM((blocks, places * held, columns), BF16),
            pltpu.SemaphoreType.DMA((blocks,)),
            pltpu.SemaphoreType.DMA((blocks,)),
        ],
        compiler_params=params(collective_id=number, has_side_effects=True),
        cost_estimate=pl.CostEstimate(
            flops=2 * rows * tokens * total, bytes_accessed=24 * 1024 * 1024, transcendentals=0
        ),
        name=name,
    )(*lefts, right)


LAGS = (1, 3, 5, 6, 7, 8)
RING, RING_XY, RING_LINE = 5, 2, 4
EARLY, DOWN_BLOCKS, LINE_LAG = 8, 4, 2


def close_kernel(blocks, rest_blocks, rest_edge, seqs, reps, h2t_ref, ot_ref, h1t_ref, rest_ref, right_ref, three_ref, w_ref, x_ref, dr_ref, gain_ref, down_ref,
                 gi_ref, rest_sum, sum_ref, down_sum,
                 prod, kept0, kept1x, kept1y, kept2, s0, r0, s1x, r1x, s1y, r1y, s2x, r2x, s2y, r2y,
                 mine, ends, others, down_ends, down_others, send_sem, recv_sem, line_sem):
    step = pl.program_id(0)
    width = h1t_ref.shape[0]
    share = mine.shape[1]
    seq, dp, rep = lax.axis_index("seq"), lax.axis_index("dp"), lax.axis_index("rep")
    core, side = lax.rem(dp, 2), dp // 2
    mate, across = dp + 1 - 2 * core, lax.rem(dp + 2, 4)
    seq_peers = [lax.rem(seq + hop, seqs) for hop in range(1, seqs)]
    inner = (rep == 1) | (rep == 2)
    beside = rep + 1 - 2 * lax.rem(rep, 2)
    slot_seq, slot_side, slot_in = 1, seqs, seqs + 1

    def copy(source, target, n, slot, device):
        turn = lax.rem(n, 2 * RING_XY)
        return pltpu.make_async_remote_copy(
            src_ref=source, dst_ref=target, send_sem=send_sem.at[turn, slot], recv_sem=recv_sem.at[turn, slot],
            device_id=device, device_id_type=MESH,
        )

    def rows(first, count):
        return pl.ds(pl.multiple_of(first * share, share), count * share)

    def half(n):
        return lax.rem(n // 2, RING_XY)

    def to_mate(n):
        slot = lax.rem(n, RING)
        return [copy(s0.at[slot], r0.at[slot], n, 0, {"dp": mate})]

    def to_seq(n, source, target):
        return [
            copy(source.at[half(n), hop], target.at[half(n), hop], n, slot_seq + hop, {"seq": peer})
            for hop, peer in enumerate(seq_peers)
        ]

    def to_side(n, source, target):
        return [copy(source.at[half(n)], target.at[half(n)], n, slot_side, {"dp": across})]

    def line(which, source, first, second, sends, arrivals):
        start, target, device = (
            (source, first, beside), (first, second, reps - 1 - rep), (second, second, beside),
        )[which]
        return pltpu.make_async_remote_copy(
            src_ref=start, dst_ref=target, send_sem=sends, recv_sem=arrivals,
            device_id={"rep": device}, device_id_type=MESH,
        )

    def own_line(n, which):
        slot, turn = slot_in + which, lax.rem(n, RING_LINE)
        return line(which, mine.at[turn], ends.at[turn], others.at[turn], send_sem.at[turn, slot], recv_sem.at[turn, slot])

    down_columns = down_ends.shape[2]
    extra = []
    for k in range(down_ends.shape[0]):
        extra.append((down_ref, down_ends, down_others, down_sum, k, slice(k * down_columns, (k + 1) * down_columns)))

    def extra_line(index, which):
        source, first, second, _, k, columns = extra[index]
        return line(
            which, source.at[:, columns], first.at[k], second.at[k],
            line_sem.at[0, index, which], line_sem.at[1, index, which],
        )

    def start(copies):
        for each in copies:
            each.start()

    def wait(copies):
        for each in copies:
            each.wait()

    @pl.when(step == 0)
    def _():
        barrier = pltpu.get_barrier_semaphore()
        partners = [{"dp": mate}, {"dp": across}]
        partners += [{"seq": peer} for peer in seq_peers] + [{"rep": beside}]
        for partner in partners:
            pl.semaphore_signal(barrier, inc=1, device_id=partner, device_id_type=MESH)

        @pl.when(inner)
        def _():
            pl.semaphore_signal(barrier, inc=1, device_id={"rep": reps - 1 - rep}, device_id_type=MESH)
            pl.semaphore_wait(barrier, len(partners) + 1)

        @pl.when(jnp.logical_not(inner))
        def _():
            pl.semaphore_wait(barrier, len(partners))

    for index in range(len(extra)):
        @pl.when((step == index) & jnp.logical_not(inner))
        def _():
            extra_line(index, 0).start()

    whole_blocks, split = rest_edge // CUT, rest_edge % CUT

    @pl.when(step < whole_blocks)
    def _():
        prod[...] = dot(h2t_ref[...], rest_ref[...])

    @pl.when((step >= whole_blocks) & (step < rest_blocks))
    def _():
        if split:
            @pl.when(step == whole_blocks)
            def _():
                prod[:, :split] = dot(h2t_ref[...], rest_ref[:, :split])
                prod[:, split:] = dot(ot_ref[...], rest_ref[:, split:])

        @pl.when(step >= whole_blocks + (split > 0))
        def _():
            prod[...] = dot(ot_ref[...], rest_ref[...])

    @pl.when((step >= rest_blocks) & (step < blocks))
    def _():
        prod[...] = dot(h1t_ref[...], right_ref[0])

    @pl.when(step < blocks)
    def _():
        for place in range(2 * seqs):
            span = slice(place * share, (place + 1) * share)
            s0[lax.rem(step, RING), span, :] = prod[rows(2 * place + 1 - core, 1), :].astype(BF16)
        start(to_mate(step))
        for place in range(2 * seqs):
            span = slice(place * share, (place + 1) * share)
            kept0[step % 2, span, :] = prod[rows(2 * place + core, 1), :]

    @pl.when((step >= blocks) & (step < blocks + gi_steps(three_ref, right_ref)))
    def _():
        back = None
        for part in range(3):
            term = dot(three_ref[part], w_ref[:, part * width : (part + 1) * width], NT)
            back = term if back is None else back + term
        unit, inverse = normed(x_ref[...].astype(F32))
        gi_ref[...] = dr_ref[...] + norm_back(back * gain_ref[...], unit, inverse)

    for index, (source, first, second, total, k, columns) in enumerate(extra):
        meet, share_out, close_out = (index + LINE_LAG * hop for hop in (1, 2, 3))

        @pl.when((step == meet) & inner)
        def _():
            extra_line(index, 0).wait_recv()
            first[k] = (source[:, columns].astype(F32) + first[k].astype(F32)).astype(BF16)
            extra_line(index, 1).start()

        @pl.when((step == share_out) & inner)
        def _():
            extra_line(index, 1).wait()
            second[k] = (first[k].astype(F32) + second[k].astype(F32)).astype(BF16)
            extra_line(index, 2).start()

        @pl.when(step == close_out)
        def _():
            @pl.when(inner)
            def _():
                extra_line(index, 2).wait_send()

            @pl.when(jnp.logical_not(inner))
            def _():
                extra_line(index, 0).wait_send()
                extra_line(index, 2).wait_recv()

            total[:, columns] = second[k]

    n6 = step - LAGS[5]

    @pl.when((n6 >= 0) & (n6 < blocks))
    def _():
        @pl.when(inner)
        def _():
            own_line(n6, 2).wait_send()

        @pl.when(jnp.logical_not(inner))
        def _():
            own_line(n6, 2).wait_recv()

        total = others[lax.rem(n6, RING_LINE)]

        @pl.when(n6 < rest_blocks)
        def _():
            rest_sum[:, pl.ds(pl.multiple_of(n6 * CUT, CUT), CUT)] = total

        @pl.when(n6 >= rest_blocks)
        def _():
            sum_ref[:, pl.ds(pl.multiple_of((n6 - rest_blocks) * CUT, CUT), CUT)] = total

    n5 = step - LAGS[4]

    @pl.when((n5 >= 0) & (n5 < blocks) & inner)
    def _():
        own_line(n5, 1).wait()
        others[lax.rem(n5, RING_LINE)] = (ends[lax.rem(n5, RING_LINE)].astype(F32) + others[lax.rem(n5, RING_LINE)].astype(F32)).astype(BF16)
        own_line(n5, 2).start()

    n4 = step - LAGS[3]

    @pl.when((n4 >= 0) & (n4 < blocks) & inner)
    def _():
        own_line(n4, 0).wait_recv()
        ends[lax.rem(n4, RING_LINE)] = (mine[lax.rem(n4, RING_LINE)].astype(F32) + ends[lax.rem(n4, RING_LINE)].astype(F32)).astype(BF16)
        own_line(n4, 1).start()

    @pl.when((n4 >= 0) & (n4 < blocks) & jnp.logical_not(inner))
    def _():
        own_line(n4, 0).wait_send()

    n3 = step - LAGS[2]

    @pl.when((n3 >= 0) & (n3 < blocks))
    def _():
        total = kept2[n3 % 2]

        @pl.when(n3 % 2 == 0)
        def _():
            wait(to_side(n3, s2y, r2y))
            mine[lax.rem(n3, RING_LINE)] = (total + r2y[half(n3)].astype(F32)).astype(BF16)

        @pl.when(n3 % 2 == 1)
        def _():
            wait(to_seq(n3, s2x, r2x))
            added = total
            for hop in range(seqs - 1):
                added = added + r2x[half(n3), hop].astype(F32)
            mine[lax.rem(n3, RING_LINE)] = added.astype(BF16)

        @pl.when(jnp.logical_not(inner))
        def _():
            own_line(n3, 0).start()

    n2 = step - LAGS[1]

    @pl.when((n2 >= 0) & (n2 < blocks) & (n2 % 2 == 0))
    def _():
        wait(to_seq(n2, s1x, r1x))
        total = kept1x[...]
        for hop in range(seqs - 1):
            total = total + r1x[half(n2), hop].astype(F32)
        kept1x[...] = total
        s2y[half(n2)] = kept1x[rows(1 - side, 1), :].astype(BF16)
        start(to_side(n2, s2y, r2y))
        kept2[0] = kept1x[rows(side, 1), :]

    @pl.when((n2 >= 0) & (n2 < blocks) & (n2 % 2 == 1))
    def _():
        wait(to_side(n2, s1y, r1y))
        kept1y[...] = kept1y[...] + r1y[half(n2)].astype(F32)
        for hop, peer in enumerate(seq_peers):
            s2x[half(n2), hop] = kept1y[rows(peer, 1), :].astype(BF16)
        start(to_seq(n2, s2x, r2x))
        kept2[1] = kept1y[rows(seq, 1), :]

    n1 = step - LAGS[0]

    @pl.when((n1 >= 0) & (n1 < blocks))
    def _():
        wait(to_mate(n1))
        held = n1 % 2
        kept0[held] = kept0[held] + r0[lax.rem(n1, RING)].astype(F32)

        @pl.when(n1 % 2 == 0)
        def _():
            for hop, peer in enumerate(seq_peers):
                s1x[half(n1), hop] = kept0[held, rows(2 * peer, 2), :].astype(BF16)
            start(to_seq(n1, s1x, r1x))
            kept1x[...] = kept0[held, rows(2 * seq, 2), :]

        @pl.when(n1 % 2 == 1)
        def _():
            for place in range(seqs):
                s1y[half(n1), place * share : (place + 1) * share, :] = kept0[held, rows(2 * place + 1 - side, 1), :].astype(BF16)
            start(to_side(n1, s1y, r1y))
            for place in range(seqs):
                kept1y[place * share : (place + 1) * share, :] = kept0[held, rows(2 * place + side, 1), :]


def gi_steps(three_ref, right_ref):
    return right_ref.shape[1] // three_ref.shape[1]


def close(h2t, mixed_t, h1t, rest, rest_edge, slopes, weight, x, dr, gain, down, seqs, dps, reps):
    assert (dps, reps) == (4, 4)
    width, tokens = h1t.shape
    share = width // (seqs * dps)
    rest_blocks = rest.shape[1] // CUT - EARLY
    rest_edge = rest_edge - EARLY * CUT
    blocks_of = lambda array, count: (count, array.shape[0], array.shape[1] // count)
    blocks = rest_blocks + 3 * width // CUT
    halves = width // CUT
    token_blocks = tokens // TILE
    steps = max(blocks + token_blocks, blocks + LAGS[5], DOWN_BLOCKS + 3 * LINE_LAG)
    late = lambda s: jnp.clip(s - blocks, 0, token_blocks - 1)
    turn_of = lambda s: jnp.clip(s - rest_blocks, 0, blocks - rest_blocks - 1)
    fixed = lambda m, n: pl.BlockSpec((m, n), lambda s: (0, 0), pipeline_mode=pl.Buffered(1))
    row = pl.BlockSpec((TILE, width), lambda s: (late(s), 0))
    half_rows = 2 * seqs * share
    buffers = lambda *shape: [pltpu.VMEM(shape + (CUT,), BF16)] * 2
    slots = seqs + 4
    return pl.pallas_call(
        functools.partial(close_kernel, blocks, rest_blocks, rest_edge, seqs, reps),
        grid=(steps,),
        in_specs=[
            fixed(width, tokens),
            fixed(width, tokens),
            fixed(width, tokens),
            pl.BlockSpec((tokens, CUT), lambda s: (0, EARLY + jnp.minimum(s, rest_blocks - 1))),
            pl.BlockSpec((1, tokens, CUT), lambda s: (turn_of(s) // halves, 0, turn_of(s) % halves)),
            pl.BlockSpec((3, TILE, width), lambda s: (0, late(s), 0)),
            fixed(*weight.shape),
            row,
            row,
            fixed(1, width),
            fixed(*down.shape),
        ],
        out_specs=[
            row, fixed(share, rest_blocks * CUT), fixed(share, 3 * width), fixed(*down.shape),
        ],
        out_shape=[
            jax.ShapeDtypeStruct((tokens, width), F32),
            jax.ShapeDtypeStruct((share, rest_blocks * CUT), BF16),
            jax.ShapeDtypeStruct((share, 3 * width), BF16),
            jax.ShapeDtypeStruct(down.shape, BF16),
        ],
        scratch_shapes=[
            pltpu.VMEM((width, CUT), F32),
            pltpu.VMEM((2, half_rows, CUT), F32),
            pltpu.VMEM((2 * share, CUT), F32),
            pltpu.VMEM((seqs * share, CUT), F32),
            pltpu.VMEM((2, share, CUT), F32),
            *buffers(RING, half_rows),
            *buffers(RING_XY, seqs - 1, 2 * share),
            *buffers(RING_XY, seqs * share),
            *buffers(RING_XY, seqs - 1, share),
            *buffers(RING_XY, share),
            *[pltpu.VMEM((RING_LINE, share, CUT), BF16)] * 3,
            *[pltpu.VMEM(blocks_of(down, DOWN_BLOCKS), BF16)] * 2,
            pltpu.SemaphoreType.DMA((max(2 * RING_XY, RING_LINE), slots)),
            pltpu.SemaphoreType.DMA((max(2 * RING_XY, RING_LINE), slots)),
            pltpu.SemaphoreType.DMA((2, DOWN_BLOCKS, 3)),
        ],
        compiler_params=params(collective_id=1, has_side_effects=True),
        cost_estimate=pl.CostEstimate(
            flops=tokens * width * width // 4, bytes_accessed=4 * 1024 * 1024, transcendentals=0
        ),
        name="close",
    )(h2t, mixed_t, h1t, rest, slopes, slopes, weight, x, dr, gain, down)


def neighbours(block, axis, along, after=None):
    count = lax.axis_size(axis)
    rows = block.shape[along]
    if count == 2:
        start = (1 - lax.axis_index(axis)) * (rows - HALF)
        facing = lax.dynamic_slice_in_dim(block, start, HALF, along)
        if after is not None:
            facing, _ = lax.optimization_barrier((facing, after))
        return lax.ppermute(facing, axis, [(0, 1), (1, 0)])
    step = min(rows, HALF)
    head = lax.slice_in_dim(block, 0, step, axis=along)
    tail = lax.slice_in_dim(block, rows - step, rows, axis=along)
    hops = range(1, HALF // step + 1)
    after = [lax.ppermute(head, axis, [(i + hop, i) for i in range(count - hop)]) for hop in hops]
    before = [lax.ppermute(tail, axis, [(i, i + hop) for i in range(count - hop)]) for hop in reversed(hops)]
    return jnp.concatenate(after + before, axis=along)


def survey(labels, stretch, extent, seq_index, seq_count):
    length = labels.shape[1]
    mem = jnp.arange(extent, dtype=jnp.int32)
    own_start = seq_index * stretch
    wraps = stretch + HALF if seq_count > 2 else jnp.where(seq_index == 0, extent, stretch)
    places = own_start + mem - jnp.where(mem >= wraps, extent, 0)
    padded = jnp.pad(labels, ((0, 0), (HALF, HALF)))
    cut = lambda first, size: lax.dynamic_slice_in_dim(padded, first + HALF, size, 1)
    parts = [cut(own_start, stretch)]
    if seq_count == 2:
        parts.append(cut(jnp.where(seq_index == 0, own_start + stretch, own_start - HALF), HALF))
    else:
        parts += [cut(own_start + stretch, HALF), cut(own_start - HALF, HALF)]
    near = jnp.concatenate(parts, axis=1)
    docs = jnp.arange(DOCS, dtype=jnp.int32)
    starts = jnp.sum(labels[:, :, None] < docs, axis=1, dtype=jnp.int32)
    stops = jnp.sum(labels[:, :, None] <= docs, axis=1, dtype=jnp.int32) - 1
    same = near[:, :, None] == docs
    positions = places - jnp.sum(jnp.where(same, starts[:, None, :], 0), axis=-1)
    lane = jnp.arange(LANES, dtype=jnp.int32)
    half_dim = HEAD_DIM // 2
    frequency = THETA ** (-((lane % half_dim).astype(F32) * 2.0 / HEAD_DIM))
    angles = positions.astype(F32)[:, :, None] * frequency
    cosines = jnp.cos(angles)
    sines = jnp.sin(angles) * jnp.where(lane % HEAD_DIM < half_dim, -1.0, 1.0)
    slot = lane % HEAD_DIM
    marks_k = jnp.where(
        slot < DOCS,
        jnp.where(near[:, :, None] == slot, 0.0, MASKED),
        jnp.where((slot >= 8) & (slot < 11), 1.0, 0.0),
    ).astype(BF16)
    kind = jnp.arange(HEAD_DIM, dtype=jnp.int32)[None, :, None]
    marks_q = jnp.where((kind < DOCS) & (near[:, None, :] == kind), 1.0, 0.0).astype(BF16)
    at = jnp.arange(length // TILE, dtype=jnp.int32) * TILE
    first_label, last_label = labels[:, ::TILE], labels[:, TILE - 1 :: TILE]
    pick = lambda table, which: jnp.sum(
        jnp.where(which[:, :, None] == docs, table[:, None, :], 0), axis=-1
    )
    lows = jnp.maximum(pick(starts, first_label), at - HALF) // TILE
    highs = jnp.minimum(pick(stops, last_label), at + TILE - 1 + HALF) // TILE + 1
    own = (own_start // TILE).astype(jnp.int32).reshape(1)
    return own, lows, highs, cosines, sines, marks_k, marks_q


def body(inputs, segments, cotangent, attn_gain, mlp_gain, w_qkv, w_out, w_in, w_down):
    stretch, width = inputs.shape[2:]
    length = segments.shape[2]
    x = inputs.reshape(-1, stretch, width)
    seeds = cotangent.reshape(-1, stretch, width)
    labels = segments.reshape(-1, length)
    batch = x.shape[0]
    group = ("seq", "dp")
    seq_index = lax.axis_index("seq")
    seq_count = lax.axis_size("seq")

    share = attn_gain.shape[0]
    shards = width // share
    gather = lambda shard: lax.all_gather(shard, group, axis=0, tiled=True)
    gain_rows = jnp.pad(jnp.stack([attn_gain, mlp_gain]), ((0, share - 2), (0, LANES - share)))
    qkv_full = gather(jnp.concatenate([w_qkv, gain_rows], axis=1))
    blank = jnp.zeros((share, FF_PAD - FF), BF16)
    halo = HALF * (1 if seq_count == 2 else 2)
    extent = stretch + halo
    own, lows, highs, cosines, sines, marks_k, marks_q = survey(labels, stretch, extent, seq_index, seq_count)
    x_halo = neighbours(x, "seq", 1, (qkv_full, cosines, sines, marks_k))
    rest_full = gather(jnp.concatenate([w_in[:, :FF], blank, w_in[:, FF:], blank, w_out], axis=1))
    down_full = gather(w_down)

    h1t, qkv = project(x, qkv_full, cosines, sines, 0, None, extent, shards)
    qkv = project(x_halo, qkv_full, cosines, sines, stretch // TILE, qkv, extent, shards)
    mixed, mixed_t, lse = attend(own, lows, highs, qkv, marks_k, marks_q, stretch)
    lse_halo = neighbours(lse, "seq", 3)
    late_full, mixed, lse_halo = lax.optimization_barrier((qkv_full, mixed, lse_halo))
    gains = late_full[:, 3 * width : 3 * width + share].reshape(shards, share, share).astype(F32)
    gain_one, gain_two = gains[:, 0].reshape(1, width), gains[:, 1].reshape(1, width)
    result, h2t, hidt, slopes, dr, do, delta, do_halo, delta_halo = feed(
        x, mixed, seeds, gain_two, rest_full, down_full, seq_count, halo
    )

    tokens = batch * stretch
    dps = lax.axis_size("dp")
    pairs = [list(range(core, seq_count * dps, 2)) for core in range(2)]
    scatter = lambda part: lax.psum_scatter(part, group, scatter_dimension=0, tiled=True, axis_index_groups=pairs)
    slopes = slopes.reshape(tokens, -1)
    part_early = weigh([h2t], slopes, CUT, EARLY, ((0, EARLY, ((0, CUT),)),), share, "weigh_early", 4)
    shard_early = scatter(part_early)
    hidt, part_early = lax.optimization_barrier((hidt, part_early))
    part_down = weigh(
        [hidt], seeds.reshape(tokens, width), TILE, width // TILE, ((0, width // TILE, ((0, TILE),)),),
        w_down.shape[0], "weigh_down", 3,
    )
    shard_down = scatter(part_down)
    do_halo, part_down = lax.optimization_barrier((do_halo, part_down))

    def back(first_batch, count, held):
        return attend_back(
            own, lows, highs, qkv, do, do_halo, lse, lse_halo, delta, delta_halo, marks_k, marks_q, cosines, sines,
            first_batch, count, held,
        )

    slopes_qkv = back(0, batch // 2, None)
    slopes_qkv, shard_early = lax.optimization_barrier((slopes_qkv, shard_early))
    early_sum = lax.psum(shard_early, "rep")
    slopes_qkv = back(batch // 2, batch - batch // 2, slopes_qkv)
    grad_x, late_sum, grad_qkv, down_sum = close(
        h2t, mixed_t, h1t, slopes, 2 * FF_PAD, slopes_qkv.reshape(3, tokens, width), qkv_full, x.reshape(tokens, width), dr.reshape(tokens, width),
        gain_one, shard_down, seq_count, dps, lax.axis_size("rep"),
    )
    grad_qkv = grad_qkv.astype(F32)
    rest_sum = jnp.concatenate([early_sum, late_sum], axis=1).astype(F32)
    grad_in = jnp.concatenate([rest_sum[:, :FF], rest_sum[:, FF_PAD : FF_PAD + FF]], axis=1)
    grad_attn_gain = jnp.sum(grad_qkv * w_qkv.astype(F32), axis=1) / attn_gain.astype(F32)
    grad_mlp_gain = jnp.sum(grad_in * w_in.astype(F32), axis=1) / mlp_gain.astype(F32)
    return (
        result.reshape(cotangent.shape),
        grad_x.reshape(inputs.shape),
        grad_attn_gain,
        grad_mlp_gain,
        grad_qkv,
        rest_sum[:, 2 * FF_PAD : 2 * FF_PAD + width],
        grad_in,
        down_sum[: w_down.shape[0]].astype(F32),
    )


def solution(mesh):
    return jax.shard_map(
        body,
        mesh=mesh,
        in_specs=(
            P(None, ("dp", "rep"), "seq", None),
            P(None, ("dp", "rep"), None),
            P(None, ("dp", "rep"), "seq", None),
            P(("seq", "dp")),
            P(("seq", "dp")),
            P(("seq", "dp"), None),
            P(("seq", "dp"), None),
            P(("seq", "dp"), None),
            P(("seq", "dp"), None),
        ),
        out_specs=(
            P(None, ("dp", "rep"), "seq", None),
            P(None, ("dp", "rep"), "seq", None),
            P(("seq", "dp")),
            P(("seq", "dp")),
            P(("seq", "dp"), None),
            P(("seq", "dp"), None),
            P(("seq", "dp"), None),
            P(("seq", "dp"), None),
        ),
        check_vma=False,
    )
```

```python
import functools

import jax
import jax.numpy as jnp
from jax import lax
from jax.experimental import pallas as pl
from jax.experimental.pallas import tpu as pltpu
from jax.sharding import PartitionSpec as P

HEADS = 16
HEAD_DIM = 64
FF = 2624
HALF = 512
DOCS = 7

EPS = 1e-05
THETA = 10000.0
MASKED = -1e30

TILE = 256
CUT = 512
REACH = HALF // TILE
LANES = 128
FF_PAD = -(-FF // LANES) * LANES
PAIRS = HEADS // 2
WIDE = 4
WIDE_BACK = 2
VMEM = 60 * 1024 * 1024

F32 = jnp.float32
BF16 = jnp.bfloat16

MESH = pl.DeviceIdType.MESH

NN = (((1,), (0,)), ((), ()))
NT = (((1,), (1,)), ((), ()))


def dot(left, right, dims=NN):
    return lax.dot_general(left, right, dims, preferred_element_type=F32)


def params(**more):
    return pltpu.CompilerParams(vmem_limit_bytes=VMEM, **more)


def normed(values):
    centre = values - jnp.mean(values, axis=-1, keepdims=True)
    spread = jnp.mean(centre * centre, axis=-1, keepdims=True)
    inverse = lax.rsqrt(spread + EPS)
    return centre * inverse, inverse


def norm_back(grads, unit, inverse):
    first = jnp.mean(grads, axis=-1, keepdims=True)
    second = jnp.mean(grads * unit, axis=-1, keepdims=True)
    return (grads - first - unit * second) * inverse


def swapped(values):
    lane = lax.broadcasted_iota(jnp.int32, values.shape, 1)
    ahead = pltpu.roll(values, LANES - HEAD_DIM // 2, 1)
    behind = pltpu.roll(values, HEAD_DIM // 2, 1)
    return jnp.where(lane % HEAD_DIM < HEAD_DIM // 2, ahead, behind)


def project_kernel(keep, shards, x_ref, w_ref, cos_ref, sin_ref, *outs):
    qkv_ref = outs[-1]
    width = x_ref.shape[2]
    share = width // shards
    gain = jnp.concatenate(
        [w_ref[share * i : share * i + 1, 3 * width : 3 * width + share] for i in range(shards)], axis=1
    ).astype(F32)
    unit, _ = normed(x_ref[0].astype(F32))
    h1 = (unit * gain).astype(BF16)
    if keep:
        outs[0][...] = h1.T
    cosines, sines = cos_ref[0], sin_ref[0]
    for start in range(0, 3 * width, 512):
        part = dot(h1, w_ref[:, start : start + 512])
        for column in range(0, 512, LANES):
            piece = part[:, column : column + LANES]
            if start < 2 * width:
                piece = piece * cosines + swapped(piece) * sines
            if start < width:
                piece = piece * HEAD_DIM**-0.5
            qkv_ref[0, :, start + column : start + column + LANES] = piece.astype(BF16)


def project(x, weight, cosines, sines, first_tile, held, extent, shards):
    batch, rows, width = x.shape
    steps = rows // TILE
    grid = (batch, steps)
    keep = held is None
    block = lambda b, i: (b, i, 0)
    shifted = lambda b, i: (b, i + first_tile, 0)
    qkv_spec = pl.BlockSpec((1, TILE, 3 * width), shifted)
    qkv_shape = jax.ShapeDtypeStruct((batch, extent, 3 * width), BF16)
    in_specs = [
        pl.BlockSpec((1, TILE, width), block),
        pl.BlockSpec(weight.shape, lambda b, i: (0, 0), pipeline_mode=pl.Buffered(1)),
        pl.BlockSpec((1, TILE, LANES), shifted),
        pl.BlockSpec((1, TILE, LANES), shifted),
    ]
    cost = pl.CostEstimate(
        flops=2 * batch * rows * width * 3 * width,
        bytes_accessed=8 * batch * rows * width + 6 * width * width,
        transcendentals=0,
    )
    if keep:
        return pl.pallas_call(
            functools.partial(project_kernel, True, shards),
            grid=grid,
            in_specs=in_specs,
            out_specs=[pl.BlockSpec((width, TILE), lambda b, i: (0, b * steps + i)), qkv_spec],
            out_shape=[jax.ShapeDtypeStruct((width, batch * rows), BF16), qkv_shape],
            compiler_params=params(),
            cost_estimate=cost,
            name="project_own",
        )(x, weight, cosines, sines)

    def halo_kernel(x_ref, w_ref, cos_ref, sin_ref, held_ref, qkv_ref):
        project_kernel(False, shards, x_ref, w_ref, cos_ref, sin_ref, qkv_ref)

    return pl.pallas_call(
        halo_kernel,
        grid=grid,
        in_specs=in_specs + [pl.BlockSpec(memory_space=pl.ANY)],
        out_specs=qkv_spec,
        out_shape=qkv_shape,
        input_output_aliases={4: 0},
        compiler_params=params(),
        cost_estimate=cost,
        name="project_halo",
    )(x, weight, cosines, sines, held)


def edge_masks():
    key = lax.broadcasted_iota(jnp.int32, (TILE, TILE), 0)
    query = lax.broadcasted_iota(jnp.int32, (TILE, TILE), 1)
    return (
        jnp.where(key >= query, 0.0, MASKED).astype(F32),
        jnp.where(key <= query, 0.0, MASKED).astype(F32),
    )


def edge_of(key_tile, query_tile):
    gap = key_tile - query_tile
    return jnp.where(gap == -REACH, 0, jnp.where(gap == REACH, 2, 1))


def low_half(rows):
    return lax.broadcasted_iota(jnp.int32, (rows, LANES), 1) < HEAD_DIM


def split3(values):
    high = values.astype(BF16).astype(F32)
    rest = values - high
    middle = rest.astype(BF16).astype(F32)
    return high, middle, rest - middle


def attend_kernel(tiles, wide, own_ref, lo_ref, hi_ref, q_ref, k_ref, v_ref, ek_ref, eq_ref, o_ref, ot_ref, lse_ref,
                  kx, qx, vx, edges):
    batch = pl.program_id(0)
    stretch, extent = q_ref.shape[1], k_ref.shape[1]

    @pl.when((batch == 0) & (pl.program_id(1) == 0))
    def _():
        before, after = edge_masks()
        edges[0] = before
        edges[1] = jnp.zeros((TILE, TILE), F32)
        edges[2] = after

    low = low_half(extent)
    marks = ek_ref[0]
    ones = jnp.ones((16, extent), BF16)
    for pair in range(wide):
        span = slice(pair * LANES, (pair + 1) * LANES)
        keys = k_ref[0, :, span]
        kx[2 * pair] = jnp.where(low, keys, marks)
        kx[2 * pair + 1] = jnp.where(low, marks, keys)
        turned = q_ref[0, :, span].T
        qx[2 * pair] = jnp.concatenate([turned[:HEAD_DIM], eq_ref[0]], axis=0)
        qx[2 * pair + 1] = jnp.concatenate([eq_ref[0], turned[HEAD_DIM:]], axis=0)
        flipped = v_ref[0, :, span].T
        vx[2 * pair] = jnp.concatenate([flipped[:HEAD_DIM], ones], axis=0)
        vx[2 * pair + 1] = jnp.concatenate([flipped[HEAD_DIM:], ones], axis=0)
    own = own_ref[0]

    def one_tile(index, carry):
        query_tile = own + index
        first, last = lo_ref[batch, query_tile], hi_ref[batch, query_tile]
        columns = pl.ds(pl.multiple_of(index * TILE, TILE), TILE)

        def some(count):
            places, masks = [], []
            for step in range(count):
                key_tile = first + step
                places.append(pl.multiple_of(lax.rem(key_tile - own + tiles, tiles) * TILE, TILE))
                masks.append(edge_of(key_tile, query_tile))

            def score(head):
                return [
                    dot(kx[head, pl.ds(place, TILE), :], qx[head, :, columns]) + edges[mask]
                    for place, mask in zip(places, masks)
                ]

            heads = 2 * wide
            scores = {head: score(head) for head in range(min(1, heads))}
            mixed, waiting = [], []

            def close_head(head, top, powers):
                sums = dot(
                    jnp.concatenate([vx[head, :, pl.ds(place, TILE)] for place in places], axis=1),
                    jnp.concatenate(powers, axis=0),
                )
                total = sums[HEAD_DIM : HEAD_DIM + 1]
                mixed.append(sums[:HEAD_DIM] * (1.0 / total))
                lse_ref[0, head // 2, head % 2 : head % 2 + 1, columns] = top + jnp.log(total)
                if head % 2 == 1:
                    both = jnp.concatenate(mixed[-2:], axis=0)
                    span = slice(head // 2 * LANES, (head // 2 + 1) * LANES)
                    ot_ref[span, columns] = both.astype(BF16)
                    o_ref[0, columns, span] = both.T.astype(BF16)

            for head in range(heads):
                if head + 1 < heads:
                    scores[head + 1] = score(head + 1)
                parts = scores.pop(head)
                top = parts[0]
                for part in parts[1:]:
                    top = jnp.maximum(top, part)
                top = jnp.max(top, axis=0, keepdims=True)
                powers = [jnp.exp(part - top).astype(BF16) for part in parts]
                waiting.append((head, top, powers))
                if len(waiting) > 1:
                    close_head(*waiting.pop(0))
            for item in waiting:
                close_head(*item)

        for count in range(1, 2 * REACH + 2):
            pl.when(last - first == count)(functools.partial(some, count))
        return carry

    lax.fori_loop(0, stretch // TILE, one_tile, 0)


def attend(own, lows, highs, qkv, marks_k, marks_q, stretch):
    batch, extent, _ = qkv.shape
    tiles = extent // TILE
    width = PAIRS * LANES
    wide = WIDE
    groups = PAIRS // wide
    spec = lambda rows, offset: pl.BlockSpec((1, rows, wide * LANES), lambda b, p, *_: (b, 0, p + offset))
    per = pl.BlockSpec((1, extent, LANES), lambda b, p, *_: (b, 0, 0))
    return pl.pallas_call(
        functools.partial(attend_kernel, tiles, wide),
        grid_spec=pltpu.PrefetchScalarGridSpec(
            num_scalar_prefetch=3,
            grid=(batch, groups),
            in_specs=[
                spec(stretch, 0),
                spec(extent, groups),
                spec(extent, 2 * groups),
                per,
                pl.BlockSpec((1, HEAD_DIM, stretch), lambda b, p, *_: (b, 0, 0)),
            ],
            out_specs=[
                spec(stretch, 0),
                pl.BlockSpec((wide * LANES, stretch), lambda b, p, *_: (p, b)),
                pl.BlockSpec((1, wide, 2, stretch), lambda b, p, *_: (b, p, 0, 0)),
            ],
            scratch_shapes=[
                pltpu.VMEM((2 * wide, extent, LANES), BF16),
                pltpu.VMEM((2 * wide, LANES, stretch), BF16),
                pltpu.VMEM((2 * wide, HEAD_DIM + 16, extent), BF16),
                pltpu.VMEM((3, TILE, TILE), F32),
            ],
        ),
        out_shape=[
            jax.ShapeDtypeStruct((batch, stretch, width), BF16),
            jax.ShapeDtypeStruct((width, batch * stretch), BF16),
            jax.ShapeDtypeStruct((batch, PAIRS, 2, stretch), F32),
        ],
        compiler_params=params(),
        cost_estimate=pl.CostEstimate(
            flops=2 * 2 * HEADS * batch * stretch * extent * 128, bytes_accessed=32 * 1024 * 1024, transcendentals=0
        ),
        name="attend",
    )(own, lows, highs, qkv, qkv, qkv, marks_k, marks_q)


def attend_back_kernel(tiles, wide, first_batch, own_ref, lo_ref, hi_ref, q_ref, k_ref, v_ref, do_ref, doh_ref, lse_ref, lseh_ref,
                       delta_ref, deltah_ref, ek_ref, eq_ref, cos_ref, sin_ref, *refs):
    out_ref, kx, vx, qx, dx, dn, kt, dqt, edges = refs[-9:]
    batch = pl.program_id(0) + first_batch
    extent = k_ref.shape[1]
    stretch = do_ref.shape[1]
    mine = stretch // TILE
    heads = 2 * wide

    @pl.when((pl.program_id(0) == 0) & (pl.program_id(1) == 0))
    def _():
        before, after = edge_masks()
        edges[0] = before
        edges[1] = jnp.zeros((TILE, TILE), F32)
        edges[2] = after

    low = low_half(extent)
    marks = ek_ref[0]
    lane = lax.broadcasted_iota(jnp.int32, (extent, LANES), 1) % HEAD_DIM
    units = jnp.where((lane >= 8) & (lane < 11), 1.0, 0.0).astype(BF16)
    row = lax.broadcasted_iota(jnp.int32, (HEAD_DIM, extent), 0)
    label_rows = eq_ref[0].astype(F32)
    dn[:stretch] = do_ref[0]
    dn[stretch:] = doh_ref[0]
    for pair in range(wide):
        span = slice(pair * LANES, (pair + 1) * LANES)
        keys, values = k_ref[0, :, span], v_ref[0, :, span]
        kx[2 * pair] = jnp.where(low, keys, marks)
        kx[2 * pair + 1] = jnp.where(low, marks, keys)
        kt[span] = keys.T
        vx[2 * pair] = jnp.where(low, values, units)
        vx[2 * pair + 1] = jnp.where(low, units, values)
        turned, flipped = q_ref[0, :, span].T, dn[:, span].T
        lses = jnp.concatenate([lse_ref[0, pair], lseh_ref[0, pair]], axis=1)
        deltas = jnp.concatenate([delta_ref[0, pair], deltah_ref[0, pair]], axis=1)
        for half in range(2):
            lse = split3(lses[half : half + 1])
            delta = split3(deltas[half : half + 1])
            mark, shift = label_rows, jnp.zeros((HEAD_DIM, extent), F32)
            for place in range(3):
                mark = jnp.where(row == 8 + place, -lse[place], mark)
                shift = jnp.where(row == 8 + place, -delta[place], shift)
            mark, shift = mark.astype(BF16), shift.astype(BF16)
            rows = slice(half * HEAD_DIM, (half + 1) * HEAD_DIM)
            order = (lambda a, b: [a, b]) if half == 0 else (lambda a, b: [b, a])
            qx[2 * pair + half] = jnp.concatenate(order(turned[rows], mark), axis=0)
            dx[2 * pair + half] = jnp.concatenate(order(flipped[rows], shift), axis=0)

    own = own_ref[0]
    dqt[...] = jnp.zeros_like(dqt)
    low_tile = low_half(TILE)

    def place(tile):
        return pl.ds(pl.multiple_of(lax.rem(tile - own + tiles, tiles) * TILE, TILE), TILE)

    def some(key_tile, begin, count, key_grad, out_rows):
        rows = place(key_tile)
        columns = [place(begin + step) for step in range(count)]
        masks = [edge_of(key_tile, begin + step) for step in range(count)]
        items = [(head, step) for head in range(heads) for step in range(count)]
        powers, slopes, sums = {}, {}, {}

        def first_products(head, step):
            score = dot(kx[head, rows, :], qx[head, :, columns[step]]) + edges[masks[step]]
            return score, dot(vx[head, rows, :], dx[head, :, columns[step]])

        def last_products(head, step):
            span = slice(head * HEAD_DIM, (head + 1) * HEAD_DIM)
            dqt[span, columns[step]] += dot(kt[span, rows], slopes[head][step])
            if not key_grad or step + 1 < count:
                return
            pair = slice(head // 2 * LANES, (head // 2 + 1) * LANES)
            grads = jnp.concatenate([dn[column, pair] for column in columns], axis=0)
            queries = jnp.concatenate([q_ref[0, column, pair] for column in columns], axis=0)
            sums[head] = (
                dot(jnp.concatenate(slopes.pop(head), axis=1), queries),
                dot(jnp.concatenate(powers.pop(head), axis=1), grads),
            )
            if head % 2 == 1:
                key_sum, value_sum = (jnp.where(low_tile, a, b) for a, b in zip(sums[head - 1], sums[head]))
                cosines, sines = cos_ref[0, out_rows, :], sin_ref[0, out_rows, :]
                out_ref[1, 0, out_rows, pair] = (key_sum * cosines - swapped(key_sum) * sines).astype(BF16)
                out_ref[2, 0, out_rows, pair] = value_sum.astype(BF16)

        ahead = [first_products(*items[0])]
        for index, (head, step) in enumerate(items):
            if index + 1 < len(items):
                ahead.append(first_products(*items[index + 1]))
            score, slope = ahead.pop(0)
            power = jnp.exp(score)
            powers.setdefault(head, []).append(power.astype(BF16))
            slopes.setdefault(head, []).append((power * slope).astype(BF16))
            if index >= 1:
                last_products(*items[index - 1])
        last_products(*items[-1])

    def own_keys(index, carry):
        key_tile = own + index
        first, last = lo_ref[batch, key_tile], hi_ref[batch, key_tile]
        out_rows = pl.ds(pl.multiple_of(index * TILE, TILE), TILE)
        for count in range(1, 2 * REACH + 2):
            pl.when(last - first == count)(functools.partial(some, key_tile, first, count, True, out_rows))
        return carry

    lax.fori_loop(0, mine, own_keys, 0)

    def other_keys(mem, carry):
        ahead = own + mem
        key_tile = jnp.where(ahead < own + mine + REACH, ahead, ahead - tiles)
        if tiles == mine + REACH:
            key_tile = jnp.where(own == 0, ahead, ahead - tiles)
        valid = (key_tile >= 0) & (key_tile < lo_ref.shape[1])
        safe = jnp.where(valid, key_tile, 0)
        begin = jnp.maximum(lo_ref[batch, safe], own)
        end = jnp.where(valid, jnp.minimum(hi_ref[batch, safe], own + mine), begin)
        for count in range(1, min(REACH, mine) + 1):
            pl.when(end - begin == count)(functools.partial(some, safe, begin, count, False, None))
        return carry

    lax.fori_loop(mine, tiles, other_keys, 0)
    for pair in range(wide):
        span = slice(pair * LANES, (pair + 1) * LANES)
        raw = dqt[span, :stretch].T * HEAD_DIM**-0.5
        out_ref[0, 0, :, span] = (raw * cos_ref[0] - swapped(raw) * sin_ref[0]).astype(BF16)


def attend_back(own, lows, highs, qkv, grads, grads_halo, lse, lse_halo, delta, delta_halo, marks_k, marks_q,
                cosines, sines, first_batch, count, held):
    batch, extent, _ = qkv.shape
    stretch, width = grads.shape[1:]
    halo = extent - stretch
    tiles = extent // TILE
    wide = WIDE_BACK
    groups = PAIRS // wide
    spec = lambda rows, offset: pl.BlockSpec((1, rows, wide * LANES), lambda b, p, *_: (b + first_batch, 0, p + offset))
    per = lambda rows: pl.BlockSpec((1, rows, LANES), lambda b, p, *_: (b + first_batch, 0, 0))
    numbers = lambda rows: pl.BlockSpec((1, wide, 2, rows), lambda b, p, *_: (b + first_batch, p, 0, 0))
    return pl.pallas_call(
        functools.partial(attend_back_kernel, tiles, wide, first_batch),
        grid_spec=pltpu.PrefetchScalarGridSpec(
            num_scalar_prefetch=3,
            grid=(count, groups),
            in_specs=[
                spec(extent, 0),
                spec(extent, groups),
                spec(extent, 2 * groups),
                spec(stretch, 0),
                spec(halo, 0),
                numbers(stretch),
                numbers(halo),
                numbers(stretch),
                numbers(halo),
                per(extent),
                pl.BlockSpec((1, HEAD_DIM, extent), lambda b, p, *_: (b + first_batch, 0, 0)),
                per(stretch),
                per(stretch),
            ]
            + ([] if held is None else [pl.BlockSpec(memory_space=pl.ANY)]),
            out_specs=pl.BlockSpec((3, 1, stretch, wide * LANES), lambda b, p, *_: (0, b + first_batch, 0, p)),
            scratch_shapes=[
                pltpu.VMEM((2 * wide, extent, LANES), BF16),
                pltpu.VMEM((2 * wide, extent, LANES), BF16),
                pltpu.VMEM((2 * wide, LANES, extent), BF16),
                pltpu.VMEM((2 * wide, LANES, extent), BF16),
                pltpu.VMEM((extent, wide * LANES), BF16),
                pltpu.VMEM((wide * LANES, extent), BF16),
                pltpu.VMEM((wide * LANES, extent), F32),
                pltpu.VMEM((3, TILE, TILE), F32),
            ],
        ),
        input_output_aliases={} if held is None else {16: 0},
        out_shape=jax.ShapeDtypeStruct((3, batch, stretch, width), BF16),
        compiler_params=params(),
        cost_estimate=pl.CostEstimate(
            flops=5 * 2 * HEADS * count * stretch * extent * 128, bytes_accessed=64 * 1024 * 1024, transcendentals=0
        ),
        name="attend_back",
    )(own, lows, highs, qkv, qkv, qkv, grads, grads_halo, lse, lse_halo, delta, delta_halo, marks_k, marks_q,
      cosines, sines, *([] if held is None else [held]))


def feed_kernel(seqs, halo_tiles, x_ref, o_ref, g_ref, gain_ref, w_ref, wd_ref,
                out_ref, h2t_ref, hidt_ref, slopes_ref, dr_ref, do_ref, delta_ref, do_halo, delta_halo,
                do_sent, delta_sent, send_sem, recv_sem):
    batch, steps = pl.num_programs(1), pl.num_programs(0)
    step, sequence = pl.program_id(0), pl.program_id(1)
    seq = lax.axis_index("seq")
    mine, tiles = steps, steps + halo_tiles
    reach = -(-REACH // mine)
    hops = [hop for hop in range(-reach, reach + 1) if hop != 0]

    def exists(hop):
        return (seq + hop >= 0) & (seq + hop < seqs)

    def sent(which, tile, hop):
        peer = seq + hop
        place = seq * mine + tile
        wanted = exists(hop) & (place >= peer * mine - REACH) & (place < (peer + 1) * mine + REACH)
        slot = lax.rem(place - peer * mine + tiles, tiles) - mine
        slot = jnp.where(wanted, slot, 0)
        return wanted, halo_copies(which, tile, slot, hops.index(hop), peer)

    def halo_copies(which, tile, slot, hop, peer):
        span = pl.ds(pl.multiple_of(slot * TILE, TILE), TILE)
        pieces = [
            (do_sent.at[which, tile], do_halo.at[which, span]),
            (delta_sent.at[which, tile], delta_halo.at[which, :, :, span]),
        ]
        return [
            pltpu.make_async_remote_copy(
                src_ref=source, dst_ref=target, send_sem=send_sem.at[kind, which, tile, hop],
                recv_sem=recv_sem.at[kind, which, slot], device_id={"seq": peer}, device_id_type=MESH,
            )
            for kind, (source, target) in enumerate(pieces)
        ]

    @pl.when((step == 0) & (sequence == 0))
    def _():
        barrier = pltpu.get_barrier_semaphore()
        for hop in hops:
            @pl.when(exists(hop))
            def _():
                pl.semaphore_signal(barrier, inc=1, device_id={"seq": seq + hop}, device_id_type=MESH)

        for hop in hops:
            @pl.when(exists(hop))
            def _():
                pl.semaphore_wait(barrier, 1)

    mixed = o_ref[0]
    seeds = g_ref[0]
    gain = gain_ref[...]
    width = mixed.shape[1]
    w_out = slice(2 * FF_PAD, 2 * FF_PAD + width)
    r1 = x_ref[0].astype(F32) + dot(mixed, w_ref[:, w_out])
    unit, inverse = normed(r1)
    h2 = (unit * gain).astype(BF16)
    h2t_ref[...] = h2.T
    total = r1
    back = jnp.zeros_like(r1)
    edges = list(range(0, FF - 511, 512))
    for start, stop in zip(edges, edges[1:] + [FF]):
        gates, ups = slice(start, stop), slice(FF_PAD + start, FF_PAD + stop)
        gate = dot(h2, w_ref[:, gates])
        up = dot(h2, w_ref[:, ups])
        grad = dot(seeds, wd_ref[start:stop, :], NT)
        phi = 0.5 + 0.5 * lax.erf(gate * (0.5**0.5))
        bell = jnp.exp(gate * gate * -0.5) * 0.3989422804014327
        act = gate * phi
        hid = (act * up).astype(BF16)
        grad_gate = (grad * up * (phi + gate * bell)).astype(BF16)
        grad_up = (grad * act).astype(BF16)
        hidt_ref[start:stop, :] = hid.T
        slopes_ref[0, :, gates] = grad_gate
        slopes_ref[0, :, ups] = grad_up
        total = total + dot(hid, wd_ref[start:stop, :])
        back = back + dot(grad_gate, w_ref[:, gates], NT) + dot(grad_up, w_ref[:, ups], NT)
    blank = jnp.zeros((TILE, FF_PAD - FF), BF16)
    slopes_ref[0, :, 2 * FF_PAD + width :] = jnp.zeros((TILE, slopes_ref.shape[2] - 2 * FF_PAD - width), BF16)
    slopes_ref[0, :, FF:FF_PAD] = blank
    slopes_ref[0, :, FF_PAD + FF : 2 * FF_PAD] = blank
    out_ref[0] = total.astype(BF16)
    dr = seeds.astype(F32) + norm_back(back * gain, unit, inverse)
    dr_ref[0] = dr
    da = dr.astype(BF16)
    slopes_ref[0, :, w_out] = da
    do = dot(da, w_ref[:, w_out], NT).astype(BF16)
    do_ref[0] = do
    product = do.astype(F32) * mixed.astype(F32)
    high = product.astype(BF16)
    rest = (product - high.astype(F32)).astype(BF16)
    head = lax.broadcasted_iota(jnp.int32, (HEADS, width), 0)
    column = lax.broadcasted_iota(jnp.int32, (HEADS, width), 1)
    pick = jnp.where(column // HEAD_DIM == head, 1.0, 0.0).astype(BF16)
    delta = dot(pick, high, NT) + dot(pick, rest, NT)
    tile = facing_first(step, steps, seqs)
    do_sent[sequence, tile] = do
    for pair in range(PAIRS):
        delta_ref[0, pair] = delta[2 * pair : 2 * pair + 2]
        delta_sent[sequence, tile, pair] = delta[2 * pair : 2 * pair + 2]
    for hop in hops:
        wanted, copies = sent(sequence, tile, hop)

        @pl.when(wanted)
        def _():
            for copy in copies:
                copy.start()

    @pl.when((step == steps - 1) & (sequence == batch - 1))
    def _():
        def settle(index, carry):
            which, tile = index // mine, lax.rem(index, mine)
            for hop in hops:
                wanted, copies = sent(which, tile, hop)

                @pl.when(wanted)
                def _():
                    for copy in copies:
                        copy.wait_send()

            return carry

        lax.fori_loop(0, batch * mine, settle, 0)

        def arrive(index, carry):
            which, slot = index // halo_tiles, lax.rem(index, halo_tiles)
            place = seq * mine + mine + slot
            if halo_tiles == REACH:
                place = jnp.where(seq == 0, place, place - tiles)
            else:
                place = jnp.where(slot < REACH, place, place - tiles)

            @pl.when((place >= 0) & (place < seqs * mine))
            def _():
                for copy in halo_copies(which, 0, slot, 0, seq):
                    copy.wait_recv()

            return carry

        lax.fori_loop(0, batch * halo_tiles, arrive, 0)


def facing_first(step, steps, seqs):
    if seqs != 2:
        return step
    return lax.rem(step + (1 - lax.axis_index("seq")) * (steps // 2), steps)


def feed(x, mixed, seeds, gain, w_rest, w_down, seqs, halo):
    batch, rows, width = x.shape
    steps = rows // TILE
    place = lambda i: facing_first(i, steps, seqs)
    block = lambda n: pl.BlockSpec((1, TILE, n), lambda i, b: (b, place(i), 0))
    turned = lambda n: pl.BlockSpec((n, TILE), lambda i, b: (0, b * steps + place(i)))
    fixed = lambda m, n: pl.BlockSpec((m, n), lambda i, b: (0, 0), pipeline_mode=pl.Buffered(1))
    shape = lambda n, t: jax.ShapeDtypeStruct((batch, rows, n), t)
    columns = w_rest.shape[1]
    padded = -(-columns // CUT) * CUT
    reach = -(-REACH // steps)
    return pl.pallas_call(
        functools.partial(feed_kernel, seqs, halo // TILE),
        grid=(steps, batch),
        in_specs=[
            block(width), block(width), block(width), fixed(1, width), fixed(width, columns), fixed(FF, width),
        ],
        out_specs=[
            block(width), turned(width), turned(FF), block(padded), block(width), block(width),
            pl.BlockSpec((1, PAIRS, 2, TILE), lambda i, b: (b, 0, 0, place(i))),
            pl.BlockSpec(memory_space=pl.ANY),
            pl.BlockSpec(memory_space=pl.ANY),
        ],
        out_shape=[
            shape(width, BF16),
            jax.ShapeDtypeStruct((width, batch * rows), BF16),
            jax.ShapeDtypeStruct((FF, batch * rows), BF16),
            shape(padded, BF16),
            shape(width, F32),
            shape(width, BF16),
            jax.ShapeDtypeStruct((batch, PAIRS, 2, rows), F32),
            jax.ShapeDtypeStruct((batch, halo, width), BF16),
            jax.ShapeDtypeStruct((batch, PAIRS, 2, halo), F32),
        ],
        scratch_shapes=[
            pltpu.VMEM((batch, steps, TILE, width), BF16),
            pltpu.VMEM((batch, steps, PAIRS, 2, TILE), F32),
            pltpu.SemaphoreType.DMA((2, batch, steps, 2 * reach)),
            pltpu.SemaphoreType.DMA((2, batch, halo // TILE)),
        ],
        compiler_params=params(collective_id=2, has_side_effects=True),
        cost_estimate=pl.CostEstimate(
            flops=2 * batch * rows * width * (6 * FF + 2 * width), bytes_accessed=64 * 1024 * 1024, transcendentals=0
        ),
        name="feed",
    )(x, mixed, seeds, gain, w_rest, w_down)


def weigh_kernel(blocks, share, held, turns, *refs):
    lefts, (right_ref, out_ref, prod, kept, sent, got, send_sem, recv_sem) = refs[:-8], refs[-8:]
    step = pl.program_id(0)
    dp = lax.axis_index("dp")
    core = lax.rem(dp, 2)
    mate = dp + 1 - 2 * core
    places = prod.shape[0] // (2 * share)

    def to_mate(n):
        return pltpu.make_async_remote_copy(
            src_ref=sent.at[n], dst_ref=got.at[n], send_sem=send_sem.at[n], recv_sem=recv_sem.at[n],
            device_id={"dp": mate}, device_id_type=MESH,
        )

    @pl.when(step == 0)
    def _():
        barrier = pltpu.get_barrier_semaphore()
        pl.semaphore_signal(barrier, inc=1, device_id={"dp": mate}, device_id_type=MESH)
        pl.semaphore_wait(barrier, 1)

    columns = right_ref.shape[1]
    for first, last, pieces in turns:

        @pl.when((step >= first) & (step < last))
        def _():
            start = 0
            for which, count in pieces:
                span = slice(start, start + count)
                prod[:, span] = dot(lefts[which][...], right_ref[:, span])
                start += count

    @pl.when(step < blocks)
    def _():
        for place in range(places):
            even = prod[2 * place * share : (2 * place + 1) * share, :]
            odd = prod[(2 * place + 1) * share : (2 * place + 2) * share, :]
            rows = slice(place * held, place * held + share)
            sent[step, rows, :] = jnp.where(core == 0, odd, even).astype(BF16)
            kept[step % 2, rows, :] = jnp.where(core == 0, even, odd)
            if held > share:
                rows = slice(place * held + share, (place + 1) * held)
                sent[step, rows, :] = jnp.zeros((held - share, columns), BF16)
                kept[step % 2, rows, :] = jnp.zeros((held - share, columns), F32)
        to_mate(step).start()

    @pl.when(step >= 1)
    def _():
        done = step - 1
        to_mate(done).wait()
        out_ref[...] = (kept[done % 2] + got[done].astype(F32)).astype(BF16)


def weigh(lefts, right, columns, blocks, turns, share, name, number):
    rows, tokens = lefts[0].shape
    total = blocks * columns
    held = -(-share // 16) * 16
    places = rows // (2 * share)
    fixed = pl.BlockSpec((rows, tokens), lambda n: (0, 0), pipeline_mode=pl.Buffered(1))
    return pl.pallas_call(
        functools.partial(weigh_kernel, blocks, share, held, turns),
        grid=(blocks + 1,),
        in_specs=[fixed] * len(lefts) + [pl.BlockSpec((tokens, columns), lambda n: (0, jnp.minimum(n, blocks - 1)))],
        out_specs=pl.BlockSpec((places * held, columns), lambda n: (0, jnp.maximum(n - 1, 0))),
        out_shape=jax.ShapeDtypeStruct((places * held, total), BF16),
        scratch_shapes=[
            pltpu.VMEM((rows, columns), F32),
            pltpu.VMEM((2, places * held, columns), F32),
            pltpu.VMEM((blocks, places * held, columns), BF16),
            pltpu.VMEM((blocks, places * held, columns), BF16),
            pltpu.SemaphoreType.DMA((blocks,)),
            pltpu.SemaphoreType.DMA((blocks,)),
        ],
        compiler_params=params(collective_id=number, has_side_effects=True),
        cost_estimate=pl.CostEstimate(
            flops=2 * rows * tokens * total, bytes_accessed=24 * 1024 * 1024, transcendentals=0
        ),
        name=name,
    )(*lefts, right)


LAGS = (1, 3, 5, 6, 7, 8)
RING, RING_XY, RING_LINE = 5, 2, 4
EARLY, DOWN_BLOCKS, LINE_LAG = 10, 4, 2


def close_kernel(blocks, rest_blocks, rest_edge, seqs, reps, h2t_ref, ot_ref, h1t_ref, rest_ref, right_ref, three_ref, w_ref, x_ref, dr_ref, gain_ref, down_ref,
                 gi_ref, rest_sum, sum_ref, down_sum,
                 prod, kept0, kept1x, kept1y, kept2, s0, r0, s1x, r1x, s1y, r1y, s2x, r2x, s2y, r2y,
                 mine, ends, others, down_ends, down_others, send_sem, recv_sem, line_sem):
    step = pl.program_id(0)
    width = h1t_ref.shape[0]
    share = mine.shape[1]
    seq, dp, rep = lax.axis_index("seq"), lax.axis_index("dp"), lax.axis_index("rep")
    core, side = lax.rem(dp, 2), dp // 2
    mate, across = dp + 1 - 2 * core, lax.rem(dp + 2, 4)
    seq_peers = [lax.rem(seq + hop, seqs) for hop in range(1, seqs)]
    inner = (rep == 1) | (rep == 2)
    beside = rep + 1 - 2 * lax.rem(rep, 2)
    slot_seq, slot_side, slot_in = 1, seqs, seqs + 1

    def copy(source, target, n, slot, device):
        turn = lax.rem(n, 2 * RING_XY)
        return pltpu.make_async_remote_copy(
            src_ref=source, dst_ref=target, send_sem=send_sem.at[turn, slot], recv_sem=recv_sem.at[turn, slot],
            device_id=device, device_id_type=MESH,
        )

    def rows(first, count):
        return pl.ds(pl.multiple_of(first * share, share), count * share)

    def half(n):
        return lax.rem(n // 2, RING_XY)

    def to_mate(n):
        slot = lax.rem(n, RING)
        return [copy(s0.at[slot], r0.at[slot], n, 0, {"dp": mate})]

    def to_seq(n, source, target):
        return [
            copy(source.at[half(n), hop], target.at[half(n), hop], n, slot_seq + hop, {"seq": peer})
            for hop, peer in enumerate(seq_peers)
        ]

    def to_side(n, source, target):
        return [copy(source.at[half(n)], target.at[half(n)], n, slot_side, {"dp": across})]

    def line(which, source, first, second, sends, arrivals):
        start, target, device = (
            (source, first, beside), (first, second, reps - 1 - rep), (second, second, beside),
        )[which]
        return pltpu.make_async_remote_copy(
            src_ref=start, dst_ref=target, send_sem=sends, recv_sem=arrivals,
            device_id={"rep": device}, device_id_type=MESH,
        )

    def own_line(n, which):
        slot, turn = slot_in + which, lax.rem(n, RING_LINE)
        return line(which, mine.at[turn], ends.at[turn], others.at[turn], send_sem.at[turn, slot], recv_sem.at[turn, slot])

    down_columns = down_ends.shape[2]
    extra = []
    for k in range(down_ends.shape[0]):
        extra.append((down_ref, down_ends, down_others, down_sum, k, slice(k * down_columns, (k + 1) * down_columns)))

    def extra_line(index, which):
        source, first, second, _, k, columns = extra[index]
        return line(
            which, source.at[:, columns], first.at[k], second.at[k],
            line_sem.at[0, index, which], line_sem.at[1, index, which],
        )

    def start(copies):
        for each in copies:
            each.start()

    def wait(copies):
        for each in copies:
            each.wait()

    @pl.when(step == 0)
    def _():
        barrier = pltpu.get_barrier_semaphore()
        partners = [{"dp": mate}, {"dp": across}]
        partners += [{"seq": peer} for peer in seq_peers] + [{"rep": beside}]
        for partner in partners:
            pl.semaphore_signal(barrier, inc=1, device_id=partner, device_id_type=MESH)

        @pl.when(inner)
        def _():
            pl.semaphore_signal(barrier, inc=1, device_id={"rep": reps - 1 - rep}, device_id_type=MESH)
            pl.semaphore_wait(barrier, len(partners) + 1)

        @pl.when(jnp.logical_not(inner))
        def _():
            pl.semaphore_wait(barrier, len(partners))

    for index in range(len(extra)):
        @pl.when((step == index) & jnp.logical_not(inner))
        def _():
            extra_line(index, 0).start()

    whole_blocks, split = rest_edge // CUT, rest_edge % CUT

    @pl.when(step < whole_blocks)
    def _():
        prod[...] = dot(h2t_ref[...], rest_ref[...])

    @pl.when((step >= whole_blocks) & (step < rest_blocks))
    def _():
        if split:
            @pl.when(step == whole_blocks)
            def _():
                prod[:, :split] = dot(h2t_ref[...], rest_ref[:, :split])
                prod[:, split:] = dot(ot_ref[...], rest_ref[:, split:])

        @pl.when(step >= whole_blocks + (split > 0))
        def _():
            prod[...] = dot(ot_ref[...], rest_ref[...])

    @pl.when((step >= rest_blocks) & (step < blocks))
    def _():
        prod[...] = dot(h1t_ref[...], right_ref[0])

    @pl.when(step < blocks)
    def _():
        for place in range(2 * seqs):
            span = slice(place * share, (place + 1) * share)
            s0[lax.rem(step, RING), span, :] = prod[rows(2 * place + 1 - core, 1), :].astype(BF16)
        start(to_mate(step))
        for place in range(2 * seqs):
            span = slice(place * share, (place + 1) * share)
            kept0[step % 2, span, :] = prod[rows(2 * place + core, 1), :]

    @pl.when((step >= blocks) & (step < blocks + gi_steps(three_ref, right_ref)))
    def _():
        back = None
        for part in range(3):
            term = dot(three_ref[part], w_ref[:, part * width : (part + 1) * width], NT)
            back = term if back is None else back + term
        unit, inverse = normed(x_ref[...].astype(F32))
        gi_ref[...] = dr_ref[...] + norm_back(back * gain_ref[...], unit, inverse)

    for index, (source, first, second, total, k, columns) in enumerate(extra):
        meet, share_out, close_out = (index + LINE_LAG * hop for hop in (1, 2, 3))

        @pl.when((step == meet) & inner)
        def _():
            extra_line(index, 0).wait_recv()
            first[k] = (source[:, columns].astype(F32) + first[k].astype(F32)).astype(BF16)
            extra_line(index, 1).start()

        @pl.when((step == share_out) & inner)
        def _():
            extra_line(index, 1).wait()
            second[k] = (first[k].astype(F32) + second[k].astype(F32)).astype(BF16)
            extra_line(index, 2).start()

        @pl.when(step == close_out)
        def _():
            @pl.when(inner)
            def _():
                extra_line(index, 2).wait_send()

            @pl.when(jnp.logical_not(inner))
            def _():
                extra_line(index, 0).wait_send()
                extra_line(index, 2).wait_recv()

            total[:, columns] = second[k]

    n6 = step - LAGS[5]

    @pl.when((n6 >= 0) & (n6 < blocks))
    def _():
        @pl.when(inner)
        def _():
            own_line(n6, 2).wait_send()

        @pl.when(jnp.logical_not(inner))
        def _():
            own_line(n6, 2).wait_recv()

        total = others[lax.rem(n6, RING_LINE)]

        @pl.when(n6 < rest_blocks)
        def _():
            rest_sum[:, pl.ds(pl.multiple_of(n6 * CUT, CUT), CUT)] = total

        @pl.when(n6 >= rest_blocks)
        def _():
            sum_ref[:, pl.ds(pl.multiple_of((n6 - rest_blocks) * CUT, CUT), CUT)] = total

    n5 = step - LAGS[4]

    @pl.when((n5 >= 0) & (n5 < blocks) & inner)
    def _():
        own_line(n5, 1).wait()
        others[lax.rem(n5, RING_LINE)] = (ends[lax.rem(n5, RING_LINE)].astype(F32) + others[lax.rem(n5, RING_LINE)].astype(F32)).astype(BF16)
        own_line(n5, 2).start()

    n4 = step - LAGS[3]

    @pl.when((n4 >= 0) & (n4 < blocks) & inner)
    def _():
        own_line(n4, 0).wait_recv()
        ends[lax.rem(n4, RING_LINE)] = (mine[lax.rem(n4, RING_LINE)].astype(F32) + ends[lax.rem(n4, RING_LINE)].astype(F32)).astype(BF16)
        own_line(n4, 1).start()

    @pl.when((n4 >= 0) & (n4 < blocks) & jnp.logical_not(inner))
    def _():
        own_line(n4, 0).wait_send()

    n3 = step - LAGS[2]

    @pl.when((n3 >= 0) & (n3 < blocks))
    def _():
        total = kept2[n3 % 2]

        @pl.when(n3 % 2 == 0)
        def _():
            wait(to_side(n3, s2y, r2y))
            mine[lax.rem(n3, RING_LINE)] = (total + r2y[half(n3)].astype(F32)).astype(BF16)

        @pl.when(n3 % 2 == 1)
        def _():
            wait(to_seq(n3, s2x, r2x))
            added = total
            for hop in range(seqs - 1):
                added = added + r2x[half(n3), hop].astype(F32)
            mine[lax.rem(n3, RING_LINE)] = added.astype(BF16)

        @pl.when(jnp.logical_not(inner))
        def _():
            own_line(n3, 0).start()

    n2 = step - LAGS[1]

    @pl.when((n2 >= 0) & (n2 < blocks) & (n2 % 2 == 0))
    def _():
        wait(to_seq(n2, s1x, r1x))
        total = kept1x[...]
        for hop in range(seqs - 1):
            total = total + r1x[half(n2), hop].astype(F32)
        kept1x[...] = total
        s2y[half(n2)] = kept1x[rows(1 - side, 1), :].astype(BF16)
        start(to_side(n2, s2y, r2y))
        kept2[0] = kept1x[rows(side, 1), :]

    @pl.when((n2 >= 0) & (n2 < blocks) & (n2 % 2 == 1))
    def _():
        wait(to_side(n2, s1y, r1y))
        kept1y[...] = kept1y[...] + r1y[half(n2)].astype(F32)
        for hop, peer in enumerate(seq_peers):
            s2x[half(n2), hop] = kept1y[rows(peer, 1), :].astype(BF16)
        start(to_seq(n2, s2x, r2x))
        kept2[1] = kept1y[rows(seq, 1), :]

    n1 = step - LAGS[0]

    @pl.when((n1 >= 0) & (n1 < blocks))
    def _():
        wait(to_mate(n1))
        held = n1 % 2
        kept0[held] = kept0[held] + r0[lax.rem(n1, RING)].astype(F32)

        @pl.when(n1 % 2 == 0)
        def _():
            for hop, peer in enumerate(seq_peers):
                s1x[half(n1), hop] = kept0[held, rows(2 * peer, 2), :].astype(BF16)
            start(to_seq(n1, s1x, r1x))
            kept1x[...] = kept0[held, rows(2 * seq, 2), :]

        @pl.when(n1 % 2 == 1)
        def _():
            for place in range(seqs):
                s1y[half(n1), place * share : (place + 1) * share, :] = kept0[held, rows(2 * place + 1 - side, 1), :].astype(BF16)
            start(to_side(n1, s1y, r1y))
            for place in range(seqs):
                kept1y[place * share : (place + 1) * share, :] = kept0[held, rows(2 * place + side, 1), :]


def gi_steps(three_ref, right_ref):
    return right_ref.shape[1] // three_ref.shape[1]


def close(h2t, mixed_t, h1t, rest, rest_edge, slopes, weight, x, dr, gain, down, seqs, dps, reps):
    assert (dps, reps) == (4, 4)
    width, tokens = h1t.shape
    share = width // (seqs * dps)
    rest_blocks = rest.shape[1] // CUT - EARLY
    rest_edge = rest_edge - EARLY * CUT
    blocks_of = lambda array, count: (count, array.shape[0], array.shape[1] // count)
    blocks = rest_blocks + 3 * width // CUT
    halves = width // CUT
    token_blocks = tokens // TILE
    steps = max(blocks + token_blocks, blocks + LAGS[5], DOWN_BLOCKS + 3 * LINE_LAG)
    late = lambda s: jnp.clip(s - blocks, 0, token_blocks - 1)
    turn_of = lambda s: jnp.clip(s - rest_blocks, 0, blocks - rest_blocks - 1)
    fixed = lambda m, n: pl.BlockSpec((m, n), lambda s: (0, 0), pipeline_mode=pl.Buffered(1))
    row = pl.BlockSpec((TILE, width), lambda s: (late(s), 0))
    half_rows = 2 * seqs * share
    buffers = lambda *shape: [pltpu.VMEM(shape + (CUT,), BF16)] * 2
    slots = seqs + 4
    return pl.pallas_call(
        functools.partial(close_kernel, blocks, rest_blocks, rest_edge, seqs, reps),
        grid=(steps,),
        in_specs=[
            fixed(width, tokens),
            fixed(width, tokens),
            fixed(width, tokens),
            pl.BlockSpec((tokens, CUT), lambda s: (0, EARLY + jnp.minimum(s, rest_blocks - 1))),
            pl.BlockSpec((1, tokens, CUT), lambda s: (turn_of(s) // halves, 0, turn_of(s) % halves)),
            pl.BlockSpec((3, TILE, width), lambda s: (0, late(s), 0)),
            fixed(*weight.shape),
            row,
            row,
            fixed(1, width),
            fixed(*down.shape),
        ],
        out_specs=[
            row, fixed(share, rest_blocks * CUT), fixed(share, 3 * width), fixed(*down.shape),
        ],
        out_shape=[
            jax.ShapeDtypeStruct((tokens, width), F32),
            jax.ShapeDtypeStruct((share, rest_blocks * CUT), BF16),
            jax.ShapeDtypeStruct((share, 3 * width), BF16),
            jax.ShapeDtypeStruct(down.shape, BF16),
        ],
        scratch_shapes=[
            pltpu.VMEM((width, CUT), F32),
            pltpu.VMEM((2, half_rows, CUT), F32),
            pltpu.VMEM((2 * share, CUT), F32),
            pltpu.VMEM((seqs * share, CUT), F32),
            pltpu.VMEM((2, share, CUT), F32),
            *buffers(RING, half_rows),
            *buffers(RING_XY, seqs - 1, 2 * share),
            *buffers(RING_XY, seqs * share),
            *buffers(RING_XY, seqs - 1, share),
            *buffers(RING_XY, share),
            *[pltpu.VMEM((RING_LINE, share, CUT), BF16)] * 3,
            *[pltpu.VMEM(blocks_of(down, DOWN_BLOCKS), BF16)] * 2,
            pltpu.SemaphoreType.DMA((max(2 * RING_XY, RING_LINE), slots)),
            pltpu.SemaphoreType.DMA((max(2 * RING_XY, RING_LINE), slots)),
            pltpu.SemaphoreType.DMA((2, DOWN_BLOCKS, 3)),
        ],
        compiler_params=params(collective_id=1, has_side_effects=True),
        cost_estimate=pl.CostEstimate(
            flops=tokens * width * width // 4, bytes_accessed=4 * 1024 * 1024, transcendentals=0
        ),
        name="close",
    )(h2t, mixed_t, h1t, rest, slopes, slopes, weight, x, dr, gain, down)


def neighbours(block, axis, along, after=None):
    count = lax.axis_size(axis)
    rows = block.shape[along]
    if count == 2:
        start = (1 - lax.axis_index(axis)) * (rows - HALF)
        facing = lax.dynamic_slice_in_dim(block, start, HALF, along)
        if after is not None:
            facing, _ = lax.optimization_barrier((facing, after))
        return lax.ppermute(facing, axis, [(0, 1), (1, 0)])
    step = min(rows, HALF)
    head = lax.slice_in_dim(block, 0, step, axis=along)
    tail = lax.slice_in_dim(block, rows - step, rows, axis=along)
    hops = range(1, HALF // step + 1)
    after = [lax.ppermute(head, axis, [(i + hop, i) for i in range(count - hop)]) for hop in hops]
    before = [lax.ppermute(tail, axis, [(i, i + hop) for i in range(count - hop)]) for hop in reversed(hops)]
    return jnp.concatenate(after + before, axis=along)


def survey(labels, stretch, extent, seq_index, seq_count):
    length = labels.shape[1]
    mem = jnp.arange(extent, dtype=jnp.int32)
    own_start = seq_index * stretch
    wraps = stretch + HALF if seq_count > 2 else jnp.where(seq_index == 0, extent, stretch)
    places = own_start + mem - jnp.where(mem >= wraps, extent, 0)
    padded = jnp.pad(labels, ((0, 0), (HALF, HALF)))
    cut = lambda first, size: lax.dynamic_slice_in_dim(padded, first + HALF, size, 1)
    parts = [cut(own_start, stretch)]
    if seq_count == 2:
        parts.append(cut(jnp.where(seq_index == 0, own_start + stretch, own_start - HALF), HALF))
    else:
        parts += [cut(own_start + stretch, HALF), cut(own_start - HALF, HALF)]
    near = jnp.concatenate(parts, axis=1)
    docs = jnp.arange(DOCS, dtype=jnp.int32)
    starts = jnp.sum(labels[:, :, None] < docs, axis=1, dtype=jnp.int32)
    stops = jnp.sum(labels[:, :, None] <= docs, axis=1, dtype=jnp.int32) - 1
    same = near[:, :, None] == docs
    positions = places - jnp.sum(jnp.where(same, starts[:, None, :], 0), axis=-1)
    lane = jnp.arange(LANES, dtype=jnp.int32)
    half_dim = HEAD_DIM // 2
    frequency = THETA ** (-((lane % half_dim).astype(F32) * 2.0 / HEAD_DIM))
    angles = positions.astype(F32)[:, :, None] * frequency
    cosines = jnp.cos(angles)
    sines = jnp.sin(angles) * jnp.where(lane % HEAD_DIM < half_dim, -1.0, 1.0)
    slot = lane % HEAD_DIM
    marks_k = jnp.where(
        slot < DOCS,
        jnp.where(near[:, :, None] == slot, 0.0, MASKED),
        jnp.where((slot >= 8) & (slot < 11), 1.0, 0.0),
    ).astype(BF16)
    kind = jnp.arange(HEAD_DIM, dtype=jnp.int32)[None, :, None]
    marks_q = jnp.where((kind < DOCS) & (near[:, None, :] == kind), 1.0, 0.0).astype(BF16)
    at = jnp.arange(length // TILE, dtype=jnp.int32) * TILE
    first_label, last_label = labels[:, ::TILE], labels[:, TILE - 1 :: TILE]
    pick = lambda table, which: jnp.sum(
        jnp.where(which[:, :, None] == docs, table[:, None, :], 0), axis=-1
    )
    lows = jnp.maximum(pick(starts, first_label), at - HALF) // TILE
    highs = jnp.minimum(pick(stops, last_label), at + TILE - 1 + HALF) // TILE + 1
    own = (own_start // TILE).astype(jnp.int32).reshape(1)
    return own, lows, highs, cosines, sines, marks_k, marks_q


def body(inputs, segments, cotangent, attn_gain, mlp_gain, w_qkv, w_out, w_in, w_down):
    stretch, width = inputs.shape[2:]
    length = segments.shape[2]
    x = inputs.reshape(-1, stretch, width)
    seeds = cotangent.reshape(-1, stretch, width)
    labels = segments.reshape(-1, length)
    batch = x.shape[0]
    group = ("seq", "dp")
    seq_index = lax.axis_index("seq")
    seq_count = lax.axis_size("seq")

    share = attn_gain.shape[0]
    shards = width // share
    gather = lambda shard: lax.all_gather(shard, group, axis=0, tiled=True)
    gain_rows = jnp.pad(jnp.stack([attn_gain, mlp_gain]), ((0, share - 2), (0, LANES - share)))
    qkv_full = gather(jnp.concatenate([w_qkv, gain_rows], axis=1))
    blank = jnp.zeros((share, FF_PAD - FF), BF16)
    halo = HALF * (1 if seq_count == 2 else 2)
    extent = stretch + halo
    own, lows, highs, cosines, sines, marks_k, marks_q = survey(labels, stretch, extent, seq_index, seq_count)
    x_halo = neighbours(x, "seq", 1, (qkv_full, cosines, sines, marks_k))
    rest_full = gather(jnp.concatenate([w_in[:, :FF], blank, w_in[:, FF:], blank, w_out], axis=1))
    down_full = gather(w_down)

    h1t, qkv = project(x, qkv_full, cosines, sines, 0, None, extent, shards)
    qkv = project(x_halo, qkv_full, cosines, sines, stretch // TILE, qkv, extent, shards)
    mixed, mixed_t, lse = attend(own, lows, highs, qkv, marks_k, marks_q, stretch)
    lse_halo = neighbours(lse, "seq", 3)
    late_full, mixed, lse_halo = lax.optimization_barrier((qkv_full, mixed, lse_halo))
    gains = late_full[:, 3 * width : 3 * width + share].reshape(shards, share, share).astype(F32)
    gain_one, gain_two = gains[:, 0].reshape(1, width), gains[:, 1].reshape(1, width)
    result, h2t, hidt, slopes, dr, do, delta, do_halo, delta_halo = feed(
        x, mixed, seeds, gain_two, rest_full, down_full, seq_count, halo
    )

    tokens = batch * stretch
    dps = lax.axis_size("dp")
    pairs = [list(range(core, seq_count * dps, 2)) for core in range(2)]
    scatter = lambda part: lax.psum_scatter(part, group, scatter_dimension=0, tiled=True, axis_index_groups=pairs)
    slopes = slopes.reshape(tokens, -1)
    part_early = weigh([h2t], slopes, CUT, EARLY, ((0, EARLY, ((0, CUT),)),), share, "weigh_early", 4)
    shard_early = scatter(part_early)
    hidt, part_early = lax.optimization_barrier((hidt, part_early))
    part_down = weigh(
        [hidt], seeds.reshape(tokens, width), TILE, width // TILE, ((0, width // TILE, ((0, TILE),)),),
        w_down.shape[0], "weigh_down", 3,
    )
    shard_down = scatter(part_down)
    do_halo, part_down = lax.optimization_barrier((do_halo, part_down))

    def back(first_batch, count, held):
        return attend_back(
            own, lows, highs, qkv, do, do_halo, lse, lse_halo, delta, delta_halo, marks_k, marks_q, cosines, sines,
            first_batch, count, held,
        )

    slopes_qkv = back(0, batch // 2, None)
    slopes_qkv, shard_early = lax.optimization_barrier((slopes_qkv, shard_early))
    early_sum = lax.psum(shard_early, "rep")
    slopes_qkv = back(batch // 2, batch - batch // 2, slopes_qkv)
    grad_x, late_sum, grad_qkv, down_sum = close(
        h2t, mixed_t, h1t, slopes, 2 * FF_PAD, slopes_qkv.reshape(3, tokens, width), qkv_full, x.reshape(tokens, width), dr.reshape(tokens, width),
        gain_one, shard_down, seq_count, dps, lax.axis_size("rep"),
    )
    grad_qkv = grad_qkv.astype(F32)
    rest_sum = jnp.concatenate([early_sum, late_sum], axis=1).astype(F32)
    grad_in = jnp.concatenate([rest_sum[:, :FF], rest_sum[:, FF_PAD : FF_PAD + FF]], axis=1)
    grad_attn_gain = jnp.sum(grad_qkv * w_qkv.astype(F32), axis=1) / attn_gain.astype(F32)
    grad_mlp_gain = jnp.sum(grad_in * w_in.astype(F32), axis=1) / mlp_gain.astype(F32)
    return (
        result.reshape(cotangent.shape),
        grad_x.reshape(inputs.shape),
        grad_attn_gain,
        grad_mlp_gain,
        grad_qkv,
        rest_sum[:, 2 * FF_PAD : 2 * FF_PAD + width],
        grad_in,
        down_sum[: w_down.shape[0]].astype(F32),
    )


def solution(mesh):
    return jax.shard_map(
        body,
        mesh=mesh,
        in_specs=(
            P(None, ("dp", "rep"), "seq", None),
            P(None, ("dp", "rep"), None),
            P(None, ("dp", "rep"), "seq", None),
            P(("seq", "dp")),
            P(("seq", "dp")),
            P(("seq", "dp"), None),
            P(("seq", "dp"), None),
            P(("seq", "dp"), None),
            P(("seq", "dp"), None),
        ),
        out_specs=(
            P(None, ("dp", "rep"), "seq", None),
            P(None, ("dp", "rep"), "seq", None),
            P(("seq", "dp")),
            P(("seq", "dp")),
            P(("seq", "dp"), None),
            P(("seq", "dp"), None),
            P(("seq", "dp"), None),
            P(("seq", "dp"), None),
        ),
        check_vma=False,
    )
```
